256 devices in a mesh: dp: 8 (over z_lo, y), seq: 32 (over z_hi, x, core).
Axes of the slice: x: 4, y: 4, z: 8 (z_hi: 4, z_lo: 2; z = z_hi * 2 + z_lo), core: 2. Of those that a mesh axis runs over, the one named last changes fastest.
Arguments:
- queries: bfloat16 [32768, 4096], P(('dp', 'seq')), may hold values from -64 to 64
- keys: bfloat16 [32768, 4096], P(('dp', 'seq')), may hold values from -64 to 64
- values: bfloat16 [32768, 4096], P(('dp', 'seq')), may hold values from -6 to 6
- out_grad: bfloat16 [32768, 4096], P(('dp', 'seq')), may hold values from -6 to 6
- gain_q: float32 [32, 128], P('seq', 'dp'), may hold values from 0.5 to 10
- gain_k: float32 [32, 128], P('seq', 'dp'), may hold values from 0.5 to 10
- clip_ids: int32 [8, 4096], P('dp', 'seq'), may hold values from 0 to 31, never falling along the last dimension, each value on 1 to 256 neighbouring positions
- counts: int32 [8, 32], P('dp', 'seq'), may hold values from 42 to 128, as said below
Outputs:
- grad_queries: bfloat16 [32768, 4096], P(('dp', 'seq'))
- grad_keys: bfloat16 [32768, 4096], P(('dp', 'seq'))
- grad_values: bfloat16 [32768, 4096], P(('dp', 'seq'))
- grad_gain_q: float32 [32, 128], P('seq')
- grad_gain_k: float32 [32, 128], P('seq')
The draws below stay inside these ranges and needn't reach their ends.
Inputs may be any that keep to these rules, and one draw needn't show every extreme that they name: `counts`: in every row one device holds 128 live slots and another a third of 128, rounded down. `clip_ids`: along a row clip numbers never fall; each clip takes 1 to 256 consecutive slots, one exactly 256.
All inputs are finite; a program needn't handle non-finite values.
Results may differ from the reference program's by a relative error of at most 0.011.
The reference program's roundings to bfloat16 on the way (of `q_norm`, `k_norm`, `weights` and `d_scores`) count: a program that leaves them out, or rounds other values in their place, can miss the bound.
Values may be sent and summed in bfloat16 or wider, within the bound.
No kernel may reach another device: no remote copies, remote signals or barrier semaphores. Data moves between devices by JAX's collectives and lax.ppermute only.
A program may use at most 192 MiB of HBM per device.

```python
import math
import jax
import jax.numpy as jnp
import numpy as np
from jax import lax

HD = 128
HEADS = 32
T_DEV = 128
CLIP_MAX = 256
S_GROUP = 4096
QB = 512
TOKENS = 32768
N_DP = 8
N_SEQ = 32


def shared_keys(key):
    return jax.random.normal(key, (TOKENS, HEADS * HD), jnp.float32)


def gain_entries(key):
    return jnp.exp(jax.random.uniform(key, (HEADS, HD), jnp.float32, -0.693, 0.916))


def draw_keys(key, part):
    normal_base = shared_keys(key)
    return jnp.clip(normal_base, -64.0, 64.0).astype(jnp.bfloat16)


def draw_queries(key, part):
    own_key = jax.random.fold_in(key, 12)
    normal_base = jax.random.normal(own_key, (TOKENS, HEADS * HD), jnp.float32)
    return jnp.clip(normal_base, -64.0, 64.0).astype(jnp.bfloat16)


def draw_gain_q(key, part):
    key = jax.random.fold_in(key, 21)
    entries = gain_entries(key)
    return entries


def draw_gain_k(key, part):
    key = jax.random.fold_in(key, 22)
    entries = gain_entries(key)
    return entries


def draw_counts(key, part):
    key = jax.random.fold_in(key, 31)
    key_base, key_peak, key_stride = jax.random.split(key, 3)
    lowest = T_DEV // 3
    drawn = jax.random.randint(key_base, (N_DP, N_SEQ), lowest, T_DEV + 1)
    peak_at = jax.random.randint(key_peak, (N_DP, 1), 0, N_SEQ)
    stride = jax.random.randint(key_stride, (N_DP, 1), 1, N_SEQ)
    floor_at = (peak_at + stride) % N_SEQ
    column = jnp.arange(N_SEQ, dtype=jnp.int32)[None, :]
    drawn = jnp.where(column == peak_at, T_DEV, drawn)
    drawn = jnp.where(column == floor_at, lowest, drawn)
    return drawn.astype(jnp.int32)


def block_scale(rng, shape, cuts, low, top_value):
    def one(axis_at, shards_of):
        draws = jax.random.uniform(jax.random.fold_in(jax.random.fold_in(rng, 6), axis_at), (shards_of,), jnp.float32, low / len(cuts), top_value / len(cuts))
        return jnp.repeat(jnp.exp(draws), shape[axis_at] // shards_of).reshape((-1,) + (1,) * (len(shape) - axis_at - 1))

    factor_of = one(*cuts[0])
    for cut in cuts[1:]:
        factor_of = factor_of * one(*cut)
    return factor_of


def profile(count, total, bound, lean):
    loads = [(1 << 20) // math.isqrt(grade ** lean) + 1 for grade in range(2, count + 1)]
    surplus, given = total - bound - (count - 1), [1] * (count - 1)
    while surplus > 0:
        candidates = [i for i in range(count - 1) if given[i] < bound]
        mass, left = sum([loads[i] for i in candidates]), surplus
        for i in candidates:
            more = min(bound - given[i], max(1, left * loads[i] // mass), surplus)
            given[i] = given[i] + more
            surplus = surplus - more
    return np.array([bound] + given)


def uneven(stream_key, count, total, reach, lean):
    if count == 2:
        one = jax.random.randint(stream_key, (), max(1, total - reach), min(reach, total - 1) + 1)
        return jnp.stack([one, total - one])
    tallies = jnp.asarray(profile(count, total, reach, lean), jnp.int32)
    twos = (count - 1) // 2
    giver, sink = tallies[1:1 + 2 * twos:2], tallies[2:2 + 2 * twos:2]
    margin = jnp.minimum(giver - 1, reach - sink)
    shifted = jax.random.randint(jax.random.fold_in(stream_key, 1), (twos,), 0, 1 << 20) % (margin + 1)
    tallies = tallies.at[1:1 + 2 * twos:2].set(giver - shifted).at[2:2 + 2 * twos:2].set(sink + shifted)
    return tallies[jax.random.permutation(jax.random.fold_in(stream_key, 2), count)]


def noise(stream_key, dims, deviation, limit, cuts=(), kind=jnp.bfloat16):
    level = block_scale(stream_key, dims, cuts, -0.22, 0.18) if cuts else 1.0
    array = jax.random.normal(stream_key, dims, jnp.float32) * deviation * level
    return jnp.minimum(jnp.maximum(array, -limit), limit).astype(kind)


def setup_inputs(seed: int = 0) -> dict:
    key_of = jax.random.split(jax.random.key(seed), 9)
    queries = draw_queries(jax.random.fold_in(key_of[8], 71), 0)
    keys = draw_keys(jax.random.fold_in(key_of[8], 71), 0)
    values = noise(key_of[2], (TOKENS, HEADS * HD), 1.0, 6.0, ((0, 256),))
    out_grad = noise(key_of[3], (TOKENS, HEADS * HD), 1.0, 6.0, ((0, 256),))
    gain_q = draw_gain_q(jax.random.fold_in(key_of[8], 71), 0)
    gain_k = draw_gain_k(jax.random.fold_in(key_of[8], 71), 0)
    clip_ids = jax.vmap(lambda own: jnp.searchsorted(jnp.cumsum(uneven(own, N_SEQ, S_GROUP, CLIP_MAX, 0)), jnp.arange(S_GROUP), side="right"))(jax.random.split(key_of[6], N_DP)).reshape((N_DP, S_GROUP)).astype(jnp.int32)
    counts = draw_counts(jax.random.fold_in(key_of[8], 71), 0)
    return {"queries": queries, "keys": keys, "values": values, "out_grad": out_grad, "gain_q": gain_q, "gain_k": gain_k, "clip_ids": clip_ids, "counts": counts}


EPS = 1e-06
NEG = -1e+30

def norm_parts(rows, gain):
    widened = rows.astype(jnp.float32)
    scaled = lax.rsqrt(lax.optimization_barrier(jnp.mean(widened * widened, axis=-1, keepdims=True)) + EPS)
    unit_rows = widened * scaled
    return (scaled, unit_rows, (unit_rows * gain).astype(jnp.bfloat16))

def norm_back(scaled, unit_rows, gain, upper):
    weighted = gain * upper
    return scaled * (weighted - unit_rows * lax.optimization_barrier(jnp.mean(unit_rows * weighted, axis=-1, keepdims=True)))

def attend(q_norm, k_norm, v_rows, d_rows, linked, q_live):
    score_scale = q_norm.shape[-1] ** (-0.5)
    qf = q_norm.astype(jnp.float32)
    kf = k_norm.astype(jnp.float32)
    vf = v_rows.astype(jnp.float32)
    df = d_rows.astype(jnp.float32)
    scores = jnp.einsum('brd,bcd->brc', qf, kf) * score_scale
    masked = jnp.where(linked, scores, NEG)
    row_top = lax.optimization_barrier(jnp.max(masked, axis=-1, keepdims=True))
    exponent = jnp.where(linked, jnp.exp(masked - row_top), 0.0)
    row_total = lax.optimization_barrier(jnp.sum(exponent, axis=-1, keepdims=True)) + (1.0 - q_live)[:, None]
    weights = (exponent / row_total).astype(jnp.bfloat16)
    wf = weights.astype(jnp.float32)
    outputs = jnp.einsum('brc,bcd->brd', wf, vf)
    row_delta = lax.optimization_barrier(jnp.sum(df * outputs, axis=-1, keepdims=True))
    d_weights = jnp.einsum('brd,bcd->brc', df, vf)
    d_scores = (wf * (d_weights - row_delta)).astype(jnp.bfloat16).astype(jnp.float32)
    dq_norm = jnp.einsum('brc,bcd->brd', d_scores, kf) * score_scale
    dk_norm = jnp.einsum('brc,brd->bcd', d_scores, qf) * score_scale
    dv_rows = jnp.einsum('brc,brd->bcd', wf, df)
    return (dq_norm, dk_norm, dv_rows)

def group_head(q_rows, k_rows, v_rows, d_rows, gain_q, gain_k, clip, live_rows, q_block, key_reach):
    batch = q_rows.shape[0]
    length = q_rows.shape[1]
    depth = q_rows.shape[2]
    q_scale, q_unit, q_norm = norm_parts(q_rows, gain_q[:, None, :])
    k_scale, k_unit, k_norm = norm_parts(k_rows, gain_k[:, None, :])
    padding = ((0, 0), (key_reach, key_reach), (0, 0))
    k_wide = jnp.pad(k_norm, padding)
    v_wide = jnp.pad(v_rows, padding)
    clip_wide = jnp.pad(clip, (key_reach, key_reach), constant_values=-1)
    live_wide = jnp.pad(live_rows, (key_reach, key_reach))
    key_span = q_block + 2 * key_reach

    def one_block(totals, position):
        dk_acc, dv_acc = totals
        first_row = position * q_block
        q_part = lax.dynamic_slice_in_dim(q_norm, first_row, q_block, 1)
        d_part = lax.dynamic_slice_in_dim(d_rows, first_row, q_block, 1)
        k_part = lax.dynamic_slice_in_dim(k_wide, first_row, key_span, 1)
        v_part = lax.dynamic_slice_in_dim(v_wide, first_row, key_span, 1)
        clip_q = lax.dynamic_slice_in_dim(clip, first_row, q_block)
        live_q = lax.dynamic_slice_in_dim(live_rows, first_row, q_block)
        clip_k = lax.dynamic_slice_in_dim(clip_wide, first_row, key_span)
        live_k = lax.dynamic_slice_in_dim(live_wide, first_row, key_span)
        linked = (clip_q[:, None] == clip_k[None, :]) & (live_q[:, None] > 0) & (live_k[None, :] > 0)
        dq_part, dk_part, dv_part = attend(q_part, k_part, v_part, d_part, linked, live_q.astype(jnp.float32))
        dk_acc = lax.dynamic_update_slice_in_dim(dk_acc, lax.dynamic_slice_in_dim(dk_acc, first_row, key_span, 1) + dk_part, first_row, 1)
        dv_acc = lax.dynamic_update_slice_in_dim(dv_acc, lax.dynamic_slice_in_dim(dv_acc, first_row, key_span, 1) + dv_part, first_row, 1)
        return ((dk_acc, dv_acc), dq_part)
    zero_rows = jnp.zeros((batch, length + 2 * key_reach, depth), jnp.float32)
    steps_index = jnp.arange(length // q_block, dtype=jnp.int32)
    (dk_acc, dv_acc), dq_parts = lax.scan(one_block, (zero_rows, zero_rows), steps_index)
    dq_norm = dq_parts.transpose(1, 0, 2, 3).reshape(batch, length, depth)
    dk_norm = dk_acc[:, key_reach:key_reach + length]
    dv_full = dv_acc[:, key_reach:key_reach + length]
    grad_q = norm_back(q_scale, q_unit, gain_q[:, None, :], dq_norm).astype(jnp.bfloat16)
    grad_k = norm_back(k_scale, k_unit, gain_k[:, None, :], dk_norm).astype(jnp.bfloat16)
    gain_grad_q = lax.optimization_barrier(jnp.sum(dq_norm * q_unit, axis=1))
    gain_grad_k = lax.optimization_barrier(jnp.sum(dk_norm * k_unit, axis=1))
    return (grad_q, grad_k, dv_full.astype(jnp.bfloat16), gain_grad_q, gain_grad_k)

def reference(queries, keys, values, out_grad, gain_q, gain_k, clip_ids, counts):

    def split_rows(tensor):
        return tensor.reshape(N_DP, S_GROUP, HEADS, HD).transpose(0, 2, 1, 3)
    slot_index = jnp.arange(T_DEV, dtype=jnp.int32)
    live = (slot_index[None, None, :] < counts[:, :, None]).astype(jnp.int32).reshape(N_DP, S_GROUP)

    def per_group(row_items):
        q_all, k_all, v_all, d_all, clip, live_rows = row_items

        def per_head(head_items):
            q_one, k_one, v_one, d_one, gq_one, gk_one = head_items
            head_out = group_head(q_one[None], k_one[None], v_one[None], d_one[None], gq_one[None], gk_one[None], clip, live_rows, QB, CLIP_MAX)
            return tuple((result[0] for result in head_out))
        return lax.map(per_head, (q_all, k_all, v_all, d_all, gain_q, gain_k))
    grad_q, grad_k, grad_v, gain_grad_q, gain_grad_k = lax.map(per_group, (split_rows(queries), split_rows(keys), split_rows(values), split_rows(out_grad), clip_ids, live))

    def join_rows(tensor):
        return tensor.transpose(0, 2, 1, 3).reshape(N_DP * S_GROUP, HEADS * HD)
    return (join_rows(grad_q), join_rows(grad_k), join_rows(grad_v), lax.optimization_barrier(jnp.sum(gain_grad_q, axis=0)), lax.optimization_barrier(jnp.sum(gain_grad_k, axis=0)))
```

```python
import jax
import jax.numpy as jnp
from jax import lax
from jax.experimental import pallas as pl
from jax.experimental.pallas import tpu as pltpu
from jax.sharding import PartitionSpec as P

EPS = 1e-06
NEG = -1e30
HD = 128
ROWS = 128
PAIR = 256
HEADS = 16
ALIGN = 16
CAP = 1152
PADDED = CAP + PAIR
SCALE = HD**-0.5
LOG2E = 1.4426950408889634
BF = jnp.bfloat16
F32 = jnp.float32
CORE, A_L, B_L, A_R, B_R, N_L, N_R, PA_L, PB_L, PA_R, PB_R = range(11)


def aligned(index):
    return pl.multiple_of(index, ALIGN)


def lanes(position):
    return pl.ds(pl.multiple_of(position * HD, HD), HD)


def dims(*semantics):
    return pltpu.CompilerParams(
        dimension_semantics=semantics or ("arbitrary",), vmem_limit_bytes=48 * 1024 * 1024
    )


def pick_kernel(core_ref, q_ref, k_ref, v_ref, d_ref, out_ref):
    other = 1 - core_ref[0]
    for t, ref in enumerate((q_ref, k_ref, v_ref, d_ref)):
        for i in range(out_ref.shape[2] // HD):
            out_ref[t, :, i * HD : (i + 1) * HD] = ref[:, lanes(2 * i + other)]


def pick_other(core, tensors, per=4):
    return pl.pallas_call(
        pick_kernel,
        out_shape=jax.ShapeDtypeStruct((4, ROWS, HEADS * HD), BF),
        grid_spec=pltpu.PrefetchScalarGridSpec(
            num_scalar_prefetch=1,
            grid=(HEADS // per,),
            in_specs=[pl.BlockSpec((ROWS, 2 * per * HD), lambda j, m: (0, j))] * 4,
            out_specs=pl.BlockSpec((4, ROWS, per * HD), lambda j, m: (0, 0, j)),
        ),
        compiler_params=dims(),
    )(core, *tensors)


def fill_window(win, slot, core, own_refs, rec_ref, i):
    mine = pl.ds(pl.multiple_of(core * ROWS, ROWS), ROWS)
    theirs = pl.ds(pl.multiple_of((1 - core) * ROWS, ROWS), ROWS)
    for t, ref in enumerate(own_refs):
        win[slot, t, mine, :] = ref[:, lanes(2 * i + core)]
        win[slot, t, theirs, :] = rec_ref[t, :, i * HD : (i + 1) * HD]


def pack_kernel(meta, q_ref, k_ref, v_ref, d_ref, rec_ref, left_ref, right_ref, win):
    per = rec_ref.shape[2] // HD
    core = meta[CORE]
    for i in range(per):
        head = pl.program_id(0) * per + i
        fill_window(win, i, core, (q_ref, k_ref, v_ref, d_ref), rec_ref, i)
        to_left = jnp.where(head < meta[N_L], meta[PB_L] // ALIGN, 0)
        to_right = jnp.where(head >= meta[N_R], meta[PA_R] // ALIGN, 0)
        left_at = head * meta[PB_L]
        right_at = (HEADS - 1 - head) * meta[PA_R]
        tail = PAIR - meta[PA_R]

        def copy_left(n, carry):
            for t in range(4):
                left_ref[t, pl.ds(aligned(left_at + n * ALIGN), ALIGN), :] = win[
                    i, t, pl.ds(aligned(n * ALIGN), ALIGN), :
                ]
            return carry

        def copy_right(n, carry):
            for t in range(4):
                right_ref[t, pl.ds(aligned(right_at + n * ALIGN), ALIGN), :] = win[
                    i, t, pl.ds(aligned(tail + n * ALIGN), ALIGN), :
                ]
            return carry

        lax.fori_loop(0, to_left, copy_left, 0)
        lax.fori_loop(0, to_right, copy_right, 0)


def pack_halos(meta, tensors, rec, per=4):
    out = jax.ShapeDtypeStruct((4, CAP, HD), BF)
    whole = pl.BlockSpec((4, CAP, HD), lambda j, m: (0, 0, 0))
    return pl.pallas_call(
        pack_kernel,
        out_shape=(out, out),
        grid_spec=pltpu.PrefetchScalarGridSpec(
            num_scalar_prefetch=1,
            grid=(HEADS // per,),
            in_specs=[pl.BlockSpec((ROWS, 2 * per * HD), lambda j, m: (0, j))] * 4
            + [pl.BlockSpec((4, ROWS, per * HD), lambda j, m: (0, 0, j))],
            out_specs=(whole, whole),
            scratch_shapes=[pltpu.VMEM((per, 4, PAIR, HD), BF)],
        ),
        compiler_params=dims(),
    )(meta, *tensors, rec)


def matmul(a, b, contract_a, contract_b):
    return lax.dot_general(
        a, b, (((contract_a,), (contract_b,)), ((), ())), preferred_element_type=F32
    )


def norm_parts(rows, gain):
    widened = rows.astype(F32)
    scaled = lax.rsqrt(jnp.mean(widened * widened, axis=-1, keepdims=True) + EPS)
    unit_rows = widened * scaled
    return scaled, unit_rows, (unit_rows * gain).astype(BF)


def norm_back(scaled, unit_rows, gain, upper):
    weighted = gain * upper
    return scaled * (weighted - unit_rows * jnp.mean(unit_rows * weighted, axis=-1, keepdims=True))


def solve(q_rows, k_rows, v_rows, d_rows, gain_q, gain_k, bias, q_live):
    q_scale, q_unit, q_norm = norm_parts(q_rows, gain_q)
    k_scale, k_unit, k_norm = norm_parts(k_rows, gain_k)
    scores = matmul(k_norm, q_norm, 1, 1) * (SCALE * LOG2E) + bias
    exponent = jnp.exp2(scores - jnp.max(scores, axis=0, keepdims=True))
    total = jnp.sum(exponent, axis=0, keepdims=True)
    weights = (exponent * (q_live / total)).astype(BF)
    d_weights = matmul(v_rows, d_rows, 1, 1)
    wide = weights.astype(F32)
    row_delta = jnp.sum(wide * d_weights, axis=0, keepdims=True)
    d_scores = (wide * (d_weights - row_delta)).astype(BF)
    dq_norm = matmul(d_scores, k_norm, 0, 0) * SCALE
    dk_norm = matmul(d_scores, q_norm, 1, 0) * SCALE
    dv_rows = matmul(weights, d_rows, 1, 0)
    grads = (
        norm_back(q_scale, q_unit, gain_q, dq_norm).astype(BF),
        norm_back(k_scale, k_unit, gain_k, dk_norm).astype(BF),
        dv_rows.astype(BF),
    )
    gain_q_part = jnp.sum(dq_norm * q_unit, axis=0, keepdims=True)
    gain_k_part = jnp.sum(dk_norm * k_unit, axis=0, keepdims=True)
    return grads, gain_q_part, gain_k_part


def link_bias(code_row, code_col):
    return jnp.where((code_col == code_row) & (code_row >= 0), 0.0, NEG).astype(F32)


def mid_kernel(
    meta, q_ref, k_ref, v_ref, d_ref, rec_ref, gains_ref, row_ref, col_ref, out_ref, gg_ref, win, bias
):
    per = rec_ref.shape[2] // HD
    core = meta[CORE]

    @pl.when(pl.program_id(0) == 0)
    def _():
        bias[...] = link_bias(row_ref[0:1, :], col_ref[:, 0:1])

    q_live = (row_ref[0:1, :] >= 0).astype(F32)
    for i in range(per):
        fill_window(win, i, core, (q_ref, k_ref, v_ref, d_ref), rec_ref, i)
    for i in range(per):
        head = pl.program_id(0) * per + i
        gains = gains_ref[head]
        grads, part_q, part_k = solve(
            win[i, 0], win[i, 1], win[i, 2], win[i, 3], gains[0:1], gains[1:2], bias[...], q_live
        )
        for t in range(3):
            out_ref[t, :, i * HD : (i + 1) * HD] = grads[t]
        gg_ref[head] = jnp.concatenate([part_q, part_k], axis=0)


def own_specs(per):
    return [pl.BlockSpec((ROWS, 2 * per * HD), lambda j, m: (0, j))] * 4 + [
        pl.BlockSpec((4, ROWS, per * HD), lambda j, m: (0, 0, j))
    ]


def code_specs():
    return [
        pl.BlockSpec((HEADS, 2, HD), lambda j, m: (0, 0, 0)),
        pl.BlockSpec((8, PAIR), lambda j, m: (0, 0)),
        pl.BlockSpec((PAIR, 8), lambda j, m: (0, 0)),
    ]


def solve_mid(meta, tensors, rec, gains, code_rows, code_cols, per=2):
    return pl.pallas_call(
        mid_kernel,
        out_shape=(
            jax.ShapeDtypeStruct((3, PAIR, HEADS * HD), BF),
            jax.ShapeDtypeStruct((HEADS, 2, HD), F32),
        ),
        grid_spec=pltpu.PrefetchScalarGridSpec(
            num_scalar_prefetch=1,
            grid=(HEADS // per,),
            in_specs=own_specs(per) + code_specs(),
            out_specs=(
                pl.BlockSpec((3, PAIR, per * HD), lambda j, m: (0, 0, j)),
                pl.BlockSpec((HEADS, 2, HD), lambda j, m: (0, 0, 0)),
            ),
            scratch_shapes=[
                pltpu.VMEM((per, 4, PAIR, HD), BF),
                pltpu.VMEM((PAIR, PAIR), F32),
            ],
        ),
        compiler_params=dims(),
    )(meta, *tensors, rec, gains, code_rows, code_cols)


def edge_kernel(
    meta,
    q_ref,
    k_ref,
    v_ref,
    d_ref,
    rec_ref,
    gains_ref,
    row_ref,
    col_ref,
    mid_ref,
    gg_mid_ref,
    from_left,
    from_right,
    out_ref,
    gg_ref,
    to_left,
    to_right,
    win,
    bias,
    held_left,
    held_right,
    back_left,
    back_right,
    sems,
):
    per = rec_ref.shape[2] // HD
    core = meta[CORE]
    step = pl.program_id(0)
    row = lax.broadcasted_iota(jnp.int32, (PAIR, HD), 0)

    @pl.when(step == 0)
    def _():
        copies = [
            pltpu.make_async_copy(from_left, held_left.at[:, pl.ds(PAIR, CAP), :], sems.at[0]),
            pltpu.make_async_copy(from_right, held_right.at[:, pl.ds(0, CAP), :], sems.at[1]),
        ]
        for copy in copies:
            copy.start()
        for side in range(2):
            bias[side] = link_bias(
                row_ref[side + 1 : side + 2, :], col_ref[:, side + 1 : side + 2]
            )
        for copy in copies:
            copy.wait()

    out_ref[...] = mid_ref[...]
    for i in range(per):
        fill_window(win, i, core, (q_ref, k_ref, v_ref, d_ref), rec_ref, i)
    for i in range(per):
        head = step * per + i
        gains = gains_ref[head]
        gg_ref[head] = gg_mid_ref[head]
        cols = slice(i * HD, (i + 1) * HD)

        def side_solve(side, held, back, at, halo, local):
            live = (row_ref[side + 1 : side + 2, :] >= 0).astype(F32)
            span = pl.ds(aligned(at), PAIR)
            window = [jnp.where(halo, held[t, span, :], win[i, t]) for t in range(4)]
            grads, part_q, part_k = solve(*window, gains[0:1], gains[1:2], bias[side], live)
            for t in range(3):
                back[t, span, :] = grads[t]
                out_ref[t, :, cols] = jnp.where(local, grads[t], out_ref[t, :, cols])
            gg_ref[head] += jnp.concatenate([part_q, part_k], axis=0)

        @pl.when(head >= meta[N_L])
        def _():
            side_solve(
                0,
                held_left,
                back_left,
                (HEADS - head) * meta[PA_L],
                row >= PAIR - meta[A_L],
                row < meta[B_L],
            )

        @pl.when(head < meta[N_R])
        def _():
            side_solve(
                1,
                held_right,
                back_right,
                head * meta[PB_R],
                row < meta[B_R],
                row >= PAIR - meta[A_R],
            )

    @pl.when(step == pl.num_programs(0) - 1)
    def _():
        copies = [
            pltpu.make_async_copy(back_left.at[:, pl.ds(PAIR, CAP), :], to_left, sems.at[0]),
            pltpu.make_async_copy(back_right.at[:, pl.ds(0, CAP), :], to_right, sems.at[1]),
        ]
        for copy in copies:
            copy.start()
        for copy in copies:
            copy.wait()


def solve_edges(meta, tensors, rec, gains, code_rows, code_cols, mid, gg_mid, halos, per=2):
    block = pl.BlockSpec((3, PAIR, per * HD), lambda j, m: (0, 0, j))
    small = pl.BlockSpec((HEADS, 2, HD), lambda j, m: (0, 0, 0))
    anywhere = pl.BlockSpec(memory_space=pl.ANY)
    back = jax.ShapeDtypeStruct((3, CAP, HD), BF)
    return pl.pallas_call(
        edge_kernel,
        out_shape=(
            jax.ShapeDtypeStruct((3, PAIR, HEADS * HD), BF),
            jax.ShapeDtypeStruct((HEADS, 2, HD), F32),
            back,
            back,
        ),
        grid_spec=pltpu.PrefetchScalarGridSpec(
            num_scalar_prefetch=1,
            grid=(HEADS // per,),
            in_specs=own_specs(per) + code_specs() + [block, small, anywhere, anywhere],
            out_specs=(block, small, anywhere, anywhere),
            scratch_shapes=[
                pltpu.VMEM((per, 4, PAIR, HD), BF),
                pltpu.VMEM((2, PAIR, PAIR), F32),
                pltpu.VMEM((4, PADDED, HD), BF),
                pltpu.VMEM((4, PADDED, HD), BF),
                pltpu.VMEM((3, PADDED, HD), BF),
                pltpu.VMEM((3, PADDED, HD), BF),
                pltpu.SemaphoreType.DMA((2,)),
            ],
        ),
        compiler_params=dims(),
    )(meta, *tensors, rec, gains, code_rows, code_cols, mid, gg_mid, *halos)


def merge_kernel(meta, own_ref, from_left, from_right, keep_ref, send_ref, held, win, sems):
    per = own_ref.shape[2] // HD
    core = meta[CORE]
    row = lax.broadcasted_iota(jnp.int32, (PAIR, HD), 0)

    @pl.when(pl.program_id(0) == 0)
    def _():
        copies = [
            pltpu.make_async_copy(from_left, held.at[0, :, pl.ds(0, CAP), :], sems.at[0]),
            pltpu.make_async_copy(from_right, held.at[1, :, pl.ds(PAIR, CAP), :], sems.at[1]),
        ]
        for copy in copies:
            copy.start()
        for copy in copies:
            copy.wait()

    mine = pl.ds(pl.multiple_of(core * ROWS, ROWS), ROWS)
    theirs = pl.ds(pl.multiple_of((1 - core) * ROWS, ROWS), ROWS)
    for i in range(per):
        head = pl.program_id(0) * per + i
        use_left = head < meta[N_L]
        use_right = head >= meta[N_R]
        left_at = jnp.where(use_left, head * meta[PB_L], 0)
        right_at = jnp.where(use_right, (HEADS - head) * meta[PA_R], 0)
        head_rows = jnp.where(use_left, meta[B_L], 0)
        tail_row = jnp.where(use_right, PAIR - meta[A_R], PAIR)
        cols = slice(i * HD, (i + 1) * HD)
        for t in range(3):
            rows = own_ref[t, :, cols]
            rows = jnp.where(row < head_rows, held[0, t, pl.ds(aligned(left_at), PAIR), :], rows)
            rows = jnp.where(row >= tail_row, held[1, t, pl.ds(aligned(right_at), PAIR), :], rows)
            win[i, t] = rows
        for t in range(3):
            keep_ref[t, :, cols] = win[i, t, mine, :]
            send_ref[t, :, cols] = win[i, t, theirs, :]


def merge_returns(meta, own, returned, per=4):
    out = jax.ShapeDtypeStruct((3, ROWS, HEADS * HD), BF)
    half = pl.BlockSpec((3, ROWS, per * HD), lambda j, m: (0, 0, j))
    anywhere = pl.BlockSpec(memory_space=pl.ANY)
    return pl.pallas_call(
        merge_kernel,
        out_shape=(out, out),
        grid_spec=pltpu.PrefetchScalarGridSpec(
            num_scalar_prefetch=1,
            grid=(HEADS // per,),
            in_specs=[
                pl.BlockSpec((3, PAIR, per * HD), lambda j, m: (0, 0, j)),
                anywhere,
                anywhere,
            ],
            out_specs=(half, half),
            scratch_shapes=[
                pltpu.VMEM((2, 3, PADDED, HD), BF),
                pltpu.VMEM((per, 3, PAIR, HD), BF),
                pltpu.SemaphoreType.DMA((2,)),
            ],
        ),
        compiler_params=dims(),
    )(meta, own, *returned)


def weave_kernel(core_ref, keep_ref, rec_ref, *outs):
    core = core_ref[0]
    for t, out in enumerate(outs):
        for i in range(keep_ref.shape[2] // HD):
            cols = slice(i * HD, (i + 1) * HD)
            out[:, lanes(2 * i + core)] = keep_ref[t, :, cols]
            out[:, lanes(2 * i + 1 - core)] = rec_ref[t, :, cols]


def weave(core, keep, rec, per=4):
    half = pl.BlockSpec((3, ROWS, per * HD), lambda j, m: (0, 0, j))
    return pl.pallas_call(
        weave_kernel,
        out_shape=(jax.ShapeDtypeStruct((ROWS, 2 * HEADS * HD), BF),) * 3,
        grid_spec=pltpu.PrefetchScalarGridSpec(
            num_scalar_prefetch=1,
            grid=(HEADS // per,),
            in_specs=[half, half],
            out_specs=(pl.BlockSpec((ROWS, 2 * per * HD), lambda j, m: (0, j)),) * 3,
        ),
        compiler_params=dims(),
    )(core, keep, rec)


def edge_split(long_a, long_b):
    blocks_a = (long_a + ALIGN - 1) // ALIGN
    blocks_b = (long_b + ALIGN - 1) // ALIGN
    both = jnp.maximum(blocks_a + blocks_b, 1)
    to_left = (2 * HEADS * blocks_a + both) // (2 * both)
    return blocks_a * ALIGN, blocks_b * ALIGN, to_left


def plan(core, chip, chips, ids, counts, left, right):
    left_ids, left_counts = left
    right_ids, right_counts = right
    slot = jnp.arange(PAIR, dtype=jnp.int32)

    def live(pair_counts):
        return slot % ROWS < jnp.where(slot < ROWS, pair_counts[0], pair_counts[1])

    def run(same, crosses):
        return jnp.where(crosses, jnp.sum(same.astype(jnp.int32)), 0)

    cross_l = (chip > 0) & (left_ids[PAIR - 1] == ids[0])
    cross_r = (chip < chips - 1) & (right_ids[0] == ids[PAIR - 1])
    a_l = run(left_ids == left_ids[PAIR - 1], cross_l)
    b_l = run(ids == ids[0], cross_l)
    a_r = run(ids == ids[PAIR - 1], cross_r)
    b_r = run(right_ids == right_ids[0], cross_r)
    pa_l, pb_l, n_l = edge_split(a_l, b_l)
    pa_r, pb_r, n_r = edge_split(a_r, b_r)
    n_l = jnp.where(cross_l, n_l, HEADS)
    n_r = jnp.where(cross_r, n_r, 0)
    own_live = live(counts)
    head_l = slot < b_l
    tail_r = slot >= PAIR - a_r
    code_m = jnp.where(own_live & ~head_l & ~tail_r, ids, -1)
    code_l = jnp.where((own_live & head_l) | (live(left_counts) & (slot >= PAIR - a_l)), 0, -1)
    code_r = jnp.where((own_live & tail_r) | (live(right_counts) & (slot < b_r)), 0, -1)
    codes = jnp.stack([code_m, code_l, code_r] + [code_m] * 5)
    meta = jnp.stack(
        [core, a_l, b_l, a_r, b_r, n_l, n_r, pa_l, pb_l, pa_r, pb_r] + [core] * 5
    ).astype(jnp.int32)
    return meta, codes, codes.T


def shards(queries, keys, values, out_grad, gain_q, gain_k, clip_ids, counts):
    size = lax.axis_size("seq")
    groups = lax.axis_size("dp")
    chips = size // 2
    seq = lax.axis_index("seq")
    core = seq % 2
    chip = seq // 2
    swap = [(i, i ^ 1) for i in range(size)]
    rightward = [(i, i + 2) for i in range(size - 2)]
    leftward = [(i + 2, i) for i in range(size - 2)]
    same_core = [list(range(0, size, 2)), list(range(1, size, 2))]
    core_at = core.reshape(1).astype(jnp.int32)
    tensors = (queries, keys, values, out_grad)

    info = jnp.concatenate([clip_ids, jnp.broadcast_to(counts, (1, ROWS))], axis=0)
    info_other = lax.ppermute(info, "seq", swap)
    first = jnp.where(core == 0, info, info_other)
    second = jnp.where(core == 0, info_other, info)
    chip_info = jnp.stack([first, second])
    info_left = lax.ppermute(chip_info, "seq", rightward)
    info_right = lax.ppermute(chip_info, "seq", leftward)

    def parts(table):
        return table[:, 0, :].reshape(PAIR), table[:, 1, 0]

    meta, code_rows, code_cols = plan(
        core, chip, chips, *parts(chip_info), parts(info_left), parts(info_right)
    )

    rec = lax.ppermute(pick_other(core_at, tensors), "seq", swap)

    gain_own = jnp.concatenate([gain_q, gain_k], axis=0)
    gain_cols = lax.all_to_all(
        jnp.broadcast_to(gain_own[None], (groups,) + gain_own.shape), "dp", 0, 0, tiled=True
    )
    gain_row = gain_cols.transpose(1, 0, 2).reshape(2, HD)
    gains = lax.all_to_all(
        jnp.broadcast_to(gain_row[None], (chips, 2, HD)),
        "seq",
        0,
        0,
        axis_index_groups=same_core,
        tiled=True,
    )

    send_left, send_right = pack_halos(meta, tensors, rec)
    from_left = lax.ppermute(send_right, "seq", rightward)
    from_right = lax.ppermute(send_left, "seq", leftward)

    mid, gg_mid = solve_mid(meta, tensors, rec, gains, code_rows, code_cols)
    own, gg, back_left, back_right = solve_edges(
        meta, tensors, rec, gains, code_rows, code_cols, mid, gg_mid, (from_left, from_right)
    )
    returned_right = lax.ppermute(back_left, "seq", leftward)
    returned_left = lax.ppermute(back_right, "seq", rightward)

    gg_parts = lax.all_to_all(gg, "seq", 0, 0, axis_index_groups=same_core, tiled=True)
    gg_head = jnp.sum(gg_parts, axis=0)
    gg_sum = lax.psum(gg_head, "dp")

    keep, send = merge_returns(meta, own, (returned_left, returned_right))
    grads = weave(core_at, keep, lax.ppermute(send, "seq", swap))
    return (*grads, gg_sum[0:1], gg_sum[1:2])


def solution(mesh):
    rows = P(("dp", "seq"), None)
    cells = P("seq", "dp")
    slots = P("dp", "seq")
    return jax.shard_map(
        shards,
        mesh=mesh,
        in_specs=(rows, rows, rows, rows, cells, cells, slots, slots),
        out_specs=(rows, rows, rows, P("seq", None), P("seq", None)),
        check_vma=False,
    )
```

```python
import functools

import jax
import jax.numpy as jnp
from jax import lax
from jax.experimental import pallas as pl
from jax.experimental.pallas import tpu as pltpu
from jax.sharding import PartitionSpec as P

EPS = 1e-06
NEG = -1e30
HD = 128
ROWS = 128
PAIR = 256
HEADS = 16
ALIGN = 16
LINE = 4
CAP = 1152
FIRST = 768
REST = CAP - FIRST
PADDED = CAP + PAIR
SCALE = HD**-0.5
LOG2E = 1.4426950408889634
BF = jnp.bfloat16
F32 = jnp.float32
CORE, CHIP, A_L, B_L, A_R, B_R, N_L, N_R, PA_L, PB_L, PA_R, PB_R = range(12)
GROUP = 2
ANYWHERE = pl.BlockSpec(memory_space=pl.ANY)
IN_VMEM = pl.BlockSpec(memory_space=pltpu.VMEM)
IN_SMEM = pl.BlockSpec(memory_space=pltpu.SMEM)


def aligned(index):
    return pl.multiple_of(index, ALIGN)


def lanes(position):
    return pl.ds(pl.multiple_of(position * HD, HD), HD)


def params(mib):
    return pltpu.CompilerParams(vmem_limit_bytes=mib * 1024 * 1024)


def whole(shape):
    return pl.BlockSpec(shape, lambda j, m: (0,) * len(shape))


def run_copies(copies):
    for copy in copies:
        copy.start()
    for copy in copies:
        copy.wait()


def rows_of(held, start, length):
    return held.at[:, pl.ds(start, length), :]


def pick_kernel(place, q_ref, k_ref, v_ref, d_ref, out_ref):
    other = 1 - place[CORE]
    for t, ref in enumerate((q_ref, k_ref, v_ref, d_ref)):
        for i in range(out_ref.shape[2] // HD):
            out_ref[t, :, i * HD : (i + 1) * HD] = ref[:, lanes(2 * i + other)]


def pick_other(place, tensors, per=4):
    return pl.pallas_call(
        pick_kernel,
        out_shape=jax.ShapeDtypeStruct((4, ROWS, HEADS * HD), BF),
        grid_spec=pltpu.PrefetchScalarGridSpec(
            num_scalar_prefetch=1,
            grid=(HEADS // per,),
            in_specs=own_specs(per)[:4],
            out_specs=own_specs(per)[4],
        ),
        compiler_params=params(12),
    )(place, *tensors)


def chip_halves(info, core):
    ids, counts = (info[1:2], info[2:3]), (info[0:1, 32:33], info[0:1, 33:34])

    def ordered(mine, other):
        return jnp.where(core == 0, mine, other), jnp.where(core == 0, other, mine)

    return ordered(*ids), ordered(*counts)


def count_equal(halves, wanted):
    hits = [jnp.where(half == wanted, 1.0, 0.0).astype(F32) for half in halves]
    return jnp.sum(hits[0] + hits[1]).astype(jnp.int32)


def edge_split(long_a, long_b):
    blocks_a = lax.div(long_a + ALIGN - 1, ALIGN)
    blocks_b = lax.div(long_b + ALIGN - 1, ALIGN)
    least = HEADS - lax.div(CAP // ALIGN, jnp.maximum(blocks_a, 1))
    most = lax.div(CAP // ALIGN, jnp.maximum(blocks_b, 1))
    to_left = jnp.minimum(jnp.maximum(HEADS // 2, least), most)
    return blocks_a * ALIGN, blocks_b * ALIGN, to_left


def write_plan(place, table, infos, meta):
    core, chip = place[CORE], place[CHIP]
    first = place[GROUP] * HEADS
    spots = (chip, jnp.maximum(chip - 1, 0), jnp.minimum(chip + 1, HEADS - 1))
    for n, spot in enumerate(spots):
        infos[n] = table[first + spot]
    own, _ = chip_halves(infos[0], core)
    left, _ = chip_halves(infos[1], core)
    right, _ = chip_halves(infos[2], core)
    left_last, own_first = jnp.max(left[1]), jnp.min(own[0])
    own_last, right_first = jnp.max(own[1]), jnp.min(right[0])
    cross_l = (chip > 0) & (left_last == own_first)
    cross_r = (chip < HEADS - 1) & (right_first == own_last)
    a_l = jnp.where(cross_l, count_equal(left, left_last), 0)
    b_l = jnp.where(cross_l, count_equal(own, own_first), 0)
    a_r = jnp.where(cross_r, count_equal(own, own_last), 0)
    b_r = jnp.where(cross_r, count_equal(right, right_first), 0)
    pa_l, pb_l, n_l = edge_split(a_l, b_l)
    pa_r, pb_r, n_r = edge_split(a_r, b_r)
    n_l = jnp.where(cross_l, n_l, HEADS)
    n_r = jnp.where(cross_r, n_r, 0)
    values = [core, chip, a_l, b_l, a_r, b_r, n_l, n_r, pa_l, pb_l, pa_r, pb_r]
    for n, value in enumerate(values):
        meta[n] = value


def turns_left(meta):
    return lax.rem(meta[CHIP], LINE) == 0


def turns_right(meta):
    return lax.rem(meta[CHIP], LINE) == LINE - 1


def either(wanted, yes, no):
    @pl.when(wanted)
    def _():
        for copy in yes:
            copy.start()

    @pl.when(jnp.logical_not(wanted))
    def _():
        for copy in no:
            copy.start()


def send_pieces(meta, left, right, left_all, right_all, turn_first, turn_rest, sems):
    def turn_copies(held):
        return [
            pltpu.make_async_copy(held.at[:, pl.ds(0, FIRST), :], turn_first, sems.at[0]),
            pltpu.make_async_copy(held.at[:, pl.ds(FIRST, REST), :], turn_rest, sems.at[1]),
        ]

    by_left, by_right = turn_copies(left), turn_copies(right)
    either(turns_left(meta), by_left, by_right)
    run_copies(
        [
            pltpu.make_async_copy(left, left_all, sems.at[2]),
            pltpu.make_async_copy(right, right_all, sems.at[3]),
        ]
    )
    for copy in by_left:
        copy.wait()


def load_pieces(all_rows, turn_first, turn_rest, held, by_turn, sems):
    spots = [held.at[:, pl.ds(0, FIRST), :], held.at[:, pl.ds(FIRST, REST), :]]
    pieces = [all_rows.at[:, pl.ds(0, FIRST), :], all_rows.at[:, pl.ds(FIRST, REST), :]]

    def copies(sources):
        return [pltpu.make_async_copy(*pair) for pair in zip(sources, spots, sems, strict=True)]

    straight = copies(pieces)
    either(by_turn, copies((turn_first, turn_rest)), straight)
    return straight


def load_both(meta, pieces, held_left, held_right, sems):
    from_left, from_right, turn_first, turn_rest = pieces
    return load_pieces(
        from_left, turn_first, turn_rest, held_left, turns_left(meta), (sems.at[0], sems.at[1])
    ) + load_pieces(
        from_right, turn_first, turn_rest, held_right, turns_right(meta), (sems.at[2], sems.at[3])
    )


def half_rows(half):
    return pl.ds(pl.multiple_of(half * ROWS, ROWS), ROWS)


def fill_windows(win, core, own_refs, rec_ref):
    for i in range(win.shape[0]):
        for t, ref in enumerate(own_refs):
            win[i, t, half_rows(core), :] = ref[:, lanes(2 * i + core)]
            win[i, t, half_rows(1 - core), :] = rec_ref[t, :, i * HD : (i + 1) * HD]


def pack_kernel(
    place,
    q_ref,
    k_ref,
    v_ref,
    d_ref,
    rec_ref,
    table,
    meta,
    infos,
    left_all,
    right_all,
    turn_first,
    turn_rest,
    win,
    left_ref,
    right_ref,
    sems,
):
    per = rec_ref.shape[2] // HD
    core = place[CORE]
    step = pl.program_id(0)

    @pl.when(step == 0)
    def _():
        write_plan(place, table, infos, meta)

    fill_windows(win, core, (q_ref, k_ref, v_ref, d_ref), rec_ref)
    for i in range(per):
        head = step * per + i

        @pl.when(head < meta[N_L])
        def _():
            for t in range(4):
                left_ref[t, pl.ds(aligned(head * meta[PB_L]), PAIR), :] = win[i, t]

        @pl.when(head >= meta[N_R])
        def _():
            for t in range(4):
                right_ref[t, pl.ds(aligned((HEADS - head) * meta[PA_R]), PAIR), :] = win[i, t]

    @pl.when(step == pl.num_programs(0) - 1)
    def _():
        send_pieces(
            meta,
            rows_of(left_ref, 0, CAP),
            rows_of(right_ref, PAIR, CAP),
            left_all,
            right_all,
            turn_first,
            turn_rest,
            sems,
        )


def own_specs(per):
    return [pl.BlockSpec((ROWS, 2 * per * HD), lambda j, m: (0, j))] * 4 + [
        pl.BlockSpec((4, ROWS, per * HD), lambda j, m: (0, 0, j))
    ]


def pieces_shape(tensors):
    return [jax.ShapeDtypeStruct((tensors, n, HD), BF) for n in (CAP, CAP, FIRST, REST)]


def pack_halos(place, tensors, rec, table, per=4):
    return pl.pallas_call(
        pack_kernel,
        out_shape=(
            jax.ShapeDtypeStruct((16,), jnp.int32),
            jax.ShapeDtypeStruct((3, 3, HD), F32),
            *pieces_shape(4),
        ),
        grid_spec=pltpu.PrefetchScalarGridSpec(
            num_scalar_prefetch=1,
            grid=(HEADS // per,),
            in_specs=own_specs(per) + [whole(table.shape)],
            out_specs=(IN_SMEM, whole((3, 3, HD)), *([ANYWHERE] * 4)),
            scratch_shapes=[
                pltpu.VMEM((per, 4, PAIR, HD), BF),
                pltpu.VMEM((4, PADDED, HD), BF),
                pltpu.VMEM((4, PADDED, HD), BF),
                pltpu.SemaphoreType.DMA((4,)),
            ],
        ),
        compiler_params=params(16),
    )(place, *tensors, rec, table)


def matmul(a, b, contract_a, contract_b):
    return lax.dot_general(
        a, b, (((contract_a,), (contract_b,)), ((), ())), preferred_element_type=F32
    )


def norm_parts(rows, gain):
    widened = rows.astype(F32)
    scaled = lax.rsqrt(jnp.mean(widened * widened, axis=-1, keepdims=True) + EPS)
    unit_rows = widened * scaled
    return scaled, unit_rows, (unit_rows * gain).astype(BF)


def norm_back(scaled, unit_rows, gain, upper):
    terms = upper * unit_rows
    gain = gain * SCALE
    mean = jnp.mean(terms * gain, axis=-1, keepdims=True)
    grad = scaled * (gain * upper - unit_rows * mean)
    return grad.astype(BF), jnp.sum(terms, axis=0, keepdims=True) * SCALE


def solve(problems):
    each = range(len(problems))
    q_rows, k_rows, v_rows, d_rows, gain_q, gain_k, bias, q_live = zip(*problems, strict=True)
    q_parts = [norm_parts(q_rows[n], gain_q[n]) for n in each]
    k_parts = [norm_parts(k_rows[n], gain_k[n]) for n in each]
    raw = [matmul(k_parts[n][2], q_parts[n][2], 1, 1) for n in each]
    d_weights = [matmul(v_rows[n], d_rows[n], 1, 1) for n in each]
    weights = []
    for n in each:
        scores = raw[n] * (SCALE * LOG2E) + bias[n]
        exponent = jnp.exp2(scores - jnp.max(scores, axis=0, keepdims=True))
        total = jnp.sum(exponent, axis=0, keepdims=True)
        weights.append((exponent * (q_live[n] / total)).astype(BF))
    dv_rows = [matmul(weights[n], d_rows[n], 1, 0) for n in each]
    d_scores = []
    for n in each:
        wide = weights[n].astype(F32)
        row_delta = jnp.sum(wide * d_weights[n], axis=0, keepdims=True)
        d_scores.append((wide * (d_weights[n] - row_delta)).astype(BF))
    dk = [matmul(d_scores[n], q_parts[n][2], 1, 0) for n in each]
    dq = [matmul(d_scores[n], k_parts[n][2], 0, 0) for n in each]
    results = []
    for n in each:
        grad_k, gain_k_part = norm_back(k_parts[n][0], k_parts[n][1], gain_k[n], dk[n])
        grad_q, gain_q_part = norm_back(q_parts[n][0], q_parts[n][1], gain_q[n], dq[n])
        grads = (grad_q, grad_k, dv_rows[n].astype(BF))
        results.append((grads, gain_q_part, gain_k_part))
    return results


def link_codes(side, core, meta, infos):
    own_ids, own_counts = chip_halves(infos[0], core)
    _, far_counts = chip_halves(infos[side], core)
    codes = []
    for half in range(2):
        lane = lax.broadcasted_iota(jnp.int32, (1, ROWS), 1)
        slot = lane + half * ROWS
        live = lane.astype(F32) < own_counts[half]
        far = lane.astype(F32) < far_counts[half]
        if side == 0:
            inside = live & (slot >= meta[B_L]) & (slot < PAIR - meta[A_R])
            code = jnp.where(inside, own_ids[half], -1.0)
        elif side == 1:
            inside = (live & (slot < meta[B_L])) | (far & (slot >= PAIR - meta[A_L]))
            code = jnp.where(inside, 0.0, -1.0)
        else:
            inside = (live & (slot >= PAIR - meta[A_R])) | (far & (slot < meta[B_R]))
            code = jnp.where(inside, 0.0, -1.0)
        codes.append(code.astype(F32))
    return codes


def fill_links(bias, q_live, codes):
    for a in range(2):
        q_live[0:1, a * ROWS : (a + 1) * ROWS] = (codes[a] >= 0.0).astype(F32)
        key_codes = jnp.broadcast_to(codes[a], (ROWS, ROWS)).T
        for b in range(2):
            linked = (key_codes == codes[b]) & (codes[b] >= 0.0)
            bias[a * ROWS : (a + 1) * ROWS, b * ROWS : (b + 1) * ROWS] = jnp.where(
                linked, 0.0, NEG
            ).astype(F32)


def gather_gains(table, gains):
    groups = table.shape[0] // HEADS
    width = HD // groups
    for n in range(groups):
        part = table[n * HEADS : (n + 1) * HEADS, 0:1, :]
        cols = slice(n * width, (n + 1) * width)
        gains[:, 0:1, cols] = part[:, :, 0:width]
        gains[:, 1:2, cols] = part[:, :, width : 2 * width]


def mid_kernel(
    meta,
    q_ref,
    k_ref,
    v_ref,
    d_ref,
    rec_ref,
    infos,
    table,
    out_ref,
    gg_ref,
    gains_ref,
    win,
    bias,
    q_live,
):
    per = rec_ref.shape[2] // HD
    core = meta[CORE]

    @pl.when(pl.program_id(0) == 0)
    def _():
        gather_gains(table, gains_ref)
        fill_links(bias, q_live, link_codes(0, core, meta, infos))

    fill_windows(win, core, (q_ref, k_ref, v_ref, d_ref), rec_ref)
    heads = [pl.program_id(0) * per + i for i in range(per)]
    gains = [gains_ref[head] for head in heads]
    results = solve(
        [
            (*(win[i, t] for t in range(4)), gains[i][0:1], gains[i][1:2], bias[...], q_live[0:1, :])
            for i in range(per)
        ]
    )
    for i, (grads, part_q, part_k) in enumerate(results):
        for t in range(3):
            for half in range(2):
                out_ref[lax.rem(half + core, 2), t, :, i * HD : (i + 1) * HD] = grads[t][
                    half * ROWS : (half + 1) * ROWS
                ]
        gg_ref[heads[i]] = jnp.concatenate([part_q, part_k], axis=0)


def solve_mid(meta, tensors, rec, infos, table, per=4):
    per_head = jax.ShapeDtypeStruct((HEADS, 2, HD), F32)
    return pl.pallas_call(
        mid_kernel,
        out_shape=(jax.ShapeDtypeStruct((2, 3, ROWS, HEADS * HD), BF), per_head, per_head),
        grid_spec=pltpu.PrefetchScalarGridSpec(
            num_scalar_prefetch=1,
            grid=(HEADS // per,),
            in_specs=own_specs(per) + [whole(infos.shape), whole(table.shape)],
            out_specs=(half_spec(per), whole(per_head.shape), whole(per_head.shape)),
            scratch_shapes=[
                pltpu.VMEM((per, 4, PAIR, HD), BF),
                pltpu.VMEM((PAIR, PAIR), F32),
                pltpu.VMEM((8, PAIR), F32),
            ],
        ),
        compiler_params=params(32),
    )(meta, *tensors, rec, infos, table)


def half_spec(per):
    return pl.BlockSpec((2, 3, ROWS, per * HD), lambda j, m: (0, 0, 0, j))


def row_numbers(rows):
    return lax.broadcasted_iota(jnp.int32, (rows, HD), 0).astype(F32).astype(BF)


def bound(value):
    return jnp.full((1, HD), value, jnp.int32).astype(F32).astype(BF)


def edge_kernel(
    meta,
    q_ref,
    k_ref,
    v_ref,
    d_ref,
    rec_ref,
    infos,
    gains_ref,
    mid_ref,
    gg_mid_ref,
    from_left,
    from_right,
    from_turn_first,
    from_turn_rest,
    out_ref,
    gg_ref,
    left_all,
    right_all,
    turn_first,
    turn_rest,
    win,
    bias,
    q_live,
    held,
    back,
    sems,
):
    per = rec_ref.shape[2] // HD
    core = meta[CORE]
    step = pl.program_id(0)

    @pl.when(step == 0)
    def _():
        copies = load_both(
            meta,
            (from_left, from_right, from_turn_first, from_turn_rest),
            rows_of(held.at[0], PAIR, CAP),
            rows_of(held.at[1], 0, CAP),
            sems,
        )
        for side in range(2):
            fill_links(
                bias.at[side], q_live.at[side], link_codes(side + 1, core, meta, infos)
            )
        gg_ref[...] = gg_mid_ref[...]
        for copy in copies:
            copy.wait()

    fill_windows(win, core, (q_ref, k_ref, v_ref, d_ref), rec_ref)
    out_ref[...] = mid_ref[...]
    heads = [step * per + i for i in range(per)]
    on_left = [head >= meta[N_L] for head in heads]
    on_right = [head < meta[N_R] for head in heads]
    row = row_numbers(PAIR)

    def solve_side(lefts, rights):
        problems, spots = [], []
        for i, head in enumerate(heads):
            side = jnp.where(lefts[i], 0, 1)
            use = jnp.logical_or(lefts[i], rights[i])
            at = jnp.where(lefts[i], (HEADS - head) * meta[PA_L], head * meta[PB_R])
            span = pl.ds(aligned(jnp.where(use, at, PADDED)), PAIR)
            source = pl.ds(aligned(jnp.where(use, at, 0)), PAIR)
            halo = (row >= bound(jnp.where(lefts[i], PAIR - meta[A_L], 0))) & (
                row < bound(jnp.where(lefts[i], PAIR, jnp.where(use, meta[B_R], 0)))
            )
            local = (row >= bound(jnp.where(lefts[i], 0, PAIR - meta[A_R]))) & (
                row < bound(jnp.where(lefts[i], meta[B_L], jnp.where(use, PAIR, 0)))
            )
            window = [jnp.where(halo, held[side, t, source, :], win[i, t]) for t in range(4)]
            gains = gains_ref[head]
            problems.append((*window, gains[0:1], gains[1:2], bias[side], q_live[side, 0:1, :]))
            spots.append((side, span, local, use.astype(F32)))
        for i, (grads, part_q, part_k) in enumerate(solve(problems)):
            side, span, local, counts = spots[i]
            cols = slice(i * HD, (i + 1) * HD)
            for t in range(3):
                back[side, t, span, :] = grads[t]
                for half in range(2):
                    rows = slice(half * ROWS, (half + 1) * ROWS)
                    place = lax.rem(half + core, 2)
                    out_ref[place, t, :, cols] = jnp.where(
                        local[rows], grads[t][rows], out_ref[place, t, :, cols]
                    )
            gg_ref[heads[i]] += jnp.concatenate([part_q, part_k], axis=0) * counts

    def some(flags):
        return functools.reduce(jnp.logical_or, flags)

    @pl.when(some(on_left + on_right))
    def _():
        solve_side(on_left, on_right)

    both = [jnp.logical_and(*pair) for pair in zip(on_left, on_right, strict=True)]

    @pl.when(some(both))
    def _():
        solve_side([jnp.logical_and(flag, jnp.logical_not(flag)) for flag in both], both)

    @pl.when(step == pl.num_programs(0) - 1)
    def _():
        send_pieces(
            meta,
            rows_of(back.at[0], PAIR, CAP),
            rows_of(back.at[1], 0, CAP),
            left_all,
            right_all,
            turn_first,
            turn_rest,
            sems,
        )


def solve_edges(meta, tensors, rec, infos, gains, mid, gg_mid, halos, per=4):
    return pl.pallas_call(
        edge_kernel,
        out_shape=(
            jax.ShapeDtypeStruct(mid.shape, BF),
            jax.ShapeDtypeStruct(gg_mid.shape, F32),
            *pieces_shape(3),
        ),
        grid_spec=pltpu.PrefetchScalarGridSpec(
            num_scalar_prefetch=1,
            grid=(HEADS // per,),
            in_specs=own_specs(per)
            + [whole(infos.shape), whole(gains.shape), half_spec(per), whole(gg_mid.shape)]
            + [ANYWHERE] * 4,
            out_specs=(half_spec(per), whole(gg_mid.shape), *([ANYWHERE] * 4)),
            scratch_shapes=[
                pltpu.VMEM((per, 4, PAIR, HD), BF),
                pltpu.VMEM((2, PAIR, PAIR), F32),
                pltpu.VMEM((2, 8, PAIR), F32),
                pltpu.VMEM((2, 4, PADDED, HD), BF),
                pltpu.VMEM((2, 3, PADDED + PAIR, HD), BF),
                pltpu.SemaphoreType.DMA((4,)),
            ],
        ),
        compiler_params=params(40),
    )(meta, *tensors, rec, infos, gains, mid, gg_mid, *halos)


def load_returned(meta, pieces, held_left, held_right, sems):
    for copy in load_both(
        meta, pieces, rows_of(held_left, 0, CAP), rows_of(held_right, PAIR, CAP), sems
    ):
        copy.wait()


def merged(meta, head, half, rows, held_left, held_right):
    use_left = head < meta[N_L]
    use_right = head >= meta[N_R]
    base = half * ROWS
    left_at = jnp.where(use_left, head * meta[PB_L], 0) + base
    right_at = jnp.where(use_right, (HEADS - head) * meta[PA_R], 0) + base
    row = row_numbers(ROWS)
    at_head = row < bound(jnp.where(use_left, meta[B_L], 0) - base)
    at_tail = row >= bound(jnp.where(use_right, PAIR - meta[A_R], PAIR) - base)
    done = []
    for t, part in enumerate(rows):
        part = jnp.where(at_head, held_left[t, pl.ds(aligned(left_at), ROWS), :], part)
        part = jnp.where(at_tail, held_right[t, pl.ds(aligned(right_at), ROWS), :], part)
        done.append(part)
    return done


def merge_kernel(meta, in_ref, *refs):
    pieces, (_, send_ref, held_left, held_right, sems) = refs[:4], refs[4:]
    per = in_ref.shape[3] // HD
    step = pl.program_id(0)

    @pl.when(step == 0)
    def _():
        load_returned(meta, pieces, held_left, held_right, sems)

    for i in range(per):
        cols = slice(i * HD, (i + 1) * HD)
        rows = [in_ref[0, t, :, cols] for t in range(3)]
        rows = merged(meta, step * per + i, 1 - meta[CORE], rows, held_left, held_right)
        for t in range(3):
            send_ref[t, :, cols] = rows[t]


def held_scratch():
    return [
        pltpu.VMEM((3, PADDED, HD), BF),
        pltpu.VMEM((3, PADDED, HD), BF),
        pltpu.SemaphoreType.DMA((4,)),
    ]


def merge_other(meta, own, returned, after, per=4):
    return pl.pallas_call(
        merge_kernel,
        out_shape=jax.ShapeDtypeStruct((3, ROWS, HEADS * HD), BF),
        grid_spec=pltpu.PrefetchScalarGridSpec(
            num_scalar_prefetch=1,
            grid=(HEADS // per,),
            in_specs=[pl.BlockSpec((1, 3, ROWS, per * HD), lambda j, m: (1, 0, 0, j))]
            + [ANYWHERE] * 5,
            out_specs=pl.BlockSpec((3, ROWS, per * HD), lambda j, m: (0, 0, j)),
            scratch_shapes=held_scratch(),
        ),
        compiler_params=params(16),
    )(meta, own, *returned, after)


def weave_kernel(meta, in_ref, rec_ref, *refs):
    pieces, (gg_parts, *outs, gg_q, gg_k, held_left, held_right, sems) = refs[:4], refs[4:]
    per = in_ref.shape[3] // HD
    core = meta[CORE]
    step = pl.program_id(0)

    @pl.when(step == 0)
    def _():
        load_returned(meta, pieces, held_left, held_right, sems)
        total = jnp.sum(gg_parts[...], axis=0)
        gg_q[...] = total[0:1]
        gg_k[...] = total[1:2]

    for i in range(per):
        cols = slice(i * HD, (i + 1) * HD)
        rows = [in_ref[0, t, :, cols] for t in range(3)]
        rows = merged(meta, step * per + i, core, rows, held_left, held_right)
        for t in range(3):
            outs[t][:, lanes(2 * i + core)] = rows[t]
            outs[t][:, lanes(2 * i + 1 - core)] = rec_ref[t, :, cols]


def weave(meta, own, rec, returned, gg_parts, per=4):
    return pl.pallas_call(
        weave_kernel,
        out_shape=(jax.ShapeDtypeStruct((ROWS, 2 * HEADS * HD), BF),) * 3
        + (jax.ShapeDtypeStruct((1, HD), F32),) * 2,
        grid_spec=pltpu.PrefetchScalarGridSpec(
            num_scalar_prefetch=1,
            grid=(HEADS // per,),
            in_specs=[
                pl.BlockSpec((1, 3, ROWS, per * HD), lambda j, m: (0, 0, 0, j)),
                pl.BlockSpec((3, ROWS, per * HD), lambda j, m: (0, 0, j)),
            ]
            + [ANYWHERE] * 4
            + [whole(gg_parts.shape)],
            out_specs=(pl.BlockSpec((ROWS, 2 * per * HD), lambda j, m: (0, j)),) * 3
            + (whole((1, HD)),) * 2,
            scratch_shapes=held_scratch(),
        ),
        compiler_params=params(16),
    )(meta, own, rec, *returned, gg_parts)


def exchange(pieces, size):
    left_all, right_all, turn_first, turn_rest = pieces
    line = 2 * LINE
    wrap = line - 2
    turns = [(i, i + 2) for i in range(size - 2) if i % line >= wrap]
    straight = [(i, i + 2) for i in range(size - 2) if i % line < wrap]

    def back(pairs):
        return [(j, i) for i, j in pairs]

    def move(array, pairs):
        return lax.ppermute(array, "seq", pairs)

    hop = move(turn_rest, [(i, i - wrap) for i, _ in turns] + [(j, j + wrap) for _, j in turns])
    from_left = move(right_all, straight)
    from_right = move(left_all, back(straight))
    from_turn = move(turn_first, turns + back(turns))
    from_hop = move(hop, [(i - wrap, j) for i, j in turns] + [(j + wrap, i) for i, j in turns])
    return from_left, from_right, from_turn, from_hop


def shards(queries, keys, values, out_grad, gain_q, gain_k, clip_ids, counts):
    size = lax.axis_size("seq")
    groups = lax.axis_size("dp")
    chips = size // 2
    seq = lax.axis_index("seq")
    swap = [(i, i ^ 1) for i in range(size)]
    place = jnp.stack([seq % 2, seq // 2, lax.axis_index("dp")]).astype(jnp.int32)
    tensors = tuple(
        pltpu.with_memory_space_constraint(t, pltpu.HBM)
        for t in (queries, keys, values, out_grad)
    )

    def all_to_all(array):
        same_core = [
            [d * size + 2 * c + core for d in range(groups) for c in range(chips)]
            for core in range(2)
        ]
        return lax.all_to_all(
            array, ("dp", "seq"), 0, 0, axis_index_groups=same_core, tiled=True
        )

    info = jnp.concatenate([clip_ids, jnp.broadcast_to(counts, (1, ROWS))], axis=0).astype(F32)
    info_other = lax.ppermute(info, "seq", swap)
    rec = lax.ppermute(pick_other(place, tensors), "seq", swap)
    cells = [gain_q, gain_k, info[1:2, 0:1], info_other[1:2, 0:1]]
    filled = sum(cell.shape[1] for cell in cells)
    first = jnp.concatenate(cells + [jnp.zeros((1, HD - filled), F32)], axis=1)
    known = jnp.concatenate([first, info[0:1], info_other[0:1]], axis=0)
    table = all_to_all(jnp.broadcast_to(known[None], (groups * chips,) + known.shape))

    meta, infos, *pieces = pack_halos(place, tensors, rec, table)
    halos = exchange(pieces, size)
    mid, gg_mid, gains = solve_mid(meta, tensors, rec, infos, table)
    own, gg, *pieces = solve_edges(meta, tensors, rec, infos, gains, mid, gg_mid, halos)
    returned = exchange(pieces, size)
    gg_parts = all_to_all(
        jnp.broadcast_to(gg[None], (groups,) + gg.shape).reshape(groups * chips, 2, HD)
    )
    send = merge_other(meta, own, returned, gg_parts)
    other = lax.ppermute(send, "seq", swap)
    return tuple(weave(meta, own, other, returned, gg_parts))


def solution(mesh):
    rows = P(("dp", "seq"), None)
    cells = P("seq", "dp")
    slots = P("dp", "seq")
    return jax.shard_map(
        shards,
        mesh=mesh,
        in_specs=(rows, rows, rows, rows, cells, cells, slots, slots),
        out_specs=(rows, rows, rows, P("seq", None), P("seq", None)),
        check_vma=False,
    )
```

```python
import functools

import jax
import jax.numpy as jnp
from jax import lax
from jax.experimental import pallas as pl
from jax.experimental.pallas import tpu as pltpu
from jax.sharding import PartitionSpec as P

EPS = 1e-06
NEG = -1e30
HD = 128
ROWS = 128
PAIR = 256
HEADS = 16
ALIGN = 16
LINE = 4
CAP = 1152
FIRST = 768
REST = CAP - FIRST
HALF = CAP // 2
PADDED = CAP + PAIR
SCALE = HD**-0.5
LOG2E = 1.4426950408889634
BF = jnp.bfloat16
F32 = jnp.float32
CORE, CHIP, A_L, B_L, A_R, B_R, N_L, N_R, PA_L, PB_L, PA_R, PB_R = range(12)
KNOWN = 5
ANYWHERE = pl.BlockSpec(memory_space=pl.ANY)
IN_VMEM = pl.BlockSpec(memory_space=pltpu.VMEM)
IN_SMEM = pl.BlockSpec(memory_space=pltpu.SMEM)


def aligned(index):
    return pl.multiple_of(index, ALIGN)


def lanes(position):
    return pl.ds(pl.multiple_of(position * HD, HD), HD)


def params(mib):
    return pltpu.CompilerParams(vmem_limit_bytes=mib * 1024 * 1024)


def whole(shape):
    return pl.BlockSpec(shape, lambda j, m: (0,) * len(shape))


def run_copies(copies):
    for copy in copies:
        copy.start()
    for copy in copies:
        copy.wait()


def rows_of(held, start, length):
    return held.at[:, pl.ds(start, length), :]


def pick_kernel(
    place, q_ref, k_ref, v_ref, d_ref, gain_cols, info, info_other, out_ref, known_ref, row
):
    other = 1 - place[CORE]

    @pl.when(pl.program_id(0) == 0)
    def _():
        width = gain_cols.shape[2]
        row[...] = jnp.zeros_like(row)
        for n in range(gain_cols.shape[0]):
            row[0:2, n * width : (n + 1) * width] = gain_cols[n]
        row[2:3, :] = info[0:1, :]
        row[3:4, :] = info_other[0:1, :]
        row[4:5, 0:1] = info[1:2, 0:1]
        row[4:5, 1:2] = info_other[1:2, 0:1]
        known_ref[...] = jnp.broadcast_to(row[0:KNOWN, :][None], known_ref.shape)

    for t, ref in enumerate((q_ref, k_ref, v_ref, d_ref)):
        for i in range(out_ref.shape[2] // HD):
            out_ref[t, :, i * HD : (i + 1) * HD] = ref[:, lanes(2 * i + other)]


def pick_other(place, tensors, gain_cols, info, info_other, per=4):
    known = jax.ShapeDtypeStruct((HEADS, KNOWN, HD), F32)
    small = (gain_cols, info, info_other)
    return pl.pallas_call(
        pick_kernel,
        out_shape=(jax.ShapeDtypeStruct((4, ROWS, HEADS * HD), BF), known),
        grid_spec=pltpu.PrefetchScalarGridSpec(
            num_scalar_prefetch=1,
            grid=(HEADS // per,),
            in_specs=own_specs(per)[:4] + [whole(array.shape) for array in small],
            out_specs=(own_specs(per)[4], whole(known.shape)),
            scratch_shapes=[pltpu.VMEM((8, HD), F32)],
        ),
        compiler_params=params(12),
    )(place, *tensors, *small)


def chip_halves(info, core):
    ids, counts = (info[0:1], info[1:2]), (info[2:3, 0:1], info[2:3, 1:2])

    def ordered(mine, other):
        return jnp.where(core == 0, mine, other), jnp.where(core == 0, other, mine)

    return ordered(*ids), ordered(*counts)


def count_equal(halves, wanted):
    hits = [jnp.where(half == wanted, 1.0, 0.0).astype(F32) for half in halves]
    return jnp.sum(hits[0] + hits[1]).astype(jnp.int32)


def edge_split(long_a, long_b):
    blocks_a = lax.div(long_a + ALIGN - 1, ALIGN)
    blocks_b = lax.div(long_b + ALIGN - 1, ALIGN)
    least = HEADS - lax.div(CAP // ALIGN, jnp.maximum(blocks_a, 1))
    most = lax.div(CAP // ALIGN, jnp.maximum(blocks_b, 1))
    to_left = jnp.minimum(jnp.maximum(HEADS // 2, least), most)
    return blocks_a * ALIGN, blocks_b * ALIGN, to_left


def chip_infos(table, chip):
    spots = (chip, jnp.maximum(chip - 1, 0), jnp.minimum(chip + 1, HEADS - 1))
    return [table[spot][2:KNOWN] for spot in spots]


def write_plan(place, table, meta):
    core, chip = place[CORE], place[CHIP]
    infos = chip_infos(table, chip)
    own, _ = chip_halves(infos[0], core)
    left, _ = chip_halves(infos[1], core)
    right, _ = chip_halves(infos[2], core)
    left_last, own_first = jnp.max(left[1]), jnp.min(own[0])
    own_last, right_first = jnp.max(own[1]), jnp.min(right[0])
    cross_l = (chip > 0) & (left_last == own_first)
    cross_r = (chip < HEADS - 1) & (right_first == own_last)
    a_l = jnp.where(cross_l, count_equal(left, left_last), 0)
    b_l = jnp.where(cross_l, count_equal(own, own_first), 0)
    a_r = jnp.where(cross_r, count_equal(own, own_last), 0)
    b_r = jnp.where(cross_r, count_equal(right, right_first), 0)
    pa_l, pb_l, n_l = edge_split(a_l, b_l)
    pa_r, pb_r, n_r = edge_split(a_r, b_r)
    n_l = jnp.where(cross_l, n_l, HEADS)
    n_r = jnp.where(cross_r, n_r, 0)
    values = [core, chip, a_l, b_l, a_r, b_r, n_l, n_r, pa_l, pb_l, pa_r, pb_r]
    for n, value in enumerate(values):
        meta[n] = value


def turns_left(meta):
    return lax.rem(meta[CHIP], LINE) == 0


def turns_right(meta):
    return lax.rem(meta[CHIP], LINE) == LINE - 1


def either(wanted, yes, no):
    @pl.when(wanted)
    def _():
        for copy in yes:
            copy.start()

    @pl.when(jnp.logical_not(wanted))
    def _():
        for copy in no:
            copy.start()


def cut(table, *lengths):
    starts = [sum(lengths[:n]) for n in range(len(lengths))]
    return [table.at[:, pl.ds(a, n), :] for a, n in zip(starts, lengths, strict=True)]


def copies_of(sources, targets, sems):
    return [pltpu.make_async_copy(*trio) for trio in zip(sources, targets, sems, strict=True)]


def send_pieces(meta, left, right, pieces, sems):
    left_pieces, right_pieces, turn_pieces = pieces[0:2], pieces[2:4], pieces[4:6]
    turn_sems = [sems.at[0], sems.at[1]]
    by_left = copies_of(cut(left, FIRST, REST), turn_pieces, turn_sems)
    by_right = copies_of(cut(right, FIRST, REST), turn_pieces, turn_sems)
    either(turns_left(meta), by_left, by_right)
    run_copies(
        copies_of(
            cut(left, HALF, HALF) + cut(right, HALF, HALF),
            (*left_pieces, *right_pieces),
            [sems.at[n] for n in range(2, 6)],
        )
    )
    for copy in by_left:
        copy.wait()


def load_pieces(straight_pieces, turn_pieces, held, by_turn, sems):
    spots = cut(held, HALF, FIRST - HALF, REST)
    straight = [straight_pieces[0], *cut(straight_pieces[1], FIRST - HALF, REST)]
    turned = [*cut(turn_pieces[0], HALF, FIRST - HALF), turn_pieces[1]]
    plain = copies_of(straight, spots, sems)
    either(by_turn, copies_of(turned, spots, sems), plain)
    return plain


def load_both(meta, pieces, held_left, held_right, sems):
    turn_pieces = pieces[4:6]
    lefts, rights = [sems.at[n] for n in range(3)], [sems.at[n] for n in range(3, 6)]
    return load_pieces(
        pieces[0:2], turn_pieces, held_left, turns_left(meta), lefts
    ) + load_pieces(pieces[2:4], turn_pieces, held_right, turns_right(meta), rights)


def half_rows(half):
    return pl.ds(pl.multiple_of(half * ROWS, ROWS), ROWS)


def fill_windows(win, core, own_refs, rec_ref):
    for i in range(win.shape[0]):
        for t, ref in enumerate(own_refs):
            win[i, t, half_rows(core), :] = ref[:, lanes(2 * i + core)]
            win[i, t, half_rows(1 - core), :] = rec_ref[t, :, i * HD : (i + 1) * HD]


def pack_kernel(
    place,
    q_ref,
    k_ref,
    v_ref,
    d_ref,
    rec_ref,
    table,
    meta,
    left_first,
    left_second,
    right_first,
    right_second,
    turn_first,
    turn_rest,
    win,
    left_ref,
    right_ref,
    sems,
):
    per = rec_ref.shape[2] // HD
    core = place[CORE]
    step = pl.program_id(0)

    @pl.when(step == 0)
    def _():
        write_plan(place, table, meta)

    fill_windows(win, core, (q_ref, k_ref, v_ref, d_ref), rec_ref)
    for i in range(per):
        head = step * per + i

        @pl.when(head < meta[N_L])
        def _():
            for t in range(4):
                left_ref[t, pl.ds(aligned(head * meta[PB_L]), PAIR), :] = win[i, t]

        @pl.when(head >= meta[N_R])
        def _():
            for t in range(4):
                right_ref[t, pl.ds(aligned((HEADS - head) * meta[PA_R]), PAIR), :] = win[i, t]

    @pl.when(step == pl.num_programs(0) - 1)
    def _():
        send_pieces(
            meta,
            rows_of(left_ref, 0, CAP),
            rows_of(right_ref, PAIR, CAP),
            (left_first, left_second, right_first, right_second, turn_first, turn_rest),
            sems,
        )


def own_specs(per):
    return [pl.BlockSpec((ROWS, 2 * per * HD), lambda j, m: (0, j))] * 4 + [
        pl.BlockSpec((4, ROWS, per * HD), lambda j, m: (0, 0, j))
    ]


def pieces_shape(tensors):
    return [jax.ShapeDtypeStruct((tensors, n, HD), BF) for n in (HALF, HALF, HALF, HALF, FIRST, REST)]


def pack_halos(place, tensors, rec, table, per=4):
    return pl.pallas_call(
        pack_kernel,
        out_shape=(
            jax.ShapeDtypeStruct((16,), jnp.int32),
            *pieces_shape(4),
        ),
        grid_spec=pltpu.PrefetchScalarGridSpec(
            num_scalar_prefetch=1,
            grid=(HEADS // per,),
            in_specs=own_specs(per) + [whole(table.shape)],
            out_specs=(IN_SMEM, *([ANYWHERE] * 6)),
            scratch_shapes=[
                pltpu.VMEM((per, 4, PAIR, HD), BF),
                pltpu.VMEM((4, PADDED, HD), BF),
                pltpu.VMEM((4, PADDED, HD), BF),
                pltpu.SemaphoreType.DMA((6,)),
            ],
        ),
        compiler_params=params(16),
    )(place, *tensors, rec, table)


def matmul(a, b, contract_a, contract_b):
    return lax.dot_general(
        a, b, (((contract_a,), (contract_b,)), ((), ())), preferred_element_type=F32
    )


def norm_parts(rows, gain):
    widened = rows.astype(F32)
    scaled = lax.rsqrt(jnp.mean(widened * widened, axis=-1, keepdims=True) + EPS)
    unit_rows = widened * scaled
    return scaled, unit_rows, (unit_rows * gain).astype(BF)


def norm_back(scaled, unit_rows, gain, upper):
    terms = upper * unit_rows
    gain = gain * SCALE
    mean = jnp.mean(terms * gain, axis=-1, keepdims=True)
    grad = scaled * (gain * upper - unit_rows * mean)
    return grad.astype(BF), jnp.sum(terms, axis=0, keepdims=True) * SCALE


def solve(problems):
    each = range(len(problems))
    q_rows, k_rows, v_rows, d_rows, gain_q, gain_k, bias, q_live = zip(*problems, strict=True)
    q_parts = [norm_parts(q_rows[n], gain_q[n]) for n in each]
    k_parts = [norm_parts(k_rows[n], gain_k[n]) for n in each]
    raw = [matmul(k_parts[n][2], q_parts[n][2], 1, 1) for n in each]
    d_weights = [matmul(v_rows[n], d_rows[n], 1, 1) for n in each]
    weights = []
    for n in each:
        scores = raw[n] * (SCALE * LOG2E) + bias[n]
        exponent = jnp.exp2(scores - jnp.max(scores, axis=0, keepdims=True))
        total = jnp.sum(exponent, axis=0, keepdims=True)
        weights.append((exponent * (q_live[n] / total)).astype(BF))
    dv_rows = [matmul(weights[n], d_rows[n], 1, 0) for n in each]
    d_scores = []
    for n in each:
        wide = weights[n].astype(F32)
        row_delta = jnp.sum(wide * d_weights[n], axis=0, keepdims=True)
        d_scores.append((wide * (d_weights[n] - row_delta)).astype(BF))
    dk = [matmul(d_scores[n], q_parts[n][2], 1, 0) for n in each]
    dq = [matmul(d_scores[n], k_parts[n][2], 0, 0) for n in each]
    results = []
    for n in each:
        grad_k, gain_k_part = norm_back(k_parts[n][0], k_parts[n][1], gain_k[n], dk[n])
        grad_q, gain_q_part = norm_back(q_parts[n][0], q_parts[n][1], gain_q[n], dq[n])
        grads = (grad_q, grad_k, dv_rows[n].astype(BF))
        results.append((grads, gain_q_part, gain_k_part))
    return results


def link_codes(side, meta, table):
    core, infos = meta[CORE], chip_infos(table, meta[CHIP])
    own_ids, own_counts = chip_halves(infos[0], core)
    _, far_counts = chip_halves(infos[side], core)
    codes = []
    for half in range(2):
        lane = lax.broadcasted_iota(jnp.int32, (1, ROWS), 1)
        slot = lane + half * ROWS
        live = lane.astype(F32) < own_counts[half]
        far = lane.astype(F32) < far_counts[half]
        if side == 0:
            inside = live & (slot >= meta[B_L]) & (slot < PAIR - meta[A_R])
            code = jnp.where(inside, own_ids[half], -1.0)
        elif side == 1:
            inside = (live & (slot < meta[B_L])) | (far & (slot >= PAIR - meta[A_L]))
            code = jnp.where(inside, 0.0, -1.0)
        else:
            inside = (live & (slot >= PAIR - meta[A_R])) | (far & (slot < meta[B_R]))
            code = jnp.where(inside, 0.0, -1.0)
        codes.append(code.astype(F32))
    return codes


def fill_links(bias, q_live, codes):
    for a in range(2):
        q_live[0:1, a * ROWS : (a + 1) * ROWS] = (codes[a] >= 0.0).astype(F32)
        key_codes = jnp.broadcast_to(codes[a], (ROWS, ROWS)).T
        for b in range(2):
            linked = (key_codes == codes[b]) & (codes[b] >= 0.0)
            bias[a * ROWS : (a + 1) * ROWS, b * ROWS : (b + 1) * ROWS] = jnp.where(
                linked, 0.0, NEG
            ).astype(F32)


def mid_kernel(
    meta,
    q_ref,
    k_ref,
    v_ref,
    d_ref,
    rec_ref,
    table,
    out_ref,
    gg_ref,
    win,
    bias,
    q_live,
):
    per = rec_ref.shape[2] // HD
    core = meta[CORE]

    @pl.when(pl.program_id(0) == 0)
    def _():
        fill_links(bias, q_live, link_codes(0, meta, table))

    fill_windows(win, core, (q_ref, k_ref, v_ref, d_ref), rec_ref)
    heads = [pl.program_id(0) * per + i for i in range(per)]
    gains = [table[head] for head in heads]
    results = solve(
        [
            (*(win[i, t] for t in range(4)), gains[i][0:1], gains[i][1:2], bias[...], q_live[0:1, :])
            for i in range(per)
        ]
    )
    for i, (grads, part_q, part_k) in enumerate(results):
        for t in range(3):
            for half in range(2):
                out_ref[lax.rem(half + core, 2), t, :, i * HD : (i + 1) * HD] = grads[t][
                    half * ROWS : (half + 1) * ROWS
                ]
        gg_ref[heads[i]] = jnp.concatenate([part_q, part_k], axis=0)


def solve_mid(meta, tensors, rec, table, per=4):
    per_head = jax.ShapeDtypeStruct((HEADS, 2, HD), F32)
    return pl.pallas_call(
        mid_kernel,
        out_shape=(jax.ShapeDtypeStruct((2, 3, ROWS, HEADS * HD), BF), per_head),
        grid_spec=pltpu.PrefetchScalarGridSpec(
            num_scalar_prefetch=1,
            grid=(HEADS // per,),
            in_specs=own_specs(per) + [whole(table.shape)],
            out_specs=(half_spec(per), whole(per_head.shape)),
            scratch_shapes=[
                pltpu.VMEM((per, 4, PAIR, HD), BF),
                pltpu.VMEM((PAIR, PAIR), F32),
                pltpu.VMEM((8, PAIR), F32),
            ],
        ),
        compiler_params=params(32),
    )(meta, *tensors, rec, table)


def half_spec(per):
    return pl.BlockSpec((2, 3, ROWS, per * HD), lambda j, m: (0, 0, 0, j))


def row_numbers(rows):
    return lax.broadcasted_iota(jnp.int32, (rows, HD), 0).astype(F32).astype(BF)


def bound(value):
    return jnp.full((1, HD), value, jnp.int32).astype(F32).astype(BF)


def edge_kernel(
    meta,
    q_ref,
    k_ref,
    v_ref,
    d_ref,
    rec_ref,
    table,
    mid_ref,
    gg_mid_ref,
    from_left_first,
    from_left_second,
    from_right_first,
    from_right_second,
    from_turn_first,
    from_turn_rest,
    out_ref,
    gg_ref,
    left_first,
    left_second,
    right_first,
    right_second,
    turn_first,
    turn_rest,
    win,
    bias,
    q_live,
    held,
    back,
    sems,
):
    per = rec_ref.shape[2] // HD
    core = meta[CORE]
    step = pl.program_id(0)

    @pl.when(step == 0)
    def _():
        copies = load_both(
            meta,
            (
                from_left_first,
                from_left_second,
                from_right_first,
                from_right_second,
                from_turn_first,
                from_turn_rest,
            ),
            rows_of(held.at[0], PAIR, CAP),
            rows_of(held.at[1], 0, CAP),
            sems,
        )
        for side in range(2):
            fill_links(
                bias.at[side], q_live.at[side], link_codes(side + 1, meta, table)
            )
        gg_ref[...] = gg_mid_ref[...]
        for copy in copies:
            copy.wait()

    fill_windows(win, core, (q_ref, k_ref, v_ref, d_ref), rec_ref)
    out_ref[...] = mid_ref[...]
    heads = [step * per + i for i in range(per)]
    on_left = [head >= meta[N_L] for head in heads]
    on_right = [head < meta[N_R] for head in heads]
    row = row_numbers(PAIR)

    def solve_side(lefts, rights):
        problems, spots = [], []
        for i, head in enumerate(heads):
            side = jnp.where(lefts[i], 0, 1)
            use = jnp.logical_or(lefts[i], rights[i])
            at = jnp.where(lefts[i], (HEADS - head) * meta[PA_L], head * meta[PB_R])
            span = pl.ds(aligned(jnp.where(use, at, PADDED)), PAIR)
            source = pl.ds(aligned(jnp.where(use, at, 0)), PAIR)
            halo = (row >= bound(jnp.where(lefts[i], PAIR - meta[A_L], 0))) & (
                row < bound(jnp.where(lefts[i], PAIR, jnp.where(use, meta[B_R], 0)))
            )
            local = (row >= bound(jnp.where(lefts[i], 0, PAIR - meta[A_R]))) & (
                row < bound(jnp.where(lefts[i], meta[B_L], jnp.where(use, PAIR, 0)))
            )
            window = [jnp.where(halo, held[side, t, source, :], win[i, t]) for t in range(4)]
            gains = table[head]
            problems.append((*window, gains[0:1], gains[1:2], bias[side], q_live[side, 0:1, :]))
            spots.append((side, span, local, use.astype(F32)))
        for i, (grads, part_q, part_k) in enumerate(solve(problems)):
            side, span, local, counts = spots[i]
            cols = slice(i * HD, (i + 1) * HD)
            for t in range(3):
                back[side, t, span, :] = grads[t]
                for half in range(2):
                    rows = slice(half * ROWS, (half + 1) * ROWS)
                    place = lax.rem(half + core, 2)
                    out_ref[place, t, :, cols] = jnp.where(
                        local[rows], grads[t][rows], out_ref[place, t, :, cols]
                    )
            gg_ref[heads[i]] += jnp.concatenate([part_q, part_k], axis=0) * counts

    def some(flags):
        return functools.reduce(jnp.logical_or, flags)

    @pl.when(some(on_left + on_right))
    def _():
        solve_side(on_left, on_right)

    both = [jnp.logical_and(*pair) for pair in zip(on_left, on_right, strict=True)]

    @pl.when(some(both))
    def _():
        solve_side([jnp.logical_and(flag, jnp.logical_not(flag)) for flag in both], both)

    @pl.when(step == pl.num_programs(0) - 1)
    def _():
        send_pieces(
            meta,
            rows_of(back.at[0], PAIR, CAP),
            rows_of(back.at[1], 0, CAP),
            (left_first, left_second, right_first, right_second, turn_first, turn_rest),
            sems,
        )


def solve_edges(meta, tensors, rec, table, mid, gg_mid, halos, per=4):
    return pl.pallas_call(
        edge_kernel,
        out_shape=(
            jax.ShapeDtypeStruct(mid.shape, BF),
            jax.ShapeDtypeStruct(gg_mid.shape, F32),
            *pieces_shape(3),
        ),
        grid_spec=pltpu.PrefetchScalarGridSpec(
            num_scalar_prefetch=1,
            grid=(HEADS // per,),
            in_specs=own_specs(per)
            + [whole(table.shape), half_spec(per), whole(gg_mid.shape)]
            + [ANYWHERE] * 6,
            out_specs=(half_spec(per), whole(gg_mid.shape), *([ANYWHERE] * 6)),
            scratch_shapes=[
                pltpu.VMEM((per, 4, PAIR, HD), BF),
                pltpu.VMEM((2, PAIR, PAIR), F32),
                pltpu.VMEM((2, 8, PAIR), F32),
                pltpu.VMEM((2, 4, PADDED, HD), BF),
                pltpu.VMEM((2, 3, PADDED + PAIR, HD), BF),
                pltpu.SemaphoreType.DMA((6,)),
            ],
        ),
        compiler_params=params(40),
    )(meta, *tensors, rec, table, mid, gg_mid, *halos)


def load_returned(meta, pieces, held_left, held_right, sems):
    for copy in load_both(
        meta, pieces, rows_of(held_left, 0, CAP), rows_of(held_right, PAIR, CAP), sems
    ):
        copy.wait()


def merged(meta, head, half, rows, held_left, held_right):
    use_left = head < meta[N_L]
    use_right = head >= meta[N_R]
    base = half * ROWS
    left_at = jnp.where(use_left, head * meta[PB_L], 0) + base
    right_at = jnp.where(use_right, (HEADS - head) * meta[PA_R], 0) + base
    row = row_numbers(ROWS)
    at_head = row < bound(jnp.where(use_left, meta[B_L], 0) - base)
    at_tail = row >= bound(jnp.where(use_right, PAIR - meta[A_R], PAIR) - base)
    done = []
    for t, part in enumerate(rows):
        part = jnp.where(at_head, held_left[t, pl.ds(aligned(left_at), ROWS), :], part)
        part = jnp.where(at_tail, held_right[t, pl.ds(aligned(right_at), ROWS), :], part)
        done.append(part)
    return done


def merge_kernel(meta, in_ref, *refs):
    pieces, (_, send_ref, held_left, held_right, sems) = refs[:6], refs[6:]
    per = in_ref.shape[3] // HD
    step = pl.program_id(0)

    @pl.when(step == 0)
    def _():
        load_returned(meta, pieces, held_left, held_right, sems)

    for i in range(per):
        cols = slice(i * HD, (i + 1) * HD)
        rows = [in_ref[0, t, :, cols] for t in range(3)]
        rows = merged(meta, step * per + i, 1 - meta[CORE], rows, held_left, held_right)
        for t in range(3):
            send_ref[t, :, cols] = rows[t]


def held_scratch():
    return [
        pltpu.VMEM((3, PADDED, HD), BF),
        pltpu.VMEM((3, PADDED, HD), BF),
        pltpu.SemaphoreType.DMA((6,)),
    ]


def merge_other(meta, own, returned, after, per=4):
    return pl.pallas_call(
        merge_kernel,
        out_shape=jax.ShapeDtypeStruct((3, ROWS, HEADS * HD), BF),
        grid_spec=pltpu.PrefetchScalarGridSpec(
            num_scalar_prefetch=1,
            grid=(HEADS // per,),
            in_specs=[pl.BlockSpec((1, 3, ROWS, per * HD), lambda j, m: (1, 0, 0, j))]
            + [ANYWHERE] * 7,
            out_specs=pl.BlockSpec((3, ROWS, per * HD), lambda j, m: (0, 0, j)),
            scratch_shapes=held_scratch(),
        ),
        compiler_params=params(16),
    )(meta, own, *returned, after)


def weave_kernel(meta, in_ref, rec_ref, *refs):
    pieces, (gg_parts, *outs, gg_q, gg_k, held_left, held_right, sems) = refs[:6], refs[6:]
    per = in_ref.shape[3] // HD
    core = meta[CORE]
    step = pl.program_id(0)

    @pl.when(step == 0)
    def _():
        load_returned(meta, pieces, held_left, held_right, sems)
        total = jnp.sum(gg_parts[...], axis=0)
        gg_q[...] = total[0:1]
        gg_k[...] = total[1:2]

    for i in range(per):
        cols = slice(i * HD, (i + 1) * HD)
        rows = [in_ref[0, t, :, cols] for t in range(3)]
        rows = merged(meta, step * per + i, core, rows, held_left, held_right)
        for t in range(3):
            outs[t][:, lanes(2 * i + core)] = rows[t]
            outs[t][:, lanes(2 * i + 1 - core)] = rec_ref[t, :, cols]


def weave(meta, own, rec, returned, gg_parts, per=4):
    return pl.pallas_call(
        weave_kernel,
        out_shape=(jax.ShapeDtypeStruct((ROWS, 2 * HEADS * HD), BF),) * 3
        + (jax.ShapeDtypeStruct((1, HD), F32),) * 2,
        grid_spec=pltpu.PrefetchScalarGridSpec(
            num_scalar_prefetch=1,
            grid=(HEADS // per,),
            in_specs=[
                pl.BlockSpec((1, 3, ROWS, per * HD), lambda j, m: (0, 0, 0, j)),
                pl.BlockSpec((3, ROWS, per * HD), lambda j, m: (0, 0, j)),
            ]
            + [ANYWHERE] * 6
            + [whole(gg_parts.shape)],
            out_specs=(pl.BlockSpec((ROWS, 2 * per * HD), lambda j, m: (0, j)),) * 3
            + (whole((1, HD)),) * 2,
            scratch_shapes=held_scratch(),
        ),
        compiler_params=params(16),
    )(meta, own, rec, *returned, gg_parts)


def exchange(pieces, size):
    lefts, rights, (turn_first, turn_rest) = pieces[0:2], pieces[2:4], pieces[4:6]
    line = 2 * LINE
    wrap = line - 2
    turns = [(i, i + 2) for i in range(size - 2) if i % line >= wrap]
    straight = [(i, i + 2) for i in range(size - 2) if i % line < wrap]

    def back(pairs):
        return [(j, i) for i, j in pairs]

    def move(array, pairs):
        return lax.ppermute(array, "seq", pairs)

    hop = move(turn_rest, [(i, i - wrap) for i, _ in turns] + [(j, j + wrap) for _, j in turns])
    from_left = [move(piece, straight) for piece in rights]
    from_right = [move(piece, back(straight)) for piece in lefts]
    from_turn = move(turn_first, turns + back(turns))
    from_hop = move(hop, [(i - wrap, j) for i, j in turns] + [(j + wrap, i) for i, j in turns])
    return (*from_left, *from_right, from_turn, from_hop)


def shards(queries, keys, values, out_grad, gain_q, gain_k, clip_ids, counts):
    size = lax.axis_size("seq")
    groups = lax.axis_size("dp")
    chips = size // 2
    seq = lax.axis_index("seq")
    swap = [(i, i ^ 1) for i in range(size)]
    place = jnp.stack([seq % 2, seq // 2]).astype(jnp.int32)
    tensors = tuple(
        pltpu.with_memory_space_constraint(t, pltpu.HBM)
        for t in (queries, keys, values, out_grad)
    )

    same_core = [list(range(core, size, 2)) for core in range(2)]
    same_cores = [
        [d * size + at for d in range(groups) for at in one_core] for one_core in same_core
    ]

    def all_to_all(array, axis, among=None):
        return lax.all_to_all(array, axis, 0, 0, axis_index_groups=among, tiled=True)

    info = jnp.concatenate([clip_ids, jnp.broadcast_to(counts, (1, ROWS))], axis=0).astype(F32)
    info_other = lax.ppermute(info, "seq", swap)
    gain_own = jnp.concatenate([gain_q, gain_k], axis=0)
    gain_cols = all_to_all(jnp.broadcast_to(gain_own[None], (groups,) + gain_own.shape), "dp")
    picked, known = pick_other(place, tensors, gain_cols, info, info_other)
    rec = lax.ppermute(picked, "seq", swap)
    table = all_to_all(known, "seq", same_core)

    meta, *pieces = pack_halos(place, tensors, rec, table)
    halos = exchange(pieces, size)
    mid, gg_mid = solve_mid(meta, tensors, rec, table)
    own, gg, *pieces = solve_edges(meta, tensors, rec, table, mid, gg_mid, halos)
    returned = exchange(pieces, size)
    gg_parts = all_to_all(
        jnp.broadcast_to(gg[None], (groups,) + gg.shape).reshape(groups * chips, 2, HD),
        ("dp", "seq"),
        same_cores,
    )
    send = merge_other(meta, own, returned, gg_parts)
    other = lax.ppermute(send, "seq", swap)
    return tuple(weave(meta, own, other, returned, gg_parts))


def solution(mesh):
    rows = P(("dp", "seq"), None)
    cells = P("seq", "dp")
    slots = P("dp", "seq")
    return jax.shard_map(
        shards,
        mesh=mesh,
        in_specs=(rows, rows, rows, rows, cells, cells, slots, slots),
        out_specs=(rows, rows, rows, P("seq", None), P("seq", None)),
        check_vma=False,
    )
```

```python
import functools

import jax
import jax.numpy as jnp
from jax import lax
from jax.experimental import pallas as pl
from jax.experimental.pallas import tpu as pltpu
from jax.sharding import PartitionSpec as P

EPS = 1e-06
NEG = -1e30
HD = 128
ROWS = 128
PAIR = 256
HEADS = 16
ALIGN = 16
LINE = 4
CAP = 1152
PARTS = (CAP // 2,) * 2
FIRST = 768
REST = CAP - FIRST
SENT = len(PARTS) + 2
PADDED = CAP + PAIR
SCALE = HD**-0.5
LOG2E = 1.4426950408889634
BF = jnp.bfloat16
F32 = jnp.float32
CORE, CHIP, A_L, B_L, A_R, B_R, N_L, N_R, PA_L, PB_L, PA_R, PB_R = range(12)
KNOWN = 5
ANYWHERE = pl.BlockSpec(memory_space=pl.ANY)
IN_VMEM = pl.BlockSpec(memory_space=pltpu.VMEM)
IN_SMEM = pl.BlockSpec(memory_space=pltpu.SMEM)


def aligned(index):
    return pl.multiple_of(index, ALIGN)


def lanes(position):
    return pl.ds(pl.multiple_of(position * HD, HD), HD)


def params(mib):
    return pltpu.CompilerParams(vmem_limit_bytes=mib * 1024 * 1024)


def whole(shape):
    return pl.BlockSpec(shape, lambda j, m: (0,) * len(shape))


def run_copies(copies):
    for copy in copies:
        copy.start()
    for copy in copies:
        copy.wait()


def rows_of(held, start, length):
    return held.at[:, pl.ds(start, length), :]


def pick_kernel(
    place, q_ref, k_ref, v_ref, d_ref, gain_cols, info, info_other, out_ref, known_ref, row
):
    other = 1 - place[CORE]

    @pl.when(pl.program_id(0) == 0)
    def _():
        width = gain_cols.shape[2]
        row[...] = jnp.zeros_like(row)
        for n in range(gain_cols.shape[0]):
            row[0:2, n * width : (n + 1) * width] = gain_cols[n]
        row[2:3, :] = info[0:1, :]
        row[3:4, :] = info_other[0:1, :]
        row[4:5, 0:1] = info[1:2, 0:1]
        row[4:5, 1:2] = info_other[1:2, 0:1]
        known_ref[...] = jnp.broadcast_to(row[0:KNOWN, :][None], known_ref.shape)

    for t, ref in enumerate((q_ref, k_ref, v_ref, d_ref)):
        for i in range(out_ref.shape[2] // HD):
            out_ref[t, :, i * HD : (i + 1) * HD] = ref[:, lanes(2 * i + other)]


def pick_other(place, tensors, gain_cols, info, info_other, per=4):
    known = jax.ShapeDtypeStruct((HEADS, KNOWN, HD), F32)
    small = (gain_cols, info, info_other)
    return pl.pallas_call(
        pick_kernel,
        out_shape=(jax.ShapeDtypeStruct((4, ROWS, HEADS * HD), BF), known),
        grid_spec=pltpu.PrefetchScalarGridSpec(
            num_scalar_prefetch=1,
            grid=(HEADS // per,),
            in_specs=own_specs(per)[:4] + [whole(array.shape) for array in small],
            out_specs=(own_specs(per)[4], whole(known.shape)),
            scratch_shapes=[pltpu.VMEM((8, HD), F32)],
        ),
        compiler_params=params(12),
    )(place, *tensors, *small)


def chip_halves(info, core):
    ids, counts = (info[0:1], info[1:2]), (info[2:3, 0:1], info[2:3, 1:2])

    def ordered(mine, other):
        return jnp.where(core == 0, mine, other), jnp.where(core == 0, other, mine)

    return ordered(*ids), ordered(*counts)


def count_equal(halves, wanted):
    hits = [jnp.where(half == wanted, 1.0, 0.0).astype(F32) for half in halves]
    return jnp.sum(hits[0] + hits[1]).astype(jnp.int32)


def edge_split(long_a, long_b):
    blocks_a = lax.div(long_a + ALIGN - 1, ALIGN)
    blocks_b = lax.div(long_b + ALIGN - 1, ALIGN)
    least = HEADS - lax.div(CAP // ALIGN, jnp.maximum(blocks_a, 1))
    most = lax.div(CAP // ALIGN, jnp.maximum(blocks_b, 1))
    to_left = jnp.minimum(jnp.maximum(HEADS // 2, least), most)
    return blocks_a * ALIGN, blocks_b * ALIGN, to_left


def chip_infos(table, chip):
    spots = (chip, jnp.maximum(chip - 1, 0), jnp.minimum(chip + 1, HEADS - 1))
    return [table[spot][2:KNOWN] for spot in spots]


def write_plan(place, table, meta):
    core, chip = place[CORE], place[CHIP]
    infos = chip_infos(table, chip)
    own, _ = chip_halves(infos[0], core)
    left, _ = chip_halves(infos[1], core)
    right, _ = chip_halves(infos[2], core)
    left_last, own_first = jnp.max(left[1]), jnp.min(own[0])
    own_last, right_first = jnp.max(own[1]), jnp.min(right[0])
    cross_l = (chip > 0) & (left_last == own_first)
    cross_r = (chip < HEADS - 1) & (right_first == own_last)
    a_l = jnp.where(cross_l, count_equal(left, left_last), 0)
    b_l = jnp.where(cross_l, count_equal(own, own_first), 0)
    a_r = jnp.where(cross_r, count_equal(own, own_last), 0)
    b_r = jnp.where(cross_r, count_equal(right, right_first), 0)
    pa_l, pb_l, n_l = edge_split(a_l, b_l)
    pa_r, pb_r, n_r = edge_split(a_r, b_r)
    n_l = jnp.where(cross_l, n_l, HEADS)
    n_r = jnp.where(cross_r, n_r, 0)
    values = [core, chip, a_l, b_l, a_r, b_r, n_l, n_r, pa_l, pb_l, pa_r, pb_r]
    for n, value in enumerate(values):
        meta[n] = value


def even(meta):
    return lax.rem(meta[CHIP], 2) == 0


def at_corner(meta):
    place = lax.rem(meta[CHIP], LINE)
    return (place == 0) | (place == LINE - 1)


def cut(table, *lengths):
    starts = [sum(lengths[:n]) for n in range(len(lengths))]
    return [table.at[:, pl.ds(a, n), :] for a, n in zip(starts, lengths, strict=True)]


def copies_of(sources, targets, sems):
    return [
        pltpu.make_async_copy(a, b, sems.at[n])
        for n, (a, b) in enumerate(zip(sources, targets, strict=True))
    ]


def start_one(cases):
    for wanted, copies in cases:

        @pl.when(wanted)
        def _():
            for copy in copies:
                copy.start()

    return cases[0][1]


def wait_all(copies):
    for copy in copies:
        copy.wait()


def send_pieces(meta, left, right, pieces, sems):
    def pieces_of(a, b):
        return copies_of(cut(a, *PARTS) + cut(b, FIRST, REST), pieces, sems)

    is_even = even(meta)
    wait_all(
        start_one(
            [
                (is_even, pieces_of(right, left)),
                (jnp.logical_not(is_even), pieces_of(left, right)),
            ]
        )
    )


def load_both(meta, pieces, held_left, held_right, sems):
    *direct, rest, relayed = pieces

    def pieces_of(a, b, last):
        return copies_of([*direct, last], cut(a, *PARTS) + cut(b, FIRST, REST), sems)

    is_even, corner = even(meta), at_corner(meta)
    is_odd, inner = jnp.logical_not(is_even), jnp.logical_not(corner)
    return start_one(
        [
            (is_even & corner, pieces_of(held_right, held_left, relayed)),
            (is_even & inner, pieces_of(held_right, held_left, rest)),
            (is_odd & corner, pieces_of(held_left, held_right, relayed)),
            (is_odd & inner, pieces_of(held_left, held_right, rest)),
        ]
    )


def half_rows(half):
    return pl.ds(pl.multiple_of(half * ROWS, ROWS), ROWS)


def fill_windows(win, core, own_refs, rec_ref):
    for i in range(win.shape[0]):
        for t, ref in enumerate(own_refs):
            win[i, t, half_rows(core), :] = ref[:, lanes(2 * i + core)]
            win[i, t, half_rows(1 - core), :] = rec_ref[t, :, i * HD : (i + 1) * HD]


def pack_kernel(place, q_ref, k_ref, v_ref, d_ref, rec_ref, table, meta, *refs):
    *pieces, win, left_ref, right_ref, sems = refs
    per = rec_ref.shape[2] // HD
    core = place[CORE]
    step = pl.program_id(0)

    @pl.when(step == 0)
    def _():
        write_plan(place, table, meta)

    fill_windows(win, core, (q_ref, k_ref, v_ref, d_ref), rec_ref)
    for i in range(per):
        head = step * per + i

        @pl.when(head < meta[N_L])
        def _():
            for t in range(4):
                left_ref[t, pl.ds(aligned(head * meta[PB_L]), PAIR), :] = win[i, t]

        @pl.when(head >= meta[N_R])
        def _():
            for t in range(4):
                right_ref[t, pl.ds(aligned((HEADS - head) * meta[PA_R]), PAIR), :] = win[i, t]

    @pl.when(step == pl.num_programs(0) - 1)
    def _():
        send_pieces(
            meta,
            rows_of(left_ref, 0, CAP),
            rows_of(right_ref, PAIR, CAP),
            pieces,
            sems,
        )


def own_specs(per):
    return [pl.BlockSpec((ROWS, 2 * per * HD), lambda j, m: (0, j))] * 4 + [
        pl.BlockSpec((4, ROWS, per * HD), lambda j, m: (0, 0, j))
    ]


def pieces_shape(tensors):
    return [jax.ShapeDtypeStruct((tensors, n, HD), BF) for n in (*PARTS, FIRST, REST)]


def pack_halos(place, tensors, rec, table, per=4):
    return pl.pallas_call(
        pack_kernel,
        out_shape=(
            jax.ShapeDtypeStruct((16,), jnp.int32),
            *pieces_shape(4),
        ),
        grid_spec=pltpu.PrefetchScalarGridSpec(
            num_scalar_prefetch=1,
            grid=(HEADS // per,),
            in_specs=own_specs(per) + [whole(table.shape)],
            out_specs=(IN_SMEM, *([ANYWHERE] * SENT)),
            scratch_shapes=[
                pltpu.VMEM((per, 4, PAIR, HD), BF),
                pltpu.VMEM((4, PADDED, HD), BF),
                pltpu.VMEM((4, PADDED, HD), BF),
                pltpu.SemaphoreType.DMA((SENT,)),
            ],
        ),
        compiler_params=params(16),
    )(place, *tensors, rec, table)


def matmul(a, b, contract_a, contract_b):
    return lax.dot_general(
        a, b, (((contract_a,), (contract_b,)), ((), ())), preferred_element_type=F32
    )


def norm_parts(rows, gain):
    widened = rows.astype(F32)
    scaled = lax.rsqrt(jnp.mean(widened * widened, axis=-1, keepdims=True) + EPS)
    unit_rows = widened * scaled
    return scaled, unit_rows, (unit_rows * gain).astype(BF)


def norm_back(scaled, unit_rows, gain, upper):
    terms = upper * unit_rows
    gain = gain * SCALE
    mean = jnp.mean(terms * gain, axis=-1, keepdims=True)
    grad = scaled * (gain * upper - unit_rows * mean)
    return grad.astype(BF), jnp.sum(terms, axis=0, keepdims=True) * SCALE


def solve(problems):
    each = range(len(problems))
    q_rows, k_rows, v_rows, d_rows, gain_q, gain_k, bias, q_live = zip(*problems, strict=True)
    q_parts = [norm_parts(q_rows[n], gain_q[n]) for n in each]
    k_parts = [norm_parts(k_rows[n], gain_k[n]) for n in each]
    raw = [matmul(k_parts[n][2], q_parts[n][2], 1, 1) for n in each]
    d_weights = [matmul(v_rows[n], d_rows[n], 1, 1) for n in each]
    weights = []
    for n in each:
        scores = raw[n] * (SCALE * LOG2E) + bias[n]
        exponent = jnp.exp2(scores - jnp.max(scores, axis=0, keepdims=True))
        total = jnp.sum(exponent, axis=0, keepdims=True)
        weights.append((exponent * (q_live[n] / total)).astype(BF))
    dv_rows = [matmul(weights[n], d_rows[n], 1, 0) for n in each]
    d_scores = []
    for n in each:
        wide = weights[n].astype(F32)
        row_delta = jnp.sum(wide * d_weights[n], axis=0, keepdims=True)
        d_scores.append((wide * (d_weights[n] - row_delta)).astype(BF))
    dk = [matmul(d_scores[n], q_parts[n][2], 1, 0) for n in each]
    dq = [matmul(d_scores[n], k_parts[n][2], 0, 0) for n in each]
    results = []
    for n in each:
        grad_k, gain_k_part = norm_back(k_parts[n][0], k_parts[n][1], gain_k[n], dk[n])
        grad_q, gain_q_part = norm_back(q_parts[n][0], q_parts[n][1], gain_q[n], dq[n])
        grads = (grad_q, grad_k, dv_rows[n].astype(BF))
        results.append((grads, gain_q_part, gain_k_part))
    return results


def link_codes(side, meta, table):
    core, infos = meta[CORE], chip_infos(table, meta[CHIP])
    own_ids, own_counts = chip_halves(infos[0], core)
    _, far_counts = chip_halves(infos[side], core)
    codes = []
    for half in range(2):
        lane = lax.broadcasted_iota(jnp.int32, (1, ROWS), 1)
        slot = lane + half * ROWS
        live = lane.astype(F32) < own_counts[half]
        far = lane.astype(F32) < far_counts[half]
        if side == 0:
            inside = live & (slot >= meta[B_L]) & (slot < PAIR - meta[A_R])
            code = jnp.where(inside, own_ids[half], -1.0)
        elif side == 1:
            inside = (live & (slot < meta[B_L])) | (far & (slot >= PAIR - meta[A_L]))
            code = jnp.where(inside, 0.0, -1.0)
        else:
            inside = (live & (slot >= PAIR - meta[A_R])) | (far & (slot < meta[B_R]))
            code = jnp.where(inside, 0.0, -1.0)
        codes.append(code.astype(F32))
    return codes


def fill_links(bias, q_live, codes):
    for a in range(2):
        q_live[0:1, a * ROWS : (a + 1) * ROWS] = (codes[a] >= 0.0).astype(F32)
        key_codes = jnp.broadcast_to(codes[a], (ROWS, ROWS)).T
        for b in range(2):
            linked = (key_codes == codes[b]) & (codes[b] >= 0.0)
            bias[a * ROWS : (a + 1) * ROWS, b * ROWS : (b + 1) * ROWS] = jnp.where(
                linked, 0.0, NEG
            ).astype(F32)


def mid_kernel(
    meta,
    q_ref,
    k_ref,
    v_ref,
    d_ref,
    rec_ref,
    table,
    out_ref,
    gg_ref,
    win,
    bias,
    q_live,
):
    per = rec_ref.shape[2] // HD
    core = meta[CORE]

    @pl.when(pl.program_id(0) == 0)
    def _():
        fill_links(bias, q_live, link_codes(0, meta, table))

    fill_windows(win, core, (q_ref, k_ref, v_ref, d_ref), rec_ref)
    heads = [pl.program_id(0) * per + i for i in range(per)]
    gains = [table[head] for head in heads]
    results = solve(
        [
            (*(win[i, t] for t in range(4)), gains[i][0:1], gains[i][1:2], bias[...], q_live[0:1, :])
            for i in range(per)
        ]
    )
    for i, (grads, part_q, part_k) in enumerate(results):
        for t in range(3):
            for half in range(2):
                out_ref[lax.rem(half + core, 2), t, :, i * HD : (i + 1) * HD] = grads[t][
                    half * ROWS : (half + 1) * ROWS
                ]
        gg_ref[heads[i]] = jnp.concatenate([part_q, part_k], axis=0)


def solve_mid(meta, tensors, rec, table, per=4):
    per_head = jax.ShapeDtypeStruct((HEADS, 2, HD), F32)
    return pl.pallas_call(
        mid_kernel,
        out_shape=(jax.ShapeDtypeStruct((2, 3, ROWS, HEADS * HD), BF), per_head),
        grid_spec=pltpu.PrefetchScalarGridSpec(
            num_scalar_prefetch=1,
            grid=(HEADS // per,),
            in_specs=own_specs(per) + [whole(table.shape)],
            out_specs=(half_spec(per), whole(per_head.shape)),
            scratch_shapes=[
                pltpu.VMEM((per, 4, PAIR, HD), BF),
                pltpu.VMEM((PAIR, PAIR), F32),
                pltpu.VMEM((8, PAIR), F32),
            ],
        ),
        compiler_params=params(32),
    )(meta, *tensors, rec, table)


def half_spec(per):
    return pl.BlockSpec((2, 3, ROWS, per * HD), lambda j, m: (0, 0, 0, j))


def row_numbers(rows):
    return lax.broadcasted_iota(jnp.int32, (rows, HD), 0).astype(F32).astype(BF)


def bound(value):
    return jnp.full((1, HD), value, jnp.int32).astype(F32).astype(BF)


def edge_kernel(
    meta, q_ref, k_ref, v_ref, d_ref, rec_ref, table, mid_ref, gg_mid_ref, *refs
):
    halos, (out_ref, gg_ref, *pieces) = refs[: SENT + 1], refs[SENT + 1 : -6]
    win, bias, q_live, held, back, sems = refs[-6:]
    per = rec_ref.shape[2] // HD
    core = meta[CORE]
    step = pl.program_id(0)

    @pl.when(step == 0)
    def _():
        copies = load_both(
            meta,
            halos,
            rows_of(held.at[0], PAIR, CAP),
            rows_of(held.at[1], 0, CAP),
            sems,
        )
        for side in range(2):
            fill_links(
                bias.at[side], q_live.at[side], link_codes(side + 1, meta, table)
            )
        gg_ref[...] = gg_mid_ref[...]
        for copy in copies:
            copy.wait()

    fill_windows(win, core, (q_ref, k_ref, v_ref, d_ref), rec_ref)
    out_ref[...] = mid_ref[...]
    heads = [step * per + i for i in range(per)]
    on_left = [head >= meta[N_L] for head in heads]
    on_right = [head < meta[N_R] for head in heads]
    row = row_numbers(PAIR)

    def solve_side(lefts, rights):
        problems, spots = [], []
        for i, head in enumerate(heads):
            side = jnp.where(lefts[i], 0, 1)
            use = jnp.logical_or(lefts[i], rights[i])
            at = jnp.where(lefts[i], (HEADS - head) * meta[PA_L], head * meta[PB_R])
            span = pl.ds(aligned(jnp.where(use, at, PADDED)), PAIR)
            source = pl.ds(aligned(jnp.where(use, at, 0)), PAIR)
            halo = (row >= bound(jnp.where(lefts[i], PAIR - meta[A_L], 0))) & (
                row < bound(jnp.where(lefts[i], PAIR, jnp.where(use, meta[B_R], 0)))
            )
            local = (row >= bound(jnp.where(lefts[i], 0, PAIR - meta[A_R]))) & (
                row < bound(jnp.where(lefts[i], meta[B_L], jnp.where(use, PAIR, 0)))
            )
            window = [jnp.where(halo, held[side, t, source, :], win[i, t]) for t in range(4)]
            gains = table[head]
            problems.append((*window, gains[0:1], gains[1:2], bias[side], q_live[side, 0:1, :]))
            spots.append((side, span, local, use.astype(F32)))
        for i, (grads, part_q, part_k) in enumerate(solve(problems)):
            side, span, local, counts = spots[i]
            cols = slice(i * HD, (i + 1) * HD)
            for t in range(3):
                back[side, t, span, :] = grads[t]
                for half in range(2):
                    rows = slice(half * ROWS, (half + 1) * ROWS)
                    place = lax.rem(half + core, 2)
                    out_ref[place, t, :, cols] = jnp.where(
                        local[rows], grads[t][rows], out_ref[place, t, :, cols]
                    )
            gg_ref[heads[i]] += jnp.concatenate([part_q, part_k], axis=0) * counts

    def some(flags):
        return functools.reduce(jnp.logical_or, flags)

    @pl.when(some(on_left + on_right))
    def _():
        solve_side(on_left, on_right)

    both = [jnp.logical_and(*pair) for pair in zip(on_left, on_right, strict=True)]

    @pl.when(some(both))
    def _():
        solve_side([jnp.logical_and(flag, jnp.logical_not(flag)) for flag in both], both)

    @pl.when(step == pl.num_programs(0) - 1)
    def _():
        send_pieces(
            meta,
            rows_of(back.at[0], PAIR, CAP),
            rows_of(back.at[1], 0, CAP),
            pieces,
            sems,
        )


def solve_edges(meta, tensors, rec, table, mid, gg_mid, halos, per=4):
    return pl.pallas_call(
        edge_kernel,
        out_shape=(
            jax.ShapeDtypeStruct(mid.shape, BF),
            jax.ShapeDtypeStruct(gg_mid.shape, F32),
            *pieces_shape(3),
        ),
        grid_spec=pltpu.PrefetchScalarGridSpec(
            num_scalar_prefetch=1,
            grid=(HEADS // per,),
            in_specs=own_specs(per)
            + [whole(table.shape), half_spec(per), whole(gg_mid.shape)]
            + [ANYWHERE] * (SENT + 1),
            out_specs=(half_spec(per), whole(gg_mid.shape), *([ANYWHERE] * SENT)),
            scratch_shapes=[
                pltpu.VMEM((per, 4, PAIR, HD), BF),
                pltpu.VMEM((2, PAIR, PAIR), F32),
                pltpu.VMEM((2, 8, PAIR), F32),
                pltpu.VMEM((2, 4, PADDED, HD), BF),
                pltpu.VMEM((2, 3, PADDED + PAIR, HD), BF),
                pltpu.SemaphoreType.DMA((SENT,)),
            ],
        ),
        compiler_params=params(40),
    )(meta, *tensors, rec, table, mid, gg_mid, *halos)


def load_returned(meta, pieces, held_left, held_right, sems):
    for copy in load_both(
        meta, pieces, rows_of(held_left, 0, CAP), rows_of(held_right, PAIR, CAP), sems
    ):
        copy.wait()


def merged(meta, head, half, rows, held_left, held_right):
    use_left = head < meta[N_L]
    use_right = head >= meta[N_R]
    base = half * ROWS
    left_at = jnp.where(use_left, head * meta[PB_L], 0) + base
    right_at = jnp.where(use_right, (HEADS - head) * meta[PA_R], 0) + base
    row = row_numbers(ROWS)
    at_head = row < bound(jnp.where(use_left, meta[B_L], 0) - base)
    at_tail = row >= bound(jnp.where(use_right, PAIR - meta[A_R], PAIR) - base)
    done = []
    for t, part in enumerate(rows):
        part = jnp.where(at_head, held_left[t, pl.ds(aligned(left_at), ROWS), :], part)
        part = jnp.where(at_tail, held_right[t, pl.ds(aligned(right_at), ROWS), :], part)
        done.append(part)
    return done


def merge_kernel(meta, in_ref, *refs):
    pieces, (_, send_ref, held_left, held_right, sems) = refs[: SENT + 1], refs[SENT + 1 :]
    per = in_ref.shape[3] // HD
    step = pl.program_id(0)

    @pl.when(step == 0)
    def _():
        load_returned(meta, pieces, held_left, held_right, sems)

    for i in range(per):
        cols = slice(i * HD, (i + 1) * HD)
        rows = [in_ref[0, t, :, cols] for t in range(3)]
        rows = merged(meta, step * per + i, 1 - meta[CORE], rows, held_left, held_right)
        for t in range(3):
            send_ref[t, :, cols] = rows[t]


def held_scratch():
    return [
        pltpu.VMEM((3, PADDED, HD), BF),
        pltpu.VMEM((3, PADDED, HD), BF),
        pltpu.SemaphoreType.DMA((SENT,)),
    ]


def merge_other(meta, own, returned, after, per=4):
    return pl.pallas_call(
        merge_kernel,
        out_shape=jax.ShapeDtypeStruct((3, ROWS, HEADS * HD), BF),
        grid_spec=pltpu.PrefetchScalarGridSpec(
            num_scalar_prefetch=1,
            grid=(HEADS // per,),
            in_specs=[pl.BlockSpec((1, 3, ROWS, per * HD), lambda j, m: (1, 0, 0, j))]
            + [ANYWHERE] * (SENT + 2),
            out_specs=pl.BlockSpec((3, ROWS, per * HD), lambda j, m: (0, 0, j)),
            scratch_shapes=held_scratch(),
        ),
        compiler_params=params(16),
    )(meta, own, *returned, after)


def weave_kernel(meta, in_ref, rec_ref, *refs):
    pieces, (gg_parts, *outs, gg_q, gg_k, held_left, held_right, sems) = refs[: SENT + 1], refs[SENT + 1 :]
    per = in_ref.shape[3] // HD
    core = meta[CORE]
    step = pl.program_id(0)

    @pl.when(step == 0)
    def _():
        load_returned(meta, pieces, held_left, held_right, sems)
        total = jnp.sum(gg_parts[...], axis=0)
        gg_q[...] = total[0:1]
        gg_k[...] = total[1:2]

    for i in range(per):
        cols = slice(i * HD, (i + 1) * HD)
        rows = [in_ref[0, t, :, cols] for t in range(3)]
        rows = merged(meta, step * per + i, core, rows, held_left, held_right)
        for t in range(3):
            outs[t][:, lanes(2 * i + core)] = rows[t]
            outs[t][:, lanes(2 * i + 1 - core)] = rec_ref[t, :, cols]


def weave(meta, own, rec, returned, gg_parts, per=4):
    return pl.pallas_call(
        weave_kernel,
        out_shape=(jax.ShapeDtypeStruct((ROWS, 2 * HEADS * HD), BF),) * 3
        + (jax.ShapeDtypeStruct((1, HD), F32),) * 2,
        grid_spec=pltpu.PrefetchScalarGridSpec(
            num_scalar_prefetch=1,
            grid=(HEADS // per,),
            in_specs=[
                pl.BlockSpec((1, 3, ROWS, per * HD), lambda j, m: (0, 0, 0, j)),
                pl.BlockSpec((3, ROWS, per * HD), lambda j, m: (0, 0, j)),
            ]
            + [ANYWHERE] * (SENT + 1)
            + [whole(gg_parts.shape)],
            out_specs=(pl.BlockSpec((ROWS, 2 * per * HD), lambda j, m: (0, j)),) * 3
            + (whole((1, HD)),) * 2,
            scratch_shapes=held_scratch(),
        ),
        compiler_params=params(16),
    )(meta, own, rec, *returned, gg_parts)


def exchange(pieces, size):
    *straight, first, rest = pieces
    line = 2 * LINE
    wrap = line - 2
    steps = [(i, i + 2) for i in range(size - 2)]
    evens = [pair for pair in steps if pair[0] // 2 % 2 == 0]
    odds = [pair for pair in steps if pair[0] // 2 % 2 == 1]
    turns = [pair for pair in odds if pair[0] % line >= wrap]
    inner = [pair for pair in odds if pair[0] % line < wrap]

    def both(pairs):
        return pairs + [(j, i) for i, j in pairs]

    def move(array, pairs):
        return lax.ppermute(array, "seq", pairs)

    along_x = [(i, i - wrap) for i, _ in turns] + [(j, j + wrap) for _, j in turns]
    along_z = [(i - wrap, j) for i, j in turns] + [(j + wrap, i) for i, j in turns]
    hop = move(rest, both(inner) + along_x)
    from_first = move(first, both(odds))
    from_even = [move(piece, both(evens)) for piece in straight]
    return (*from_even, from_first, hop, move(hop, along_z))


def shards(queries, keys, values, out_grad, gain_q, gain_k, clip_ids, counts):
    size = lax.axis_size("seq")
    groups = lax.axis_size("dp")
    chips = size // 2
    seq = lax.axis_index("seq")
    swap = [(i, i ^ 1) for i in range(size)]
    place = jnp.stack([seq % 2, seq // 2]).astype(jnp.int32)
    tensors = tuple(
        pltpu.with_memory_space_constraint(t, pltpu.HBM)
        for t in (queries, keys, values, out_grad)
    )

    same_core = [list(range(core, size, 2)) for core in range(2)]
    same_cores = [
        [d * size + at for d in range(groups) for at in one_core] for one_core in same_core
    ]

    def all_to_all(array, axis, among=None):
        return lax.all_to_all(array, axis, 0, 0, axis_index_groups=among, tiled=True)

    info = jnp.concatenate([clip_ids, jnp.broadcast_to(counts, (1, ROWS))], axis=0).astype(F32)
    info_other = lax.ppermute(info, "seq", swap)
    gain_own = jnp.concatenate([gain_q, gain_k], axis=0)
    gain_cols = all_to_all(jnp.broadcast_to(gain_own[None], (groups,) + gain_own.shape), "dp")
    picked, known = pick_other(place, tensors, gain_cols, info, info_other)
    rec = lax.ppermute(picked, "seq", swap)
    table = all_to_all(known, "seq", same_core)

    meta, *pieces = pack_halos(place, tensors, rec, table)
    halos = exchange(pieces, size)
    mid, gg_mid = solve_mid(meta, tensors, rec, table)
    own, gg, *pieces = solve_edges(meta, tensors, rec, table, mid, gg_mid, halos)
    returned = exchange(pieces, size)
    gg_parts = all_to_all(
        jnp.broadcast_to(gg[None], (groups,) + gg.shape).reshape(groups * chips, 2, HD),
        ("dp", "seq"),
        same_cores,
    )
    send = merge_other(meta, own, returned, gg_parts)
    other = lax.ppermute(send, "seq", swap)
    return tuple(weave(meta, own, other, returned, gg_parts))


def solution(mesh):
    rows = P(("dp", "seq"), None)
    cells = P("seq", "dp")
    slots = P("dp", "seq")
    return jax.shard_map(
        shards,
        mesh=mesh,
        in_specs=(rows, rows, rows, rows, cells, cells, slots, slots),
        out_specs=(rows, rows, rows, P("seq", None), P("seq", None)),
        check_vma=False,
    )
```

```python
import functools

import jax
import jax.numpy as jnp
from jax import lax
from jax.experimental import pallas as pl
from jax.experimental.pallas import tpu as pltpu
from jax.sharding import PartitionSpec as P

EPS = 1e-06
NEG = -1e30
HD = 128
ROWS = 128
PAIR = 256
HEADS = 16
ALIGN = 16
LINE = 4
CAP = 1152
PARTS = (CAP // 2,) * 2
FIRST = 768
REST = CAP - FIRST
SENT = len(PARTS) + 2
PADDED = CAP + PAIR
SCALE = HD**-0.5
LOG2E = 1.4426950408889634
BF = jnp.bfloat16
F32 = jnp.float32
CORE, CHIP, A_L, B_L, A_R, B_R, N_L, N_R, PA_L, PB_L, PA_R, PB_R = range(12)
KNOWN = 5
ANYWHERE = pl.BlockSpec(memory_space=pl.ANY)
IN_VMEM = pl.BlockSpec(memory_space=pltpu.VMEM)
IN_SMEM = pl.BlockSpec(memory_space=pltpu.SMEM)


def aligned(index):
    return pl.multiple_of(index, ALIGN)


def lanes(position):
    return pl.ds(pl.multiple_of(position * HD, HD), HD)


def params(mib):
    return pltpu.CompilerParams(vmem_limit_bytes=mib * 1024 * 1024)


def whole(shape):
    return pl.BlockSpec(shape, lambda j, m: (0,) * len(shape))


def run_copies(copies):
    for copy in copies:
        copy.start()
    for copy in copies:
        copy.wait()


def rows_of(held, start, length):
    return held.at[:, pl.ds(start, length), :]


def pick_kernel(
    place, q_ref, k_ref, v_ref, d_ref, gain_cols, info, info_other, out_ref, known_ref, row
):
    other = 1 - place[CORE]

    @pl.when(pl.program_id(0) == 0)
    def _():
        width = gain_cols.shape[2]
        row[...] = jnp.zeros_like(row)
        for n in range(gain_cols.shape[0]):
            row[0:2, n * width : (n + 1) * width] = gain_cols[n]
        row[2:3, :] = info[0:1, :]
        row[3:4, :] = info_other[0:1, :]
        row[4:5, 0:1] = info[1:2, 0:1]
        row[4:5, 1:2] = info_other[1:2, 0:1]
        known_ref[...] = jnp.broadcast_to(row[0:KNOWN, :][None], known_ref.shape)

    for t, ref in enumerate((q_ref, k_ref, v_ref, d_ref)):
        for i in range(out_ref.shape[2] // HD):
            out_ref[t, :, i * HD : (i + 1) * HD] = ref[:, lanes(2 * i + other)]


def pick_other(place, tensors, gain_cols, info, info_other, per=4):
    known = jax.ShapeDtypeStruct((HEADS, KNOWN, HD), F32)
    small = (gain_cols, info, info_other)
    return pl.pallas_call(
        pick_kernel,
        out_shape=(jax.ShapeDtypeStruct((4, ROWS, HEADS * HD), BF), known),
        grid_spec=pltpu.PrefetchScalarGridSpec(
            num_scalar_prefetch=1,
            grid=(HEADS // per,),
            in_specs=own_specs(per)[:4] + [whole(array.shape) for array in small],
            out_specs=(own_specs(per)[4], whole(known.shape)),
            scratch_shapes=[pltpu.VMEM((8, HD), F32)],
        ),
        compiler_params=params(12),
    )(place, *tensors, *small)


def chip_halves(info, core):
    ids, counts = (info[0:1], info[1:2]), (info[2:3, 0:1], info[2:3, 1:2])

    def ordered(mine, other):
        return jnp.where(core == 0, mine, other), jnp.where(core == 0, other, mine)

    return ordered(*ids), ordered(*counts)


def count_equal(halves, wanted):
    hits = [jnp.where(half == wanted, 1.0, 0.0).astype(F32) for half in halves]
    return jnp.sum(hits[0] + hits[1]).astype(jnp.int32)


def edge_split(long_a, long_b, left_chip):
    blocks_a = lax.div(long_a + ALIGN - 1, ALIGN)
    blocks_b = lax.div(long_b + ALIGN - 1, ALIGN)
    least = HEADS - lax.div(CAP // ALIGN, jnp.maximum(blocks_a, 1))
    most = lax.div(CAP // ALIGN, jnp.maximum(blocks_b, 1))
    spot = lax.rem(left_chip, LINE)
    wanted = jnp.where(spot == 0, 0, jnp.where(spot == LINE - 2, HEADS, HEADS // 2))
    to_left = jnp.minimum(jnp.maximum(wanted, least), most)
    return blocks_a * ALIGN, blocks_b * ALIGN, to_left


def chip_infos(table, chip):
    spots = (chip, jnp.maximum(chip - 1, 0), jnp.minimum(chip + 1, HEADS - 1))
    return [table[spot][2:KNOWN] for spot in spots]


def write_plan(place, table, meta):
    core, chip = place[CORE], place[CHIP]
    infos = chip_infos(table, chip)
    own, _ = chip_halves(infos[0], core)
    left, _ = chip_halves(infos[1], core)
    right, _ = chip_halves(infos[2], core)
    left_last, own_first = jnp.max(left[1]), jnp.min(own[0])
    own_last, right_first = jnp.max(own[1]), jnp.min(right[0])
    cross_l = (chip > 0) & (left_last == own_first)
    cross_r = (chip < HEADS - 1) & (right_first == own_last)
    a_l = jnp.where(cross_l, count_equal(left, left_last), 0)
    b_l = jnp.where(cross_l, count_equal(own, own_first), 0)
    a_r = jnp.where(cross_r, count_equal(own, own_last), 0)
    b_r = jnp.where(cross_r, count_equal(right, right_first), 0)
    pa_l, pb_l, n_l = edge_split(a_l, b_l, jnp.maximum(chip - 1, 0))
    pa_r, pb_r, n_r = edge_split(a_r, b_r, chip)
    n_l = jnp.where(cross_l, n_l, HEADS)
    n_r = jnp.where(cross_r, n_r, 0)
    values = [core, chip, a_l, b_l, a_r, b_r, n_l, n_r, pa_l, pb_l, pa_r, pb_r]
    for n, value in enumerate(values):
        meta[n] = value


def even(meta):
    return lax.rem(meta[CHIP], 2) == 0


def at_corner(meta):
    place = lax.rem(meta[CHIP], LINE)
    return (place == 0) | (place == LINE - 1)


def cut(table, *lengths):
    starts = [sum(lengths[:n]) for n in range(len(lengths))]
    return [table.at[:, pl.ds(a, n), :] for a, n in zip(starts, lengths, strict=True)]


def copies_of(sources, targets, sems):
    return [
        pltpu.make_async_copy(a, b, sems.at[n])
        for n, (a, b) in enumerate(zip(sources, targets, strict=True))
    ]


def start_one(cases):
    for wanted, copies in cases:

        @pl.when(wanted)
        def _():
            for copy in copies:
                copy.start()

    return cases[0][1]


def wait_all(copies):
    for copy in copies:
        copy.wait()


def send_pieces(meta, left, right, pieces, sems):
    def pieces_of(a, b):
        return copies_of(cut(a, *PARTS) + cut(b, FIRST, REST), pieces, sems)

    is_even = even(meta)
    wait_all(
        start_one(
            [
                (is_even, pieces_of(right, left)),
                (jnp.logical_not(is_even), pieces_of(left, right)),
            ]
        )
    )


def load_both(meta, pieces, held_left, held_right, sems):
    *direct, rest, relayed = pieces

    def pieces_of(a, b, last):
        return copies_of([*direct, last], cut(a, *PARTS) + cut(b, FIRST, REST), sems)

    is_even, corner = even(meta), at_corner(meta)
    is_odd, inner = jnp.logical_not(is_even), jnp.logical_not(corner)
    return start_one(
        [
            (is_even & corner, pieces_of(held_right, held_left, relayed)),
            (is_even & inner, pieces_of(held_right, held_left, rest)),
            (is_odd & corner, pieces_of(held_left, held_right, relayed)),
            (is_odd & inner, pieces_of(held_left, held_right, rest)),
        ]
    )


def half_rows(half):
    return pl.ds(pl.multiple_of(half * ROWS, ROWS), ROWS)


def fill_windows(win, core, own_refs, rec_ref):
    for i in range(win.shape[0]):
        for t, ref in enumerate(own_refs):
            win[i, t, half_rows(core), :] = ref[:, lanes(2 * i + core)]
            win[i, t, half_rows(1 - core), :] = rec_ref[t, :, i * HD : (i + 1) * HD]


def pack_kernel(place, q_ref, k_ref, v_ref, d_ref, rec_ref, table, meta, *refs):
    *pieces, win, left_ref, right_ref, sems = refs
    per = rec_ref.shape[2] // HD
    core = place[CORE]
    step = pl.program_id(0)

    @pl.when(step == 0)
    def _():
        write_plan(place, table, meta)

    fill_windows(win, core, (q_ref, k_ref, v_ref, d_ref), rec_ref)
    for i in range(per):
        head = step * per + i

        @pl.when(head < meta[N_L])
        def _():
            for t in range(4):
                left_ref[t, pl.ds(aligned(head * meta[PB_L]), PAIR), :] = win[i, t]

        @pl.when(head >= meta[N_R])
        def _():
            for t in range(4):
                right_ref[t, pl.ds(aligned((HEADS - head) * meta[PA_R]), PAIR), :] = win[i, t]

    @pl.when(step == pl.num_programs(0) - 1)
    def _():
        send_pieces(
            meta,
            rows_of(left_ref, 0, CAP),
            rows_of(right_ref, PAIR, CAP),
            pieces,
            sems,
        )


def own_specs(per):
    return [pl.BlockSpec((ROWS, 2 * per * HD), lambda j, m: (0, j))] * 4 + [
        pl.BlockSpec((4, ROWS, per * HD), lambda j, m: (0, 0, j))
    ]


def pieces_shape(tensors):
    return [jax.ShapeDtypeStruct((tensors, n, HD), BF) for n in (*PARTS, FIRST, REST)]


def pack_halos(place, tensors, rec, table, per=4):
    return pl.pallas_call(
        pack_kernel,
        out_shape=(
            jax.ShapeDtypeStruct((16,), jnp.int32),
            *pieces_shape(4),
        ),
        grid_spec=pltpu.PrefetchScalarGridSpec(
            num_scalar_prefetch=1,
            grid=(HEADS // per,),
            in_specs=own_specs(per) + [whole(table.shape)],
            out_specs=(IN_SMEM, *([ANYWHERE] * SENT)),
            scratch_shapes=[
                pltpu.VMEM((per, 4, PAIR, HD), BF),
                pltpu.VMEM((4, PADDED, HD), BF),
                pltpu.VMEM((4, PADDED, HD), BF),
                pltpu.SemaphoreType.DMA((SENT,)),
            ],
        ),
        compiler_params=params(16),
    )(place, *tensors, rec, table)


def matmul(a, b, contract_a, contract_b):
    return lax.dot_general(
        a, b, (((contract_a,), (contract_b,)), ((), ())), preferred_element_type=F32
    )


def norm_parts(rows, gain):
    widened = rows.astype(F32)
    scaled = lax.rsqrt(jnp.mean(widened * widened, axis=-1, keepdims=True) + EPS)
    unit_rows = widened * scaled
    return scaled, unit_rows, (unit_rows * gain).astype(BF)


def norm_back(scaled, unit_rows, gain, upper):
    terms = upper * unit_rows
    gain = gain * SCALE
    mean = jnp.mean(terms * gain, axis=-1, keepdims=True)
    grad = scaled * (gain * upper - unit_rows * mean)
    return grad.astype(BF), jnp.sum(terms, axis=0, keepdims=True) * SCALE


def solve(problems):
    each = range(len(problems))
    q_rows, k_rows, v_rows, d_rows, gain_q, gain_k, bias, q_live = zip(*problems, strict=True)
    q_parts = [norm_parts(q_rows[n], gain_q[n]) for n in each]
    k_parts = [norm_parts(k_rows[n], gain_k[n]) for n in each]
    raw = [matmul(k_parts[n][2], q_parts[n][2], 1, 1) for n in each]
    d_weights = [matmul(v_rows[n], d_rows[n], 1, 1) for n in each]
    weights = []
    for n in each:
        scores = raw[n] * (SCALE * LOG2E) + bias[n]
        exponent = jnp.exp2(scores - jnp.max(scores, axis=0, keepdims=True))
        total = jnp.sum(exponent, axis=0, keepdims=True)
        weights.append((exponent * (q_live[n] / total)).astype(BF))
    dv_rows = [matmul(weights[n], d_rows[n], 1, 0) for n in each]
    d_scores = []
    for n in each:
        wide = weights[n].astype(F32)
        row_delta = jnp.sum(wide * d_weights[n], axis=0, keepdims=True)
        d_scores.append((wide * (d_weights[n] - row_delta)).astype(BF))
    dk = [matmul(d_scores[n], q_parts[n][2], 1, 0) for n in each]
    dq = [matmul(d_scores[n], k_parts[n][2], 0, 0) for n in each]
    results = []
    for n in each:
        grad_k, gain_k_part = norm_back(k_parts[n][0], k_parts[n][1], gain_k[n], dk[n])
        grad_q, gain_q_part = norm_back(q_parts[n][0], q_parts[n][1], gain_q[n], dq[n])
        grads = (grad_q, grad_k, dv_rows[n].astype(BF))
        results.append((grads, gain_q_part, gain_k_part))
    return results


def link_codes(side, meta, table):
    core, infos = meta[CORE], chip_infos(table, meta[CHIP])
    own_ids, own_counts = chip_halves(infos[0], core)
    _, far_counts = chip_halves(infos[side], core)
    codes = []
    for half in range(2):
        lane = lax.broadcasted_iota(jnp.int32, (1, ROWS), 1)
        slot = lane + half * ROWS
        live = lane.astype(F32) < own_counts[half]
        far = lane.astype(F32) < far_counts[half]
        if side == 0:
            inside = live & (slot >= meta[B_L]) & (slot < PAIR - meta[A_R])
            code = jnp.where(inside, own_ids[half], -1.0)
        elif side == 1:
            inside = (live & (slot < meta[B_L])) | (far & (slot >= PAIR - meta[A_L]))
            code = jnp.where(inside, 0.0, -1.0)
        else:
            inside = (live & (slot >= PAIR - meta[A_R])) | (far & (slot < meta[B_R]))
            code = jnp.where(inside, 0.0, -1.0)
        codes.append(code.astype(F32))
    return codes


def fill_links(bias, q_live, codes):
    for a in range(2):
        q_live[0:1, a * ROWS : (a + 1) * ROWS] = (codes[a] >= 0.0).astype(F32)
        key_codes = jnp.broadcast_to(codes[a], (ROWS, ROWS)).T
        for b in range(2):
            linked = (key_codes == codes[b]) & (codes[b] >= 0.0)
            bias[a * ROWS : (a + 1) * ROWS, b * ROWS : (b + 1) * ROWS] = jnp.where(
                linked, 0.0, NEG
            ).astype(F32)


def mid_kernel(
    meta,
    q_ref,
    k_ref,
    v_ref,
    d_ref,
    rec_ref,
    table,
    out_ref,
    gg_ref,
    win,
    bias,
    q_live,
):
    per = rec_ref.shape[2] // HD
    core = meta[CORE]

    @pl.when(pl.program_id(0) == 0)
    def _():
        fill_links(bias, q_live, link_codes(0, meta, table))

    fill_windows(win, core, (q_ref, k_ref, v_ref, d_ref), rec_ref)
    heads = [pl.program_id(0) * per + i for i in range(per)]
    gains = [table[head] for head in heads]
    results = solve(
        [
            (*(win[i, t] for t in range(4)), gains[i][0:1], gains[i][1:2], bias[...], q_live[0:1, :])
            for i in range(per)
        ]
    )
    for i, (grads, part_q, part_k) in enumerate(results):
        for t in range(3):
            for half in range(2):
                out_ref[lax.rem(half + core, 2), t, :, i * HD : (i + 1) * HD] = grads[t][
                    half * ROWS : (half + 1) * ROWS
                ]
        gg_ref[heads[i]] = jnp.concatenate([part_q, part_k], axis=0)


def solve_mid(meta, tensors, rec, table, per=4):
    per_head = jax.ShapeDtypeStruct((HEADS, 2, HD), F32)
    return pl.pallas_call(
        mid_kernel,
        out_shape=(jax.ShapeDtypeStruct((2, 3, ROWS, HEADS * HD), BF), per_head),
        grid_spec=pltpu.PrefetchScalarGridSpec(
            num_scalar_prefetch=1,
            grid=(HEADS // per,),
            in_specs=own_specs(per) + [whole(table.shape)],
            out_specs=(half_spec(per), whole(per_head.shape)),
            scratch_shapes=[
                pltpu.VMEM((per, 4, PAIR, HD), BF),
                pltpu.VMEM((PAIR, PAIR), F32),
                pltpu.VMEM((8, PAIR), F32),
            ],
        ),
        compiler_params=params(32),
    )(meta, *tensors, rec, table)


def half_spec(per):
    return pl.BlockSpec((2, 3, ROWS, per * HD), lambda j, m: (0, 0, 0, j))


def row_numbers(rows):
    return lax.broadcasted_iota(jnp.int32, (rows, HD), 0).astype(F32).astype(BF)


def bound(value):
    return jnp.full((1, HD), value, jnp.int32).astype(F32).astype(BF)


def edge_kernel(
    meta, q_ref, k_ref, v_ref, d_ref, rec_ref, table, mid_ref, gg_mid_ref, *refs
):
    halos, (out_ref, gg_ref, *pieces) = refs[: SENT + 1], refs[SENT + 1 : -6]
    win, bias, q_live, held, back, sems = refs[-6:]
    per = rec_ref.shape[2] // HD
    core = meta[CORE]
    step = pl.program_id(0)

    @pl.when(step == 0)
    def _():
        copies = load_both(
            meta,
            halos,
            rows_of(held.at[0], PAIR, CAP),
            rows_of(held.at[1], 0, CAP),
            sems,
        )
        for side in range(2):
            fill_links(
                bias.at[side], q_live.at[side], link_codes(side + 1, meta, table)
            )
        gg_ref[...] = gg_mid_ref[...]
        for copy in copies:
            copy.wait()

    fill_windows(win, core, (q_ref, k_ref, v_ref, d_ref), rec_ref)
    out_ref[...] = mid_ref[...]
    heads = [step * per + i for i in range(per)]
    on_left = [head >= meta[N_L] for head in heads]
    on_right = [head < meta[N_R] for head in heads]
    row = row_numbers(PAIR)

    def solve_side(lefts, rights):
        problems, spots = [], []
        for i, head in enumerate(heads):
            side = jnp.where(lefts[i], 0, 1)
            use = jnp.logical_or(lefts[i], rights[i])
            at = jnp.where(lefts[i], (HEADS - head) * meta[PA_L], head * meta[PB_R])
            span = pl.ds(aligned(jnp.where(use, at, PADDED)), PAIR)
            source = pl.ds(aligned(jnp.where(use, at, 0)), PAIR)
            halo = (row >= bound(jnp.where(lefts[i], PAIR - meta[A_L], 0))) & (
                row < bound(jnp.where(lefts[i], PAIR, jnp.where(use, meta[B_R], 0)))
            )
            local = (row >= bound(jnp.where(lefts[i], 0, PAIR - meta[A_R]))) & (
                row < bound(jnp.where(lefts[i], meta[B_L], jnp.where(use, PAIR, 0)))
            )
            window = [jnp.where(halo, held[side, t, source, :], win[i, t]) for t in range(4)]
            gains = table[head]
            problems.append((*window, gains[0:1], gains[1:2], bias[side], q_live[side, 0:1, :]))
            spots.append((side, span, local, use.astype(F32)))
        for i, (grads, part_q, part_k) in enumerate(solve(problems)):
            side, span, local, counts = spots[i]
            cols = slice(i * HD, (i + 1) * HD)
            for t in range(3):
                back[side, t, span, :] = grads[t]
                for half in range(2):
                    rows = slice(half * ROWS, (half + 1) * ROWS)
                    place = lax.rem(half + core, 2)
                    out_ref[place, t, :, cols] = jnp.where(
                        local[rows], grads[t][rows], out_ref[place, t, :, cols]
                    )
            gg_ref[heads[i]] += jnp.concatenate([part_q, part_k], axis=0) * counts

    def some(flags):
        return functools.reduce(jnp.logical_or, flags)

    @pl.when(some(on_left + on_right))
    def _():
        solve_side(on_left, on_right)

    both = [jnp.logical_and(*pair) for pair in zip(on_left, on_right, strict=True)]

    @pl.when(some(both))
    def _():
        solve_side([jnp.logical_and(flag, jnp.logical_not(flag)) for flag in both], both)

    @pl.when(step == pl.num_programs(0) - 1)
    def _():
        send_pieces(
            meta,
            rows_of(back.at[0], PAIR, CAP),
            rows_of(back.at[1], 0, CAP),
            pieces,
            sems,
        )


def solve_edges(meta, tensors, rec, table, mid, gg_mid, halos, per=4):
    return pl.pallas_call(
        edge_kernel,
        out_shape=(
            jax.ShapeDtypeStruct(mid.shape, BF),
            jax.ShapeDtypeStruct(gg_mid.shape, F32),
            *pieces_shape(3),
        ),
        grid_spec=pltpu.PrefetchScalarGridSpec(
            num_scalar_prefetch=1,
            grid=(HEADS // per,),
            in_specs=own_specs(per)
            + [whole(table.shape), half_spec(per), whole(gg_mid.shape)]
            + [ANYWHERE] * (SENT + 1),
            out_specs=(half_spec(per), whole(gg_mid.shape), *([ANYWHERE] * SENT)),
            scratch_shapes=[
                pltpu.VMEM((per, 4, PAIR, HD), BF),
                pltpu.VMEM((2, PAIR, PAIR), F32),
                pltpu.VMEM((2, 8, PAIR), F32),
                pltpu.VMEM((2, 4, PADDED, HD), BF),
                pltpu.VMEM((2, 3, PADDED + PAIR, HD), BF),
                pltpu.SemaphoreType.DMA((SENT,)),
            ],
        ),
        compiler_params=params(40),
    )(meta, *tensors, rec, table, mid, gg_mid, *halos)


def load_returned(meta, pieces, held_left, held_right, sems):
    for copy in load_both(
        meta, pieces, rows_of(held_left, 0, CAP), rows_of(held_right, PAIR, CAP), sems
    ):
        copy.wait()


def merged(meta, head, half, rows, held_left, held_right):
    use_left = head < meta[N_L]
    use_right = head >= meta[N_R]
    base = half * ROWS
    left_at = jnp.where(use_left, head * meta[PB_L], 0) + base
    right_at = jnp.where(use_right, (HEADS - head) * meta[PA_R], 0) + base
    row = row_numbers(ROWS)
    at_head = row < bound(jnp.where(use_left, meta[B_L], 0) - base)
    at_tail = row >= bound(jnp.where(use_right, PAIR - meta[A_R], PAIR) - base)
    done = []
    for t, part in enumerate(rows):
        part = jnp.where(at_head, held_left[t, pl.ds(aligned(left_at), ROWS), :], part)
        part = jnp.where(at_tail, held_right[t, pl.ds(aligned(right_at), ROWS), :], part)
        done.append(part)
    return done


def merge_kernel(meta, in_ref, *refs):
    pieces, (_, send_ref, held_left, held_right, sems) = refs[: SENT + 1], refs[SENT + 1 :]
    per = in_ref.shape[3] // HD
    step = pl.program_id(0)

    @pl.when(step == 0)
    def _():
        load_returned(meta, pieces, held_left, held_right, sems)

    for i in range(per):
        cols = slice(i * HD, (i + 1) * HD)
        rows = [in_ref[0, t, :, cols] for t in range(3)]
        rows = merged(meta, step * per + i, 1 - meta[CORE], rows, held_left, held_right)
        for t in range(3):
            send_ref[t, :, cols] = rows[t]


def held_scratch():
    return [
        pltpu.VMEM((3, PADDED, HD), BF),
        pltpu.VMEM((3, PADDED, HD), BF),
        pltpu.SemaphoreType.DMA((SENT,)),
    ]


def merge_other(meta, own, returned, after, per=4):
    return pl.pallas_call(
        merge_kernel,
        out_shape=jax.ShapeDtypeStruct((3, ROWS, HEADS * HD), BF),
        grid_spec=pltpu.PrefetchScalarGridSpec(
            num_scalar_prefetch=1,
            grid=(HEADS // per,),
            in_specs=[pl.BlockSpec((1, 3, ROWS, per * HD), lambda j, m: (1, 0, 0, j))]
            + [ANYWHERE] * (SENT + 2),
            out_specs=pl.BlockSpec((3, ROWS, per * HD), lambda j, m: (0, 0, j)),
            scratch_shapes=held_scratch(),
        ),
        compiler_params=params(16),
    )(meta, own, *returned, after)


def weave_kernel(meta, in_ref, rec_ref, *refs):
    pieces, (gg_parts, *outs, gg_q, gg_k, held_left, held_right, sems) = refs[: SENT + 1], refs[SENT + 1 :]
    per = in_ref.shape[3] // HD
    core = meta[CORE]
    step = pl.program_id(0)

    @pl.when(step == 0)
    def _():
        load_returned(meta, pieces, held_left, held_right, sems)
        total = jnp.sum(gg_parts[...], axis=0)
        gg_q[...] = total[0:1]
        gg_k[...] = total[1:2]

    for i in range(per):
        cols = slice(i * HD, (i + 1) * HD)
        rows = [in_ref[0, t, :, cols] for t in range(3)]
        rows = merged(meta, step * per + i, core, rows, held_left, held_right)
        for t in range(3):
            outs[t][:, lanes(2 * i + core)] = rows[t]
            outs[t][:, lanes(2 * i + 1 - core)] = rec_ref[t, :, cols]


def weave(meta, own, rec, returned, gg_parts, per=4):
    return pl.pallas_call(
        weave_kernel,
        out_shape=(jax.ShapeDtypeStruct((ROWS, 2 * HEADS * HD), BF),) * 3
        + (jax.ShapeDtypeStruct((1, HD), F32),) * 2,
        grid_spec=pltpu.PrefetchScalarGridSpec(
            num_scalar_prefetch=1,
            grid=(HEADS // per,),
            in_specs=[
                pl.BlockSpec((1, 3, ROWS, per * HD), lambda j, m: (0, 0, 0, j)),
                pl.BlockSpec((3, ROWS, per * HD), lambda j, m: (0, 0, j)),
            ]
            + [ANYWHERE] * (SENT + 1)
            + [whole(gg_parts.shape)],
            out_specs=(pl.BlockSpec((ROWS, 2 * per * HD), lambda j, m: (0, j)),) * 3
            + (whole((1, HD)),) * 2,
            scratch_shapes=held_scratch(),
        ),
        compiler_params=params(16),
    )(meta, own, rec, *returned, gg_parts)


def exchange(pieces, size):
    *straight, first, rest = pieces
    line = 2 * LINE
    wrap = line - 2
    steps = [(i, i + 2) for i in range(size - 2)]
    evens = [pair for pair in steps if pair[0] // 2 % 2 == 0]
    odds = [pair for pair in steps if pair[0] // 2 % 2 == 1]
    turns = [pair for pair in odds if pair[0] % line >= wrap]
    inner = [pair for pair in odds if pair[0] % line < wrap]

    def both(pairs):
        return pairs + [(j, i) for i, j in pairs]

    def move(array, pairs):
        return lax.ppermute(array, "seq", pairs)

    along_x = [(i, i - wrap) for i, _ in turns] + [(j, j + wrap) for _, j in turns]
    along_z = [(i - wrap, j) for i, j in turns] + [(j + wrap, i) for i, j in turns]
    hop = move(rest, both(inner) + along_x)
    from_first = move(first, both(odds))
    from_even = [move(piece, both(evens)) for piece in straight]
    return (*from_even, from_first, hop, move(hop, along_z))


def shards(queries, keys, values, out_grad, gain_q, gain_k, clip_ids, counts):
    size = lax.axis_size("seq")
    groups = lax.axis_size("dp")
    chips = size // 2
    seq = lax.axis_index("seq")
    swap = [(i, i ^ 1) for i in range(size)]
    place = jnp.stack([seq % 2, seq // 2]).astype(jnp.int32)
    tensors = tuple(
        pltpu.with_memory_space_constraint(t, pltpu.HBM)
        for t in (queries, keys, values, out_grad)
    )

    same_core = [list(range(core, size, 2)) for core in range(2)]
    same_cores = [
        [d * size + at for d in range(groups) for at in one_core] for one_core in same_core
    ]

    def all_to_all(array, axis, among=None):
        return lax.all_to_all(array, axis, 0, 0, axis_index_groups=among, tiled=True)

    info = jnp.concatenate([clip_ids, jnp.broadcast_to(counts, (1, ROWS))], axis=0).astype(F32)
    info_other = lax.ppermute(info, "seq", swap)
    gain_own = jnp.concatenate([gain_q, gain_k], axis=0)
    gain_cols = all_to_all(jnp.broadcast_to(gain_own[None], (groups,) + gain_own.shape), "dp")
    picked, known = pick_other(place, tensors, gain_cols, info, info_other)
    rec = lax.ppermute(picked, "seq", swap)
    table = all_to_all(known, "seq", same_core)

    meta, *pieces = pack_halos(place, tensors, rec, table)
    halos = exchange(pieces, size)
    mid, gg_mid = solve_mid(meta, tensors, rec, table)
    own, gg, *pieces = solve_edges(meta, tensors, rec, table, mid, gg_mid, halos)
    returned = exchange(pieces, size)
    gg_parts = all_to_all(
        jnp.broadcast_to(gg[None], (groups,) + gg.shape).reshape(groups * chips, 2, HD),
        ("dp", "seq"),
        same_cores,
    )
    send = merge_other(meta, own, returned, gg_parts)
    other = lax.ppermute(send, "seq", swap)
    return tuple(weave(meta, own, other, returned, gg_parts))


def solution(mesh):
    rows = P(("dp", "seq"), None)
    cells = P("seq", "dp")
    slots = P("dp", "seq")
    return jax.shard_map(
        shards,
        mesh=mesh,
        in_specs=(rows, rows, rows, rows, cells, cells, slots, slots),
        out_specs=(rows, rows, rows, P("seq", None), P("seq", None)),
        check_vma=False,
    )
```

```python
import functools

import jax
import jax.numpy as jnp
from jax import lax
from jax.experimental import pallas as pl
from jax.experimental.pallas import tpu as pltpu
from jax.sharding import PartitionSpec as P

EPS = 1e-06
NEG = -1e30
HD = 128
ROWS = 128
PAIR = 256
HEADS = 16
ALIGN = 16
LINE = 4
CAP = 1152
PARTS = (CAP // 2,) * 2
FIRST = 768
REST = CAP - FIRST
SENT = len(PARTS) + 2
PADDED = CAP + PAIR
SCALE = HD**-0.5
LOG2E = 1.4426950408889634
BF = jnp.bfloat16
F32 = jnp.float32
CORE, CHIP, A_L, B_L, A_R, B_R, N_L, N_R, PA_L, PB_L, PA_R, PB_R = range(12)
KNOWN = 5
ANYWHERE = pl.BlockSpec(memory_space=pl.ANY)
IN_VMEM = pl.BlockSpec(memory_space=pltpu.VMEM)
IN_SMEM = pl.BlockSpec(memory_space=pltpu.SMEM)


def aligned(index):
    return pl.multiple_of(index, ALIGN)


def lanes(position):
    return pl.ds(pl.multiple_of(position * HD, HD), HD)


def params(mib):
    return pltpu.CompilerParams(vmem_limit_bytes=mib * 1024 * 1024)


def whole(shape):
    return pl.BlockSpec(shape, lambda j, m: (0,) * len(shape))


def run_copies(copies):
    for copy in copies:
        copy.start()
    for copy in copies:
        copy.wait()


def rows_of(held, start, length):
    return held.at[:, pl.ds(start, length), :]


def pick_kernel(
    place, q_ref, k_ref, v_ref, d_ref, gain_cols, info, info_other, out_ref, known_ref, row
):
    other = 1 - place[CORE]

    @pl.when(pl.program_id(0) == 0)
    def _():
        width = gain_cols.shape[2]
        row[...] = jnp.zeros_like(row)
        for n in range(gain_cols.shape[0]):
            row[0:2, n * width : (n + 1) * width] = gain_cols[n]
        row[2:3, :] = info[0:1, :]
        row[3:4, :] = info_other[0:1, :]
        row[4:5, 0:1] = info[1:2, 0:1]
        row[4:5, 1:2] = info_other[1:2, 0:1]
        known_ref[...] = jnp.broadcast_to(row[0:KNOWN, :][None], known_ref.shape)

    for t, ref in enumerate((q_ref, k_ref, v_ref, d_ref)):
        for i in range(out_ref.shape[2] // HD):
            out_ref[t, :, i * HD : (i + 1) * HD] = ref[:, lanes(2 * i + other)]


def pick_other(place, tensors, gain_cols, info, info_other, per=8):
    known = jax.ShapeDtypeStruct((HEADS, KNOWN, HD), F32)
    small = (gain_cols, info, info_other)
    return pl.pallas_call(
        pick_kernel,
        out_shape=(jax.ShapeDtypeStruct((4, ROWS, HEADS * HD), BF), known),
        grid_spec=pltpu.PrefetchScalarGridSpec(
            num_scalar_prefetch=1,
            grid=(HEADS // per,),
            in_specs=own_specs(per)[:4] + [whole(array.shape) for array in small],
            out_specs=(own_specs(per)[4], whole(known.shape)),
            scratch_shapes=[pltpu.VMEM((8, HD), F32)],
        ),
        compiler_params=params(12),
    )(place, *tensors, *small)


def chip_halves(info, core):
    ids, counts = (info[0:1], info[1:2]), (info[2:3, 0:1], info[2:3, 1:2])

    def ordered(mine, other):
        return jnp.where(core == 0, mine, other), jnp.where(core == 0, other, mine)

    return ordered(*ids), ordered(*counts)


def count_equal(halves, wanted):
    hits = [jnp.where(half == wanted, 1.0, 0.0).astype(F32) for half in halves]
    return jnp.sum(hits[0] + hits[1]).astype(jnp.int32)


def edge_split(long_a, long_b, left_chip):
    blocks_a = lax.div(long_a + ALIGN - 1, ALIGN)
    blocks_b = lax.div(long_b + ALIGN - 1, ALIGN)
    least = HEADS - lax.div(CAP // ALIGN, jnp.maximum(blocks_a, 1))
    most = lax.div(CAP // ALIGN, jnp.maximum(blocks_b, 1))
    spot = lax.rem(left_chip, LINE)
    wanted = jnp.where(spot == 0, 0, jnp.where(spot == LINE - 2, HEADS, HEADS // 2))
    to_left = jnp.minimum(jnp.maximum(wanted, least), most)
    return blocks_a * ALIGN, blocks_b * ALIGN, to_left


def chip_infos(table, chip):
    spots = (chip, jnp.maximum(chip - 1, 0), jnp.minimum(chip + 1, HEADS - 1))
    return [table[spot][2:KNOWN] for spot in spots]


def write_plan(place, table, meta):
    core, chip = place[CORE], place[CHIP]
    infos = chip_infos(table, chip)
    own, _ = chip_halves(infos[0], core)
    left, _ = chip_halves(infos[1], core)
    right, _ = chip_halves(infos[2], core)
    left_last, own_first = jnp.max(left[1]), jnp.min(own[0])
    own_last, right_first = jnp.max(own[1]), jnp.min(right[0])
    cross_l = (chip > 0) & (left_last == own_first)
    cross_r = (chip < HEADS - 1) & (right_first == own_last)
    a_l = jnp.where(cross_l, count_equal(left, left_last), 0)
    b_l = jnp.where(cross_l, count_equal(own, own_first), 0)
    a_r = jnp.where(cross_r, count_equal(own, own_last), 0)
    b_r = jnp.where(cross_r, count_equal(right, right_first), 0)
    pa_l, pb_l, n_l = edge_split(a_l, b_l, jnp.maximum(chip - 1, 0))
    pa_r, pb_r, n_r = edge_split(a_r, b_r, chip)
    n_l = jnp.where(cross_l, n_l, HEADS)
    n_r = jnp.where(cross_r, n_r, 0)
    values = [core, chip, a_l, b_l, a_r, b_r, n_l, n_r, pa_l, pb_l, pa_r, pb_r]
    for n, value in enumerate(values):
        meta[n] = value


def even(meta):
    return lax.rem(meta[CHIP], 2) == 0


def at_corner(meta):
    place = lax.rem(meta[CHIP], LINE)
    return (place == 0) | (place == LINE - 1)


def cut(table, *lengths):
    starts = [sum(lengths[:n]) for n in range(len(lengths))]
    return [table.at[:, pl.ds(a, n), :] for a, n in zip(starts, lengths, strict=True)]


def copies_of(sources, targets, sems):
    return [
        pltpu.make_async_copy(a, b, sems.at[n])
        for n, (a, b) in enumerate(zip(sources, targets, strict=True))
    ]


def start_one(cases):
    for wanted, copies in cases:

        @pl.when(wanted)
        def _():
            for copy in copies:
                copy.start()

    return cases[0][1]


def wait_all(copies):
    for copy in copies:
        copy.wait()


def send_pieces(meta, left, right, pieces, sems):
    def pieces_of(a, b):
        return copies_of(cut(a, *PARTS) + cut(b, FIRST, REST), pieces, sems)

    is_even = even(meta)
    wait_all(
        start_one(
            [
                (is_even, pieces_of(right, left)),
                (jnp.logical_not(is_even), pieces_of(left, right)),
            ]
        )
    )


def load_both(meta, pieces, held_left, held_right, sems):
    *direct, rest, relayed = pieces

    def pieces_of(a, b, last):
        return copies_of([*direct, last], cut(a, *PARTS) + cut(b, FIRST, REST), sems)

    is_even, corner = even(meta), at_corner(meta)
    is_odd, inner = jnp.logical_not(is_even), jnp.logical_not(corner)
    return start_one(
        [
            (is_even & corner, pieces_of(held_right, held_left, relayed)),
            (is_even & inner, pieces_of(held_right, held_left, rest)),
            (is_odd & corner, pieces_of(held_left, held_right, relayed)),
            (is_odd & inner, pieces_of(held_left, held_right, rest)),
        ]
    )


def half_rows(half):
    return pl.ds(pl.multiple_of(half * ROWS, ROWS), ROWS)


def fill_windows(win, core, own_refs, rec_ref):
    for i in range(win.shape[0]):
        for t, ref in enumerate(own_refs):
            win[i, t, half_rows(core), :] = ref[:, lanes(2 * i + core)]
            win[i, t, half_rows(1 - core), :] = rec_ref[t, :, i * HD : (i + 1) * HD]


def pack_kernel(place, q_ref, k_ref, v_ref, d_ref, rec_ref, table, meta, *refs):
    *pieces, win, left_ref, right_ref, sems = refs
    per = rec_ref.shape[2] // HD
    core = place[CORE]
    step = pl.program_id(0)

    @pl.when(step == 0)
    def _():
        write_plan(place, table, meta)

    fill_windows(win, core, (q_ref, k_ref, v_ref, d_ref), rec_ref)
    for i in range(per):
        head = step * per + i

        @pl.when(head < meta[N_L])
        def _():
            for t in range(4):
                left_ref[t, pl.ds(aligned(head * meta[PB_L]), PAIR), :] = win[i, t]

        @pl.when(head >= meta[N_R])
        def _():
            for t in range(4):
                right_ref[t, pl.ds(aligned((HEADS - head) * meta[PA_R]), PAIR), :] = win[i, t]

    @pl.when(step == pl.num_programs(0) - 1)
    def _():
        send_pieces(
            meta,
            rows_of(left_ref, 0, CAP),
            rows_of(right_ref, PAIR, CAP),
            pieces,
            sems,
        )


def own_specs(per):
    return [pl.BlockSpec((ROWS, 2 * per * HD), lambda j, m: (0, j))] * 4 + [
        pl.BlockSpec((4, ROWS, per * HD), lambda j, m: (0, 0, j))
    ]


def pieces_shape(tensors):
    return [jax.ShapeDtypeStruct((tensors, n, HD), BF) for n in (*PARTS, FIRST, REST)]


def pack_halos(place, tensors, rec, table, per=8):
    return pl.pallas_call(
        pack_kernel,
        out_shape=(
            jax.ShapeDtypeStruct((16,), jnp.int32),
            *pieces_shape(4),
        ),
        grid_spec=pltpu.PrefetchScalarGridSpec(
            num_scalar_prefetch=1,
            grid=(HEADS // per,),
            in_specs=own_specs(per) + [whole(table.shape)],
            out_specs=(IN_SMEM, *([ANYWHERE] * SENT)),
            scratch_shapes=[
                pltpu.VMEM((per, 4, PAIR, HD), BF),
                pltpu.VMEM((4, PADDED, HD), BF),
                pltpu.VMEM((4, PADDED, HD), BF),
                pltpu.SemaphoreType.DMA((SENT,)),
            ],
        ),
        compiler_params=params(16),
    )(place, *tensors, rec, table)


def matmul(a, b, contract_a, contract_b):
    return lax.dot_general(
        a, b, (((contract_a,), (contract_b,)), ((), ())), preferred_element_type=F32
    )


def norm_parts(rows, gain):
    widened = rows.astype(F32)
    scaled = lax.rsqrt(jnp.mean(widened * widened, axis=-1, keepdims=True) + EPS)
    unit_rows = widened * scaled
    return scaled, unit_rows, (unit_rows * gain).astype(BF)


def norm_back(scaled, unit_rows, gain, upper):
    terms = upper * unit_rows
    gain = gain * SCALE
    mean = jnp.mean(terms * gain, axis=-1, keepdims=True)
    grad = scaled * (gain * upper - unit_rows * mean)
    return grad.astype(BF), jnp.sum(terms, axis=0, keepdims=True) * SCALE


def solve(problems):
    each = range(len(problems))
    q_rows, k_rows, v_rows, d_rows, gain_q, gain_k, bias, q_live = zip(*problems, strict=True)
    q_parts = [norm_parts(q_rows[n], gain_q[n]) for n in each]
    k_parts = [norm_parts(k_rows[n], gain_k[n]) for n in each]
    raw = [matmul(k_parts[n][2], q_parts[n][2], 1, 1) for n in each]
    d_weights = [matmul(v_rows[n], d_rows[n], 1, 1) for n in each]
    weights = []
    for n in each:
        scores = raw[n] * (SCALE * LOG2E) + bias[n]
        exponent = jnp.exp2(scores - jnp.max(scores, axis=0, keepdims=True))
        total = jnp.sum(exponent, axis=0, keepdims=True)
        weights.append((exponent * (q_live[n] / total)).astype(BF))
    dv_rows = [matmul(weights[n], d_rows[n], 1, 0) for n in each]
    d_scores = []
    for n in each:
        wide = weights[n].astype(F32)
        row_delta = jnp.sum(wide * d_weights[n], axis=0, keepdims=True)
        d_scores.append((wide * (d_weights[n] - row_delta)).astype(BF))
    dk = [matmul(d_scores[n], q_parts[n][2], 1, 0) for n in each]
    dq = [matmul(d_scores[n], k_parts[n][2], 0, 0) for n in each]
    results = []
    for n in each:
        grad_k, gain_k_part = norm_back(k_parts[n][0], k_parts[n][1], gain_k[n], dk[n])
        grad_q, gain_q_part = norm_back(q_parts[n][0], q_parts[n][1], gain_q[n], dq[n])
        grads = (grad_q, grad_k, dv_rows[n].astype(BF))
        results.append((grads, gain_q_part, gain_k_part))
    return results


def link_codes(side, meta, table):
    core, infos = meta[CORE], chip_infos(table, meta[CHIP])
    own_ids, own_counts = chip_halves(infos[0], core)
    _, far_counts = chip_halves(infos[side], core)
    codes = []
    for half in range(2):
        lane = lax.broadcasted_iota(jnp.int32, (1, ROWS), 1)
        slot = lane + half * ROWS
        live = lane.astype(F32) < own_counts[half]
        far = lane.astype(F32) < far_counts[half]
        if side == 0:
            inside = live & (slot >= meta[B_L]) & (slot < PAIR - meta[A_R])
            code = jnp.where(inside, own_ids[half], -1.0)
        elif side == 1:
            inside = (live & (slot < meta[B_L])) | (far & (slot >= PAIR - meta[A_L]))
            code = jnp.where(inside, 0.0, -1.0)
        else:
            inside = (live & (slot >= PAIR - meta[A_R])) | (far & (slot < meta[B_R]))
            code = jnp.where(inside, 0.0, -1.0)
        codes.append(code.astype(F32))
    return codes


def fill_links(bias, q_live, codes):
    for a in range(2):
        q_live[0:1, a * ROWS : (a + 1) * ROWS] = (codes[a] >= 0.0).astype(F32)
        key_codes = jnp.broadcast_to(codes[a], (ROWS, ROWS)).T
        for b in range(2):
            linked = (key_codes == codes[b]) & (codes[b] >= 0.0)
            bias[a * ROWS : (a + 1) * ROWS, b * ROWS : (b + 1) * ROWS] = jnp.where(
                linked, 0.0, NEG
            ).astype(F32)


def mid_kernel(
    meta,
    q_ref,
    k_ref,
    v_ref,
    d_ref,
    rec_ref,
    table,
    out_ref,
    gg_ref,
    win,
    bias,
    q_live,
):
    per = rec_ref.shape[2] // HD
    core = meta[CORE]

    @pl.when(pl.program_id(0) == 0)
    def _():
        fill_links(bias, q_live, link_codes(0, meta, table))

    fill_windows(win, core, (q_ref, k_ref, v_ref, d_ref), rec_ref)
    heads = [pl.program_id(0) * per + i for i in range(per)]
    gains = [table[head] for head in heads]
    results = solve(
        [
            (*(win[i, t] for t in range(4)), gains[i][0:1], gains[i][1:2], bias[...], q_live[0:1, :])
            for i in range(per)
        ]
    )
    for i, (grads, part_q, part_k) in enumerate(results):
        for t in range(3):
            for half in range(2):
                out_ref[lax.rem(half + core, 2), t, :, i * HD : (i + 1) * HD] = grads[t][
                    half * ROWS : (half + 1) * ROWS
                ]
        gg_ref[heads[i]] = jnp.concatenate([part_q, part_k], axis=0)


def solve_mid(meta, tensors, rec, table, per=4):
    per_head = jax.ShapeDtypeStruct((HEADS, 2, HD), F32)
    return pl.pallas_call(
        mid_kernel,
        out_shape=(jax.ShapeDtypeStruct((2, 3, ROWS, HEADS * HD), BF), per_head),
        grid_spec=pltpu.PrefetchScalarGridSpec(
            num_scalar_prefetch=1,
            grid=(HEADS // per,),
            in_specs=own_specs(per) + [whole(table.shape)],
            out_specs=(half_spec(per), whole(per_head.shape)),
            scratch_shapes=[
                pltpu.VMEM((per, 4, PAIR, HD), BF),
                pltpu.VMEM((PAIR, PAIR), F32),
                pltpu.VMEM((8, PAIR), F32),
            ],
        ),
        compiler_params=params(32),
    )(meta, *tensors, rec, table)


def half_spec(per):
    return pl.BlockSpec((2, 3, ROWS, per * HD), lambda j, m: (0, 0, 0, j))


def row_numbers(rows):
    return lax.broadcasted_iota(jnp.int32, (rows, HD), 0).astype(F32).astype(BF)


def bound(value):
    return jnp.full((1, HD), value, jnp.int32).astype(F32).astype(BF)


def edge_kernel(
    meta, q_ref, k_ref, v_ref, d_ref, rec_ref, table, mid_ref, gg_mid_ref, *refs
):
    halos, (out_ref, gg_ref, *pieces) = refs[: SENT + 1], refs[SENT + 1 : -6]
    win, bias, q_live, held, back, sems = refs[-6:]
    per = rec_ref.shape[2] // HD
    core = meta[CORE]
    step = pl.program_id(0)

    @pl.when(step == 0)
    def _():
        copies = load_both(
            meta,
            halos,
            rows_of(held.at[0], PAIR, CAP),
            rows_of(held.at[1], 0, CAP),
            sems,
        )
        for side in range(2):
            fill_links(
                bias.at[side], q_live.at[side], link_codes(side + 1, meta, table)
            )
        gg_ref[...] = gg_mid_ref[...]
        for copy in copies:
            copy.wait()

    fill_windows(win, core, (q_ref, k_ref, v_ref, d_ref), rec_ref)
    out_ref[...] = mid_ref[...]
    heads = [step * per + i for i in range(per)]
    on_left = [head >= meta[N_L] for head in heads]
    on_right = [head < meta[N_R] for head in heads]
    row = row_numbers(PAIR)

    def solve_side(lefts, rights):
        problems, spots = [], []
        for i, head in enumerate(heads):
            side = jnp.where(lefts[i], 0, 1)
            use = jnp.logical_or(lefts[i], rights[i])
            at = jnp.where(lefts[i], (HEADS - head) * meta[PA_L], head * meta[PB_R])
            span = pl.ds(aligned(jnp.where(use, at, PADDED)), PAIR)
            source = pl.ds(aligned(jnp.where(use, at, 0)), PAIR)
            halo = (row >= bound(jnp.where(lefts[i], PAIR - meta[A_L], 0))) & (
                row < bound(jnp.where(lefts[i], PAIR, jnp.where(use, meta[B_R], 0)))
            )
            local = (row >= bound(jnp.where(lefts[i], 0, PAIR - meta[A_R]))) & (
                row < bound(jnp.where(lefts[i], meta[B_L], jnp.where(use, PAIR, 0)))
            )
            window = [jnp.where(halo, held[side, t, source, :], win[i, t]) for t in range(4)]
            gains = table[head]
            problems.append((*window, gains[0:1], gains[1:2], bias[side], q_live[side, 0:1, :]))
            spots.append((side, span, local, use.astype(F32)))
        for i, (grads, part_q, part_k) in enumerate(solve(problems)):
            side, span, local, counts = spots[i]
            cols = slice(i * HD, (i + 1) * HD)
            for t in range(3):
                back[side, t, span, :] = grads[t]
                for half in range(2):
                    rows = slice(half * ROWS, (half + 1) * ROWS)
                    place = lax.rem(half + core, 2)
                    out_ref[place, t, :, cols] = jnp.where(
                        local[rows], grads[t][rows], out_ref[place, t, :, cols]
                    )
            gg_ref[heads[i]] += jnp.concatenate([part_q, part_k], axis=0) * counts

    def some(flags):
        return functools.reduce(jnp.logical_or, flags)

    @pl.when(some(on_left + on_right))
    def _():
        solve_side(on_left, on_right)

    both = [jnp.logical_and(*pair) for pair in zip(on_left, on_right, strict=True)]

    @pl.when(some(both))
    def _():
        solve_side([jnp.logical_and(flag, jnp.logical_not(flag)) for flag in both], both)

    @pl.when(step == pl.num_programs(0) - 1)
    def _():
        send_pieces(
            meta,
            rows_of(back.at[0], PAIR, CAP),
            rows_of(back.at[1], 0, CAP),
            pieces,
            sems,
        )


def solve_edges(meta, tensors, rec, table, mid, gg_mid, halos, per=4):
    return pl.pallas_call(
        edge_kernel,
        out_shape=(
            jax.ShapeDtypeStruct(mid.shape, BF),
            jax.ShapeDtypeStruct(gg_mid.shape, F32),
            *pieces_shape(3),
        ),
        grid_spec=pltpu.PrefetchScalarGridSpec(
            num_scalar_prefetch=1,
            grid=(HEADS // per,),
            in_specs=own_specs(per)
            + [whole(table.shape), half_spec(per), whole(gg_mid.shape)]
            + [ANYWHERE] * (SENT + 1),
            out_specs=(half_spec(per), whole(gg_mid.shape), *([ANYWHERE] * SENT)),
            scratch_shapes=[
                pltpu.VMEM((per, 4, PAIR, HD), BF),
                pltpu.VMEM((2, PAIR, PAIR), F32),
                pltpu.VMEM((2, 8, PAIR), F32),
                pltpu.VMEM((2, 4, PADDED, HD), BF),
                pltpu.VMEM((2, 3, PADDED + PAIR, HD), BF),
                pltpu.SemaphoreType.DMA((SENT,)),
            ],
        ),
        compiler_params=params(40),
    )(meta, *tensors, rec, table, mid, gg_mid, *halos)


def load_returned(meta, pieces, held_left, held_right, sems):
    for copy in load_both(
        meta, pieces, rows_of(held_left, 0, CAP), rows_of(held_right, PAIR, CAP), sems
    ):
        copy.wait()


def merged(meta, head, half, rows, held_left, held_right):
    use_left = head < meta[N_L]
    use_right = head >= meta[N_R]
    base = half * ROWS
    left_at = jnp.where(use_left, head * meta[PB_L], 0) + base
    right_at = jnp.where(use_right, (HEADS - head) * meta[PA_R], 0) + base
    row = row_numbers(ROWS)
    at_head = row < bound(jnp.where(use_left, meta[B_L], 0) - base)
    at_tail = row >= bound(jnp.where(use_right, PAIR - meta[A_R], PAIR) - base)
    done = []
    for t, part in enumerate(rows):
        part = jnp.where(at_head, held_left[t, pl.ds(aligned(left_at), ROWS), :], part)
        part = jnp.where(at_tail, held_right[t, pl.ds(aligned(right_at), ROWS), :], part)
        done.append(part)
    return done


def merge_kernel(meta, in_ref, *refs):
    pieces, (_, send_ref, held_left, held_right, sems) = refs[: SENT + 1], refs[SENT + 1 :]
    per = in_ref.shape[3] // HD
    step = pl.program_id(0)

    @pl.when(step == 0)
    def _():
        load_returned(meta, pieces, held_left, held_right, sems)

    for i in range(per):
        cols = slice(i * HD, (i + 1) * HD)
        rows = [in_ref[0, t, :, cols] for t in range(3)]
        rows = merged(meta, step * per + i, 1 - meta[CORE], rows, held_left, held_right)
        for t in range(3):
            send_ref[t, :, cols] = rows[t]


def held_scratch():
    return [
        pltpu.VMEM((3, PADDED, HD), BF),
        pltpu.VMEM((3, PADDED, HD), BF),
        pltpu.SemaphoreType.DMA((SENT,)),
    ]


def merge_other(meta, own, returned, after, per=8):
    return pl.pallas_call(
        merge_kernel,
        out_shape=jax.ShapeDtypeStruct((3, ROWS, HEADS * HD), BF),
        grid_spec=pltpu.PrefetchScalarGridSpec(
            num_scalar_prefetch=1,
            grid=(HEADS // per,),
            in_specs=[pl.BlockSpec((1, 3, ROWS, per * HD), lambda j, m: (1, 0, 0, j))]
            + [ANYWHERE] * (SENT + 2),
            out_specs=pl.BlockSpec((3, ROWS, per * HD), lambda j, m: (0, 0, j)),
            scratch_shapes=held_scratch(),
        ),
        compiler_params=params(16),
    )(meta, own, *returned, after)


def weave_kernel(meta, in_ref, rec_ref, *refs):
    pieces, (gg_parts, *outs, gg_q, gg_k, held_left, held_right, sems) = refs[: SENT + 1], refs[SENT + 1 :]
    per = in_ref.shape[3] // HD
    core = meta[CORE]
    step = pl.program_id(0)

    @pl.when(step == 0)
    def _():
        load_returned(meta, pieces, held_left, held_right, sems)
        total = jnp.sum(gg_parts[...], axis=0)
        gg_q[...] = total[0:1]
        gg_k[...] = total[1:2]

    for i in range(per):
        cols = slice(i * HD, (i + 1) * HD)
        rows = [in_ref[0, t, :, cols] for t in range(3)]
        rows = merged(meta, step * per + i, core, rows, held_left, held_right)
        for t in range(3):
            outs[t][:, lanes(2 * i + core)] = rows[t]
            outs[t][:, lanes(2 * i + 1 - core)] = rec_ref[t, :, cols]


def weave(meta, own, rec, returned, gg_parts, per=8):
    return pl.pallas_call(
        weave_kernel,
        out_shape=(jax.ShapeDtypeStruct((ROWS, 2 * HEADS * HD), BF),) * 3
        + (jax.ShapeDtypeStruct((1, HD), F32),) * 2,
        grid_spec=pltpu.PrefetchScalarGridSpec(
            num_scalar_prefetch=1,
            grid=(HEADS // per,),
            in_specs=[
                pl.BlockSpec((1, 3, ROWS, per * HD), lambda j, m: (0, 0, 0, j)),
                pl.BlockSpec((3, ROWS, per * HD), lambda j, m: (0, 0, j)),
            ]
            + [ANYWHERE] * (SENT + 1)
            + [whole(gg_parts.shape)],
            out_specs=(pl.BlockSpec((ROWS, 2 * per * HD), lambda j, m: (0, j)),) * 3
            + (whole((1, HD)),) * 2,
            scratch_shapes=held_scratch(),
        ),
        compiler_params=params(16),
    )(meta, own, rec, *returned, gg_parts)


def exchange(pieces, size):
    *straight, first, rest = pieces
    line = 2 * LINE
    wrap = line - 2
    steps = [(i, i + 2) for i in range(size - 2)]
    evens = [pair for pair in steps if pair[0] // 2 % 2 == 0]
    odds = [pair for pair in steps if pair[0] // 2 % 2 == 1]
    turns = [pair for pair in odds if pair[0] % line >= wrap]
    inner = [pair for pair in odds if pair[0] % line < wrap]

    def both(pairs):
        return pairs + [(j, i) for i, j in pairs]

    def move(array, pairs):
        return lax.ppermute(array, "seq", pairs)

    along_x = [(i, i - wrap) for i, _ in turns] + [(j, j + wrap) for _, j in turns]
    along_z = [(i - wrap, j) for i, j in turns] + [(j + wrap, i) for i, j in turns]
    hop = move(rest, both(inner) + along_x)
    from_first = move(first, both(odds))
    from_even = [move(piece, both(evens)) for piece in straight]
    return (*from_even, from_first, hop, move(hop, along_z))


def shards(queries, keys, values, out_grad, gain_q, gain_k, clip_ids, counts):
    size = lax.axis_size("seq")
    groups = lax.axis_size("dp")
    chips = size // 2
    seq = lax.axis_index("seq")
    swap = [(i, i ^ 1) for i in range(size)]
    place = jnp.stack([seq % 2, seq // 2]).astype(jnp.int32)
    tensors = tuple(
        pltpu.with_memory_space_constraint(t, pltpu.HBM)
        for t in (queries, keys, values, out_grad)
    )

    same_core = [list(range(core, size, 2)) for core in range(2)]
    same_cores = [
        [d * size + at for d in range(groups) for at in one_core] for one_core in same_core
    ]

    def all_to_all(array, axis, among=None):
        return lax.all_to_all(array, axis, 0, 0, axis_index_groups=among, tiled=True)

    info = jnp.concatenate([clip_ids, jnp.broadcast_to(counts, (1, ROWS))], axis=0).astype(F32)
    info_other = lax.ppermute(info, "seq", swap)
    gain_own = jnp.concatenate([gain_q, gain_k], axis=0)
    gain_cols = all_to_all(jnp.broadcast_to(gain_own[None], (groups,) + gain_own.shape), "dp")
    picked, known = pick_other(place, tensors, gain_cols, info, info_other)
    rec = lax.ppermute(picked, "seq", swap)
    table = all_to_all(known, "seq", same_core)

    meta, *pieces = pack_halos(place, tensors, rec, table)
    halos = exchange(pieces, size)
    mid, gg_mid = solve_mid(meta, tensors, rec, table)
    own, gg, *pieces = solve_edges(meta, tensors, rec, table, mid, gg_mid, halos)
    returned = exchange(pieces, size)
    gg_parts = all_to_all(
        jnp.broadcast_to(gg[None], (groups,) + gg.shape).reshape(groups * chips, 2, HD),
        ("dp", "seq"),
        same_cores,
    )
    send = merge_other(meta, own, returned, gg_parts)
    other = lax.ppermute(send, "seq", swap)
    return tuple(weave(meta, own, other, returned, gg_parts))


def solution(mesh):
    rows = P(("dp", "seq"), None)
    cells = P("seq", "dp")
    slots = P("dp", "seq")
    return jax.shard_map(
        shards,
        mesh=mesh,
        in_specs=(rows, rows, rows, rows, cells, cells, slots, slots),
        out_specs=(rows, rows, rows, P("seq", None), P("seq", None)),
        check_vma=False,
    )
```

```python
import functools

import jax
import jax.numpy as jnp
from jax import lax
from jax.experimental import pallas as pl
from jax.experimental.pallas import tpu as pltpu
from jax.sharding import PartitionSpec as P

EPS = 1e-06
NEG = -1e30
HD = 128
ROWS = 128
PAIR = 256
HEADS = 16
ALIGN = 16
LINE = 4
CAP = 1152
PARTS = (CAP,)
FIRST = 768
REST = CAP - FIRST
SENT = len(PARTS) + 2
PADDED = CAP + PAIR
SCALE = HD**-0.5
LOG2E = 1.4426950408889634
BF = jnp.bfloat16
F32 = jnp.float32
CORE, CHIP, A_L, B_L, A_R, B_R, N_L, N_R, PA_L, PB_L, PA_R, PB_R = range(12)
KNOWN = 5
ANYWHERE = pl.BlockSpec(memory_space=pl.ANY)
IN_VMEM = pl.BlockSpec(memory_space=pltpu.VMEM)
IN_SMEM = pl.BlockSpec(memory_space=pltpu.SMEM)


def aligned(index):
    return pl.multiple_of(index, ALIGN)


def lanes(position):
    return pl.ds(pl.multiple_of(position * HD, HD), HD)


def params(mib):
    return pltpu.CompilerParams(vmem_limit_bytes=mib * 1024 * 1024)


def whole(shape):
    return pl.BlockSpec(shape, lambda j, m: (0,) * len(shape))


def run_copies(copies):
    for copy in copies:
        copy.start()
    for copy in copies:
        copy.wait()


def rows_of(held, start, length):
    return held.at[:, pl.ds(start, length), :]


def pick_kernel(
    place, q_ref, k_ref, v_ref, d_ref, gain_cols, info, info_other, out_ref, known_ref, row
):
    other = 1 - place[CORE]

    @pl.when(pl.program_id(0) == 0)
    def _():
        width = gain_cols.shape[2]
        row[...] = jnp.zeros_like(row)
        for n in range(gain_cols.shape[0]):
            row[0:2, n * width : (n + 1) * width] = gain_cols[n]
        row[2:3, :] = info[0:1, :]
        row[3:4, :] = info_other[0:1, :]
        row[4:5, 0:1] = info[1:2, 0:1]
        row[4:5, 1:2] = info_other[1:2, 0:1]
        known_ref[...] = jnp.broadcast_to(row[0:KNOWN, :][None], known_ref.shape)

    for t, ref in enumerate((q_ref, k_ref, v_ref, d_ref)):
        for i in range(out_ref.shape[2] // HD):
            out_ref[t, :, i * HD : (i + 1) * HD] = ref[:, lanes(2 * i + other)]


def pick_other(place, tensors, gain_cols, info, info_other, per=8):
    known = jax.ShapeDtypeStruct((HEADS, KNOWN, HD), F32)
    small = (gain_cols, info, info_other)
    return pl.pallas_call(
        pick_kernel,
        out_shape=(jax.ShapeDtypeStruct((4, ROWS, HEADS * HD), BF), known),
        grid_spec=pltpu.PrefetchScalarGridSpec(
            num_scalar_prefetch=1,
            grid=(HEADS // per,),
            in_specs=own_specs(per)[:4] + [whole(array.shape) for array in small],
            out_specs=(own_specs(per)[4], whole(known.shape)),
            scratch_shapes=[pltpu.VMEM((8, HD), F32)],
        ),
        compiler_params=params(12),
    )(place, *tensors, *small)


def chip_halves(info, core):
    ids, counts = (info[0:1], info[1:2]), (info[2:3, 0:1], info[2:3, 1:2])

    def ordered(mine, other):
        return jnp.where(core == 0, mine, other), jnp.where(core == 0, other, mine)

    return ordered(*ids), ordered(*counts)


def count_equal(halves, wanted):
    hits = [jnp.where(half == wanted, 1.0, 0.0).astype(F32) for half in halves]
    return jnp.sum(hits[0] + hits[1]).astype(jnp.int32)


def edge_split(long_a, long_b, left_chip):
    blocks_a = lax.div(long_a + ALIGN - 1, ALIGN)
    blocks_b = lax.div(long_b + ALIGN - 1, ALIGN)
    least = HEADS - lax.div(CAP // ALIGN, jnp.maximum(blocks_a, 1))
    most = lax.div(CAP // ALIGN, jnp.maximum(blocks_b, 1))
    spot = lax.rem(left_chip, LINE)
    wanted = jnp.where(spot == 0, 0, jnp.where(spot == LINE - 2, HEADS, HEADS // 2))
    to_left = jnp.minimum(jnp.maximum(wanted, least), most)
    return blocks_a * ALIGN, blocks_b * ALIGN, to_left


def chip_infos(table, chip):
    spots = (chip, jnp.maximum(chip - 1, 0), jnp.minimum(chip + 1, HEADS - 1))
    return [table[spot][2:KNOWN] for spot in spots]


def write_plan(place, table, meta):
    core, chip = place[CORE], place[CHIP]
    infos = chip_infos(table, chip)
    own, _ = chip_halves(infos[0], core)
    left, _ = chip_halves(infos[1], core)
    right, _ = chip_halves(infos[2], core)
    left_last, own_first = jnp.max(left[1]), jnp.min(own[0])
    own_last, right_first = jnp.max(own[1]), jnp.min(right[0])
    cross_l = (chip > 0) & (left_last == own_first)
    cross_r = (chip < HEADS - 1) & (right_first == own_last)
    a_l = jnp.where(cross_l, count_equal(left, left_last), 0)
    b_l = jnp.where(cross_l, count_equal(own, own_first), 0)
    a_r = jnp.where(cross_r, count_equal(own, own_last), 0)
    b_r = jnp.where(cross_r, count_equal(right, right_first), 0)
    pa_l, pb_l, n_l = edge_split(a_l, b_l, jnp.maximum(chip - 1, 0))
    pa_r, pb_r, n_r = edge_split(a_r, b_r, chip)
    n_l = jnp.where(cross_l, n_l, HEADS)
    n_r = jnp.where(cross_r, n_r, 0)
    values = [core, chip, a_l, b_l, a_r, b_r, n_l, n_r, pa_l, pb_l, pa_r, pb_r]
    for n, value in enumerate(values):
        meta[n] = value


def even(meta):
    return lax.rem(meta[CHIP], 2) == 0


def at_corner(meta):
    place = lax.rem(meta[CHIP], LINE)
    return (place == 0) | (place == LINE - 1)


def cut(table, *lengths):
    starts = [sum(lengths[:n]) for n in range(len(lengths))]
    return [table.at[:, pl.ds(a, n), :] for a, n in zip(starts, lengths, strict=True)]


def copies_of(sources, targets, sems):
    return [
        pltpu.make_async_copy(a, b, sems.at[n])
        for n, (a, b) in enumerate(zip(sources, targets, strict=True))
    ]


def start_one(cases):
    for wanted, copies in cases:

        @pl.when(wanted)
        def _():
            for copy in copies:
                copy.start()

    return cases[0][1]


def wait_all(copies):
    for copy in copies:
        copy.wait()


def send_pieces(meta, left, right, pieces, sems):
    def pieces_of(a, b):
        return copies_of(cut(a, *PARTS) + cut(b, FIRST, REST), pieces, sems)

    is_even = even(meta)
    wait_all(
        start_one(
            [
                (is_even, pieces_of(right, left)),
                (jnp.logical_not(is_even), pieces_of(left, right)),
            ]
        )
    )


def load_both(meta, pieces, held_left, held_right, sems):
    *direct, rest, relayed = pieces

    def pieces_of(a, b, last):
        return copies_of([*direct, last], cut(a, *PARTS) + cut(b, FIRST, REST), sems)

    is_even, corner = even(meta), at_corner(meta)
    is_odd, inner = jnp.logical_not(is_even), jnp.logical_not(corner)
    return start_one(
        [
            (is_even & corner, pieces_of(held_right, held_left, relayed)),
            (is_even & inner, pieces_of(held_right, held_left, rest)),
            (is_odd & corner, pieces_of(held_left, held_right, relayed)),
            (is_odd & inner, pieces_of(held_left, held_right, rest)),
        ]
    )


def half_rows(half):
    return pl.ds(pl.multiple_of(half * ROWS, ROWS), ROWS)


def fill_windows(win, core, own_refs, rec_ref):
    for i in range(win.shape[0]):
        for t, ref in enumerate(own_refs):
            win[i, t, half_rows(core), :] = ref[:, lanes(2 * i + core)]
            win[i, t, half_rows(1 - core), :] = rec_ref[t, :, i * HD : (i + 1) * HD]


def pack_kernel(place, q_ref, k_ref, v_ref, d_ref, rec_ref, table, meta, *refs):
    *pieces, win, left_ref, right_ref, sems = refs
    per = rec_ref.shape[2] // HD
    core = place[CORE]
    step = pl.program_id(0)

    @pl.when(step == 0)
    def _():
        write_plan(place, table, meta)

    fill_windows(win, core, (q_ref, k_ref, v_ref, d_ref), rec_ref)
    for i in range(per):
        head = step * per + i

        @pl.when(head < meta[N_L])
        def _():
            for t in range(4):
                left_ref[t, pl.ds(aligned(head * meta[PB_L]), PAIR), :] = win[i, t]

        @pl.when(head >= meta[N_R])
        def _():
            for t in range(4):
                right_ref[t, pl.ds(aligned((HEADS - head) * meta[PA_R]), PAIR), :] = win[i, t]

    @pl.when(step == pl.num_programs(0) - 1)
    def _():
        send_pieces(
            meta,
            rows_of(left_ref, 0, CAP),
            rows_of(right_ref, PAIR, CAP),
            pieces,
            sems,
        )


def own_specs(per):
    return [pl.BlockSpec((ROWS, 2 * per * HD), lambda j, m: (0, j))] * 4 + [
        pl.BlockSpec((4, ROWS, per * HD), lambda j, m: (0, 0, j))
    ]


def pieces_shape(tensors):
    return [jax.ShapeDtypeStruct((tensors, n, HD), BF) for n in (*PARTS, FIRST, REST)]


def pack_halos(place, tensors, rec, table, per=8):
    return pl.pallas_call(
        pack_kernel,
        out_shape=(
            jax.ShapeDtypeStruct((16,), jnp.int32),
            *pieces_shape(4),
        ),
        grid_spec=pltpu.PrefetchScalarGridSpec(
            num_scalar_prefetch=1,
            grid=(HEADS // per,),
            in_specs=own_specs(per) + [whole(table.shape)],
            out_specs=(IN_SMEM, *([ANYWHERE] * SENT)),
            scratch_shapes=[
                pltpu.VMEM((per, 4, PAIR, HD), BF),
                pltpu.VMEM((4, PADDED, HD), BF),
                pltpu.VMEM((4, PADDED, HD), BF),
                pltpu.SemaphoreType.DMA((SENT,)),
            ],
        ),
        compiler_params=params(16),
    )(place, *tensors, rec, table)


def matmul(a, b, contract_a, contract_b):
    return lax.dot_general(
        a, b, (((contract_a,), (contract_b,)), ((), ())), preferred_element_type=F32
    )


def norm_parts(rows, gain):
    widened = rows.astype(F32)
    scaled = lax.rsqrt(jnp.mean(widened * widened, axis=-1, keepdims=True) + EPS)
    unit_rows = widened * scaled
    return scaled, unit_rows, (unit_rows * gain).astype(BF)


def norm_back(scaled, unit_rows, gain, upper):
    terms = upper * unit_rows
    gain = gain * SCALE
    mean = jnp.mean(terms * gain, axis=-1, keepdims=True)
    grad = scaled * (gain * upper - unit_rows * mean)
    return grad.astype(BF), jnp.sum(terms, axis=0, keepdims=True) * SCALE


def solve(problems):
    each = range(len(problems))
    q_rows, k_rows, v_rows, d_rows, gain_q, gain_k, bias, q_live = zip(*problems, strict=True)
    q_parts = [norm_parts(q_rows[n], gain_q[n]) for n in each]
    k_parts = [norm_parts(k_rows[n], gain_k[n]) for n in each]
    raw = [matmul(k_parts[n][2], q_parts[n][2], 1, 1) for n in each]
    d_weights = [matmul(v_rows[n], d_rows[n], 1, 1) for n in each]
    weights = []
    for n in each:
        scores = raw[n] * (SCALE * LOG2E) + bias[n]
        exponent = jnp.exp2(scores - jnp.max(scores, axis=0, keepdims=True))
        total = jnp.sum(exponent, axis=0, keepdims=True)
        weights.append((exponent * (q_live[n] / total)).astype(BF))
    dv_rows = [matmul(weights[n], d_rows[n], 1, 0) for n in each]
    d_scores = []
    for n in each:
        wide = weights[n].astype(F32)
        row_delta = jnp.sum(wide * d_weights[n], axis=0, keepdims=True)
        d_scores.append((wide * (d_weights[n] - row_delta)).astype(BF))
    dk = [matmul(d_scores[n], q_parts[n][2], 1, 0) for n in each]
    dq = [matmul(d_scores[n], k_parts[n][2], 0, 0) for n in each]
    results = []
    for n in each:
        grad_k, gain_k_part = norm_back(k_parts[n][0], k_parts[n][1], gain_k[n], dk[n])
        grad_q, gain_q_part = norm_back(q_parts[n][0], q_parts[n][1], gain_q[n], dq[n])
        grads = (grad_q, grad_k, dv_rows[n].astype(BF))
        results.append((grads, gain_q_part, gain_k_part))
    return results


def link_codes(side, meta, table):
    core, infos = meta[CORE], chip_infos(table, meta[CHIP])
    own_ids, own_counts = chip_halves(infos[0], core)
    _, far_counts = chip_halves(infos[side], core)
    codes = []
    for half in range(2):
        lane = lax.broadcasted_iota(jnp.int32, (1, ROWS), 1)
        slot = lane + half * ROWS
        live = lane.astype(F32) < own_counts[half]
        far = lane.astype(F32) < far_counts[half]
        if side == 0:
            inside = live & (slot >= meta[B_L]) & (slot < PAIR - meta[A_R])
            code = jnp.where(inside, own_ids[half], -1.0)
        elif side == 1:
            inside = (live & (slot < meta[B_L])) | (far & (slot >= PAIR - meta[A_L]))
            code = jnp.where(inside, 0.0, -1.0)
        else:
            inside = (live & (slot >= PAIR - meta[A_R])) | (far & (slot < meta[B_R]))
            code = jnp.where(inside, 0.0, -1.0)
        codes.append(code.astype(F32))
    return codes


def fill_links(bias, q_live, codes):
    for a in range(2):
        q_live[0:1, a * ROWS : (a + 1) * ROWS] = (codes[a] >= 0.0).astype(F32)
        key_codes = jnp.broadcast_to(codes[a], (ROWS, ROWS)).T
        for b in range(2):
            linked = (key_codes == codes[b]) & (codes[b] >= 0.0)
            bias[a * ROWS : (a + 1) * ROWS, b * ROWS : (b + 1) * ROWS] = jnp.where(
                linked, 0.0, NEG
            ).astype(F32)


def mid_kernel(
    meta,
    q_ref,
    k_ref,
    v_ref,
    d_ref,
    rec_ref,
    table,
    out_ref,
    gg_ref,
    win,
    bias,
    q_live,
):
    per = rec_ref.shape[2] // HD
    core = meta[CORE]

    @pl.when(pl.program_id(0) == 0)
    def _():
        fill_links(bias, q_live, link_codes(0, meta, table))

    fill_windows(win, core, (q_ref, k_ref, v_ref, d_ref), rec_ref)
    heads = [pl.program_id(0) * per + i for i in range(per)]
    gains = [table[head] for head in heads]
    results = solve(
        [
            (*(win[i, t] for t in range(4)), gains[i][0:1], gains[i][1:2], bias[...], q_live[0:1, :])
            for i in range(per)
        ]
    )
    for i, (grads, part_q, part_k) in enumerate(results):
        for t in range(3):
            for half in range(2):
                out_ref[lax.rem(half + core, 2), t, :, i * HD : (i + 1) * HD] = grads[t][
                    half * ROWS : (half + 1) * ROWS
                ]
        gg_ref[heads[i]] = jnp.concatenate([part_q, part_k], axis=0)


def solve_mid(meta, tensors, rec, table, per=4):
    per_head = jax.ShapeDtypeStruct((HEADS, 2, HD), F32)
    return pl.pallas_call(
        mid_kernel,
        out_shape=(jax.ShapeDtypeStruct((2, 3, ROWS, HEADS * HD), BF), per_head),
        grid_spec=pltpu.PrefetchScalarGridSpec(
            num_scalar_prefetch=1,
            grid=(HEADS // per,),
            in_specs=own_specs(per) + [whole(table.shape)],
            out_specs=(half_spec(per), whole(per_head.shape)),
            scratch_shapes=[
                pltpu.VMEM((per, 4, PAIR, HD), BF),
                pltpu.VMEM((PAIR, PAIR), F32),
                pltpu.VMEM((8, PAIR), F32),
            ],
        ),
        compiler_params=params(32),
    )(meta, *tensors, rec, table)


def half_spec(per):
    return pl.BlockSpec((2, 3, ROWS, per * HD), lambda j, m: (0, 0, 0, j))


def row_numbers(rows):
    return lax.broadcasted_iota(jnp.int32, (rows, HD), 0).astype(F32).astype(BF)


def bound(value):
    return jnp.full((1, HD), value, jnp.int32).astype(F32).astype(BF)


def edge_kernel(
    meta, q_ref, k_ref, v_ref, d_ref, rec_ref, table, mid_ref, gg_mid_ref, *refs
):
    halos, (out_ref, gg_ref, *pieces) = refs[: SENT + 1], refs[SENT + 1 : -6]
    win, bias, q_live, held, back, sems = refs[-6:]
    per = rec_ref.shape[2] // HD
    core = meta[CORE]
    step = pl.program_id(0)

    @pl.when(step == 0)
    def _():
        copies = load_both(
            meta,
            halos,
            rows_of(held.at[0], PAIR, CAP),
            rows_of(held.at[1], 0, CAP),
            sems,
        )
        for side in range(2):
            fill_links(
                bias.at[side], q_live.at[side], link_codes(side + 1, meta, table)
            )
        gg_ref[...] = gg_mid_ref[...]
        for copy in copies:
            copy.wait()

    fill_windows(win, core, (q_ref, k_ref, v_ref, d_ref), rec_ref)
    out_ref[...] = mid_ref[...]
    heads = [step * per + i for i in range(per)]
    on_left = [head >= meta[N_L] for head in heads]
    on_right = [head < meta[N_R] for head in heads]
    row = row_numbers(PAIR)

    def solve_side(lefts, rights):
        problems, spots = [], []
        for i, head in enumerate(heads):
            side = jnp.where(lefts[i], 0, 1)
            use = jnp.logical_or(lefts[i], rights[i])
            at = jnp.where(lefts[i], (HEADS - head) * meta[PA_L], head * meta[PB_R])
            span = pl.ds(aligned(jnp.where(use, at, PADDED)), PAIR)
            source = pl.ds(aligned(jnp.where(use, at, 0)), PAIR)
            halo = (row >= bound(jnp.where(lefts[i], PAIR - meta[A_L], 0))) & (
                row < bound(jnp.where(lefts[i], PAIR, jnp.where(use, meta[B_R], 0)))
            )
            local = (row >= bound(jnp.where(lefts[i], 0, PAIR - meta[A_R]))) & (
                row < bound(jnp.where(lefts[i], meta[B_L], jnp.where(use, PAIR, 0)))
            )
            window = [jnp.where(halo, held[side, t, source, :], win[i, t]) for t in range(4)]
            gains = table[head]
            problems.append((*window, gains[0:1], gains[1:2], bias[side], q_live[side, 0:1, :]))
            spots.append((side, span, local, use.astype(F32)))
        for i, (grads, part_q, part_k) in enumerate(solve(problems)):
            side, span, local, counts = spots[i]
            cols = slice(i * HD, (i + 1) * HD)
            for t in range(3):
                back[side, t, span, :] = grads[t]
                for half in range(2):
                    rows = slice(half * ROWS, (half + 1) * ROWS)
                    place = lax.rem(half + core, 2)
                    out_ref[place, t, :, cols] = jnp.where(
                        local[rows], grads[t][rows], out_ref[place, t, :, cols]
                    )
            gg_ref[heads[i]] += jnp.concatenate([part_q, part_k], axis=0) * counts

    def some(flags):
        return functools.reduce(jnp.logical_or, flags)

    @pl.when(some(on_left + on_right))
    def _():
        solve_side(on_left, on_right)

    both = [jnp.logical_and(*pair) for pair in zip(on_left, on_right, strict=True)]

    @pl.when(some(both))
    def _():
        solve_side([jnp.logical_and(flag, jnp.logical_not(flag)) for flag in both], both)

    @pl.when(step == pl.num_programs(0) - 1)
    def _():
        send_pieces(
            meta,
            rows_of(back.at[0], PAIR, CAP),
            rows_of(back.at[1], 0, CAP),
            pieces,
            sems,
        )


def solve_edges(meta, tensors, rec, table, mid, gg_mid, halos, per=4):
    return pl.pallas_call(
        edge_kernel,
        out_shape=(
            jax.ShapeDtypeStruct(mid.shape, BF),
            jax.ShapeDtypeStruct(gg_mid.shape, F32),
            *pieces_shape(3),
        ),
        grid_spec=pltpu.PrefetchScalarGridSpec(
            num_scalar_prefetch=1,
            grid=(HEADS // per,),
            in_specs=own_specs(per)
            + [whole(table.shape), half_spec(per), whole(gg_mid.shape)]
            + [ANYWHERE] * (SENT + 1),
            out_specs=(half_spec(per), whole(gg_mid.shape), *([ANYWHERE] * SENT)),
            scratch_shapes=[
                pltpu.VMEM((per, 4, PAIR, HD), BF),
                pltpu.VMEM((2, PAIR, PAIR), F32),
                pltpu.VMEM((2, 8, PAIR), F32),
                pltpu.VMEM((2, 4, PADDED, HD), BF),
                pltpu.VMEM((2, 3, PADDED + PAIR, HD), BF),
                pltpu.SemaphoreType.DMA((SENT,)),
            ],
        ),
        compiler_params=params(40),
    )(meta, *tensors, rec, table, mid, gg_mid, *halos)


def load_returned(meta, pieces, held_left, held_right, sems):
    for copy in load_both(
        meta, pieces, rows_of(held_left, 0, CAP), rows_of(held_right, PAIR, CAP), sems
    ):
        copy.wait()


def merged(meta, head, half, rows, held_left, held_right):
    use_left = head < meta[N_L]
    use_right = head >= meta[N_R]
    base = half * ROWS
    left_at = jnp.where(use_left, head * meta[PB_L], 0) + base
    right_at = jnp.where(use_right, (HEADS - head) * meta[PA_R], 0) + base
    row = row_numbers(ROWS)
    at_head = row < bound(jnp.where(use_left, meta[B_L], 0) - base)
    at_tail = row >= bound(jnp.where(use_right, PAIR - meta[A_R], PAIR) - base)
    done = []
    for t, part in enumerate(rows):
        part = jnp.where(at_head, held_left[t, pl.ds(aligned(left_at), ROWS), :], part)
        part = jnp.where(at_tail, held_right[t, pl.ds(aligned(right_at), ROWS), :], part)
        done.append(part)
    return done


def merge_kernel(meta, in_ref, *refs):
    pieces, (_, send_ref, held_left, held_right, sems) = refs[: SENT + 1], refs[SENT + 1 :]
    per = in_ref.shape[3] // HD
    step = pl.program_id(0)

    @pl.when(step == 0)
    def _():
        load_returned(meta, pieces, held_left, held_right, sems)

    for i in range(per):
        cols = slice(i * HD, (i + 1) * HD)
        rows = [in_ref[0, t, :, cols] for t in range(3)]
        rows = merged(meta, step * per + i, 1 - meta[CORE], rows, held_left, held_right)
        for t in range(3):
            send_ref[t, :, cols] = rows[t]


def held_scratch():
    return [
        pltpu.VMEM((3, PADDED, HD), BF),
        pltpu.VMEM((3, PADDED, HD), BF),
        pltpu.SemaphoreType.DMA((SENT,)),
    ]


def merge_other(meta, own, returned, after, per=8):
    return pl.pallas_call(
        merge_kernel,
        out_shape=jax.ShapeDtypeStruct((3, ROWS, HEADS * HD), BF),
        grid_spec=pltpu.PrefetchScalarGridSpec(
            num_scalar_prefetch=1,
            grid=(HEADS // per,),
            in_specs=[pl.BlockSpec((1, 3, ROWS, per * HD), lambda j, m: (1, 0, 0, j))]
            + [ANYWHERE] * (SENT + 2),
            out_specs=pl.BlockSpec((3, ROWS, per * HD), lambda j, m: (0, 0, j)),
            scratch_shapes=held_scratch(),
        ),
        compiler_params=params(16),
    )(meta, own, *returned, after)


def weave_kernel(meta, in_ref, rec_ref, *refs):
    pieces, (gg_parts, *outs, gg_q, gg_k, held_left, held_right, sems) = refs[: SENT + 1], refs[SENT + 1 :]
    per = in_ref.shape[3] // HD
    core = meta[CORE]
    step = pl.program_id(0)

    @pl.when(step == 0)
    def _():
        load_returned(meta, pieces, held_left, held_right, sems)
        total = jnp.sum(gg_parts[...], axis=0)
        gg_q[...] = total[0:1]
        gg_k[...] = total[1:2]

    for i in range(per):
        cols = slice(i * HD, (i + 1) * HD)
        rows = [in_ref[0, t, :, cols] for t in range(3)]
        rows = merged(meta, step * per + i, core, rows, held_left, held_right)
        for t in range(3):
            outs[t][:, lanes(2 * i + core)] = rows[t]
            outs[t][:, lanes(2 * i + 1 - core)] = rec_ref[t, :, cols]


def weave(meta, own, rec, returned, gg_parts, per=8):
    return pl.pallas_call(
        weave_kernel,
        out_shape=(jax.ShapeDtypeStruct((ROWS, 2 * HEADS * HD), BF),) * 3
        + (jax.ShapeDtypeStruct((1, HD), F32),) * 2,
        grid_spec=pltpu.PrefetchScalarGridSpec(
            num_scalar_prefetch=1,
            grid=(HEADS // per,),
            in_specs=[
                pl.BlockSpec((1, 3, ROWS, per * HD), lambda j, m: (0, 0, 0, j)),
                pl.BlockSpec((3, ROWS, per * HD), lambda j, m: (0, 0, j)),
            ]
            + [ANYWHERE] * (SENT + 1)
            + [whole(gg_parts.shape)],
            out_specs=(pl.BlockSpec((ROWS, 2 * per * HD), lambda j, m: (0, j)),) * 3
            + (whole((1, HD)),) * 2,
            scratch_shapes=held_scratch(),
        ),
        compiler_params=params(16),
    )(meta, own, rec, *returned, gg_parts)


def exchange(pieces, size):
    *straight, first, rest = pieces
    line = 2 * LINE
    wrap = line - 2
    steps = [(i, i + 2) for i in range(size - 2)]
    evens = [pair for pair in steps if pair[0] // 2 % 2 == 0]
    odds = [pair for pair in steps if pair[0] // 2 % 2 == 1]
    turns = [pair for pair in odds if pair[0] % line >= wrap]
    inner = [pair for pair in odds if pair[0] % line < wrap]

    def both(pairs):
        return pairs + [(j, i) for i, j in pairs]

    def move(array, pairs):
        return lax.ppermute(array, "seq", pairs)

    along_x = [(i, i - wrap) for i, _ in turns] + [(j, j + wrap) for _, j in turns]
    along_z = [(i - wrap, j) for i, j in turns] + [(j + wrap, i) for i, j in turns]
    hop = move(rest, both(inner) + along_x)
    from_first = move(first, both(odds))
    from_even = [move(piece, both(evens)) for piece in straight]
    return (*from_even, from_first, hop, move(hop, along_z))


def shards(queries, keys, values, out_grad, gain_q, gain_k, clip_ids, counts):
    size = lax.axis_size("seq")
    groups = lax.axis_size("dp")
    chips = size // 2
    seq = lax.axis_index("seq")
    swap = [(i, i ^ 1) for i in range(size)]
    place = jnp.stack([seq % 2, seq // 2]).astype(jnp.int32)
    tensors = tuple(
        pltpu.with_memory_space_constraint(t, pltpu.HBM)
        for t in (queries, keys, values, out_grad)
    )

    same_core = [list(range(core, size, 2)) for core in range(2)]
    same_cores = [
        [d * size + at for d in range(groups) for at in one_core] for one_core in same_core
    ]

    def all_to_all(array, axis, among=None):
        return lax.all_to_all(array, axis, 0, 0, axis_index_groups=among, tiled=True)

    info = jnp.concatenate([clip_ids, jnp.broadcast_to(counts, (1, ROWS))], axis=0).astype(F32)
    info_other = lax.ppermute(info, "seq", swap)
    gain_own = jnp.concatenate([gain_q, gain_k], axis=0)
    gain_cols = all_to_all(jnp.broadcast_to(gain_own[None], (groups,) + gain_own.shape), "dp")
    picked, known = pick_other(place, tensors, gain_cols, info, info_other)
    rec = lax.ppermute(picked, "seq", swap)
    table = all_to_all(known, "seq", same_core)

    meta, *pieces = pack_halos(place, tensors, rec, table)
    halos = exchange(pieces, size)
    mid, gg_mid = solve_mid(meta, tensors, rec, table)
    own, gg, *pieces = solve_edges(meta, tensors, rec, table, mid, gg_mid, halos)
    returned = exchange(pieces, size)
    gg_parts = all_to_all(
        jnp.broadcast_to(gg[None], (groups,) + gg.shape).reshape(groups * chips, 2, HD),
        ("dp", "seq"),
        same_cores,
    )
    send = merge_other(meta, own, returned, gg_parts)
    other = lax.ppermute(send, "seq", swap)
    return tuple(weave(meta, own, other, returned, gg_parts))


def solution(mesh):
    rows = P(("dp", "seq"), None)
    cells = P("seq", "dp")
    slots = P("dp", "seq")
    return jax.shard_map(
        shards,
        mesh=mesh,
        in_specs=(rows, rows, rows, rows, cells, cells, slots, slots),
        out_specs=(rows, rows, rows, P("seq", None), P("seq", None)),
        check_vma=False,
    )
```
